32 devices in a mesh: domain: 8 (over y, x, core), band: 4 (over z).
Axes of the slice: x: 2, y: 2, z: 4, core: 2. Of those that a mesh axis runs over, the one named last changes fastest.
Arguments:
- wavefunctions: bfloat16 [3072, 16384], P('domain', 'band'), may hold values from -6 to 6
- rotation: bfloat16 [16384, 1024], P('band', 'domain'), may hold values from -0.0625 to 0.0625
- cell_matrices: bfloat16 [8, 512, 512], P('domain'), may hold values from -0.25 to 0.25
- cell_nodes: int32 [8, 512], P('domain'), may hold values from 0 to 511, as said below
- face_map: int32 [1024], P('domain'), may hold values from 0 to 383, as said below
Outputs:
- applied: float32 [3072, 1024], P('domain', 'band')
The draws below stay inside these ranges and needn't reach their ends.
Inputs may be any that keep to these rules, and one draw needn't show every extreme that they name: `cell_nodes`: each cell names 512 distinct positions of its device's extended list (the 384 own nodes, then the 128 shared nodes of the next device); consecutive cells of a device share 128 positions; only the last cell of each device names shared nodes, and it names all of them. `face_map`: each device's block holds 128 distinct own nodes, all of them nodes of its first cell that no other of its cells names.
All inputs are finite; a program needn't handle non-finite values.
Results may differ from the reference program's by a relative error of at most 0.0029.
Values may be sent and summed in bfloat16 or wider, within the bound.
No kernel may reach another device: no remote copies, remote signals or barrier semaphores. Data moves between devices by JAX's collectives and lax.ppermute only.
A program may use at most 64 MiB of HBM per device.

```python
import jax
import jax.numpy as jnp
from jax import lax

STATES = 16384
OUT = 1024
CELL_NODES = 512
FACE = 128
CELL_DEV = 1
NODE_DEV = 384
NODES = 3072
CELLS = 8


def draw_cell_nodes(key, part):
    domain_count = CELLS // CELL_DEV
    stride = CELL_NODES - FACE

    def one_cell(cell_key, cell_number):
        return jax.random.permutation(cell_key, CELL_NODES) + cell_number * stride

    def one_device(device_key):
        cell_keys = jax.random.split(device_key, CELL_DEV)
        return jax.vmap(one_cell)(cell_keys, jnp.arange(CELL_DEV))
    own_key = jax.random.fold_in(key, 11)
    result = jax.vmap(one_device)(jax.random.split(own_key, domain_count))
    return result.reshape(CELLS, CELL_NODES).astype(jnp.int32)


def draw_face_map(key, part):
    domain_count = NODES // NODE_DEV
    stride = CELL_NODES - FACE

    def one_device(device_key):
        first_key, second_key = jax.random.split(device_key)
        chosen = jax.random.permutation(first_key, stride - 1)[:FACE - 1]
        with_top = jnp.concatenate([chosen, jnp.full((1,), stride - 1, chosen.dtype)])
        return jax.random.permutation(second_key, with_top)
    own_key = jax.random.fold_in(key, 23)
    result = jax.vmap(one_device)(jax.random.split(own_key, domain_count))
    return result.reshape(FACE * domain_count).astype(jnp.int32)


def with_spikes(entries, key, source, target, shards_of, factor):
    owner, partner = [(jnp.arange(entries.shape[axis_at]) // (entries.shape[axis_at] // shards_of)).reshape([-1 if axis == axis_at else 1 for axis in range(entries.ndim)]) for axis_at in (source, target)]
    chosen = jax.random.permutation(key, shards_of)[partner]
    strong = (owner == chosen) | (owner == (partner + shards_of // 2) % shards_of)
    return jnp.where(strong, factor * entries, entries)


def levels(stream_key, extent, pieces, low, top_value):
    def one(dim, shards_of):
        draws = jax.random.uniform(jax.random.fold_in(jax.random.fold_in(stream_key, 6), dim), (shards_of,), jnp.float32, low / len(pieces), top_value / len(pieces))
        return jnp.repeat(jnp.exp(draws), extent[dim] // shards_of).reshape((-1,) + (1,) * (len(extent) - dim - 1))

    loudness = one(*pieces[0])
    for cut in pieces[1:]:
        loudness = loudness * one(*cut)
    return loudness


def gaussian(stream_key, dims, scale, most, shards=(), held_as=jnp.bfloat16):
    gain = levels(stream_key, dims, shards, -0.22, 0.18) if shards else 1.0
    drawn = jax.random.normal(stream_key, dims, jnp.float32) * scale * gain
    return jnp.minimum(jnp.maximum(drawn, -most), most).astype(held_as)


def gaussian_with(key, extent, spread, limit, shards, heavy, held_as=jnp.bfloat16):
    drawn = spread * jax.random.normal(key, extent, jnp.float32)
    if shards:
        drawn = drawn * levels(key, extent, shards, -0.22, 0.18)
    return jnp.clip(with_spikes(drawn, jax.random.fold_in(key, 3), *heavy), -limit, limit).astype(held_as)


def setup_inputs(seed: int = 0) -> dict:
    streams_of = jax.random.split(jax.random.key(seed), 6)
    return {
        "wavefunctions": gaussian(streams_of[0], (NODES, STATES), 1.0, 6.0, ((0, 8), (1, 4))),
        "rotation": gaussian_with(streams_of[1], (STATES, OUT), STATES ** -0.5, 0.0625, ((0, 4), (1, 8)), (0, 1, 8, 2.0)),
        "cell_matrices": gaussian(streams_of[2], (CELLS, CELL_NODES, CELL_NODES), CELL_NODES ** -0.5, 0.25, ((0, 8),)),
        "cell_nodes": draw_cell_nodes(jax.random.fold_in(streams_of[5], 71), 0),
        "face_map": draw_face_map(jax.random.fold_in(streams_of[5], 71), 0),
    }


def reference(wavefunctions, rotation, cell_matrices, cell_nodes, face_map):
    domain_count = NODES // NODE_DEV
    rotation_wide = rotation.astype(jnp.float32)
    row_blocks = wavefunctions.reshape(domain_count, NODE_DEV, STATES)

    def rotate_block(block):
        return jnp.dot(block.astype(jnp.float32), rotation_wide, precision=lax.Precision.HIGHEST).astype(jnp.bfloat16)

    blocks = lax.map(rotate_block, row_blocks)
    maps = face_map.reshape(domain_count, FACE)
    next_blocks = jnp.concatenate([blocks[1:], jnp.zeros((1, NODE_DEV, OUT), jnp.bfloat16)], axis=0)
    next_maps = jnp.concatenate([maps[1:], jnp.zeros((1, FACE), jnp.int32)], axis=0)
    matrices = cell_matrices.reshape(domain_count, CELL_DEV, CELL_NODES, CELL_NODES)
    nodes = cell_nodes.reshape(domain_count, CELL_DEV, CELL_NODES)

    def one_domain(items):
        own, after_block, after_map, mats, index_list = items
        incoming = jnp.take(after_block, after_map, axis=0)
        extended = jnp.concatenate([own, incoming], axis=0)
        gathered = jnp.take(extended, index_list, axis=0).astype(jnp.float32)
        products = jnp.einsum("cij,cjo->cio", mats.astype(jnp.float32), gathered)
        return jax.ops.segment_sum(products.reshape(-1, OUT), index_list.reshape(-1), num_segments=NODE_DEV + FACE)

    accumulated = lax.map(one_domain, (blocks, next_blocks, next_maps, matrices, nodes))
    outgoing = accumulated[:, NODE_DEV:]
    returned = jnp.concatenate([jnp.zeros((1, FACE, OUT), jnp.float32), outgoing[:-1]], axis=0)

    def add_back(owned, where, values):
        return owned.at[where].add(values)

    applied = jax.vmap(add_back)(accumulated[:, :NODE_DEV], maps, returned)
    return applied.reshape(NODES, OUT)
```

```python
import jax
import jax.numpy as jnp
from jax import lax
from jax.sharding import PartitionSpec as P

CORE, NEAR, FAR = 1, 2, 4


def dot(left, right):
    precision = lax.Precision.HIGHEST if left.dtype == jnp.float32 else None
    return jnp.dot(left, right, precision=precision, preferred_element_type=jnp.float32)


def split(value):
    high = lax.reduce_precision(value, 8, 7)
    return high.astype(jnp.bfloat16), (value - high).astype(jnp.bfloat16)


def shifted(value, axis, steps):
    count = lax.axis_size(axis)
    leading, last = (max(0, -steps), min(count, count - steps))
    return lax.ppermute(value, axis, [(source, source + steps) for source in range(leading, last)])


def exchanged(value, axis, mask):
    return lax.ppermute(value, axis, [(source, source ^ mask) for source in range(lax.axis_size(axis))])


def rotate_square(wavefunctions, rotation):
    domain, band = lax.axis_index("domain"), lax.axis_index("band")
    chip, core = domain // 2, domain % 2
    half = rotation.shape[0] // 2
    top, bottom = rotation[:half], rotation[half:]
    near_top = exchanged(top, "domain", NEAR)
    far_bottom = exchanged(bottom, "domain", FAR)
    near_bottom = exchanged(bottom, "domain", NEAR)
    far_top = exchanged(top, "domain", FAR)
    both_top = exchanged(near_top, "domain", FAR)
    both_bottom = exchanged(far_bottom, "domain", NEAR)
    pieces = [(top, bottom), (near_top, near_bottom), (far_top, far_bottom), (both_top, both_bottom)]
    w_top, w_bottom = wavefunctions[:, :half], wavefunctions[:, half:]
    blocks = []
    for upper, lower in pieces:
        other_upper = exchanged(upper, "domain", CORE)
        other_lower = exchanged(lower, "domain", CORE)
        mine = dot(w_top, upper) + dot(w_bottom, lower)
        other = dot(w_top, other_upper) + dot(w_bottom, other_lower)
        blocks.append(jnp.where(core == 0, jnp.concatenate([mine, other], 1), jnp.concatenate([other, mine], 1)))
    partial = jnp.stack(blocks)
    rounded = partial.astype(jnp.bfloat16)
    place = chip ^ band
    total = lax.dynamic_index_in_dim(partial, place, 0, keepdims=False)
    for mask in range(1, lax.axis_size("band")):
        sent = lax.dynamic_index_in_dim(rounded, place ^ mask, 0, keepdims=False)
        total = total + exchanged(sent, "band", mask).astype(jnp.float32)
    return total


def rotate_any(wavefunctions, rotation):
    columns = lax.all_gather(rotation, "domain", axis=1, tiled=True)
    return lax.psum_scatter(dot(wavefunctions, columns), "band", scatter_dimension=1, tiled=True)


def local(wavefunctions, rotation, cell_matrices, cell_nodes, face_map):
    cells = cell_nodes.shape[0]
    own = wavefunctions.shape[0]
    extent = own + face_map.shape[0]
    held = jnp.bfloat16 if cells == 1 else jnp.float32

    places = jax.nn.one_hot(cell_nodes, extent, dtype=held)
    assembled = jnp.zeros((extent, extent), jnp.float32)
    for cell in range(cells):
        rows = dot(places[cell].T, cell_matrices[cell].astype(held)).astype(held)
        assembled = assembled + dot(rows, places[cell])
    assembled = assembled.astype(held)
    pick = jax.nn.one_hot(face_map, own, dtype=held)
    corner = shifted(assembled[own:, own:], "domain", 1)
    returned = dot(dot(pick.T, corner).astype(held), pick).astype(held)

    chips = lax.axis_size("domain") // 2
    square = chips == FAR and chips == lax.axis_size("band")
    rotated = (rotate_square if square else rotate_any)(wavefunctions, rotation)

    high, low = split(rotated)
    if cells == 1:
        def apply(matrix):
            return dot(matrix, high) + dot(matrix, low)
    else:
        def apply(matrix):
            return dot(matrix, rotated)

    faces = dot(pick, high.astype(held)).astype(jnp.bfloat16)
    incoming = shifted(faces, "domain", -1)
    back = shifted(apply(assembled[own:, :own]), "domain", 1)
    result = apply(assembled[:own, :own]) + apply(returned) + dot(assembled[:own, own:], incoming.astype(held))
    if cells == 1:
        back_high, back_low = split(back)
        return result + dot(pick.T, back_high) + dot(pick.T, back_low)
    return result + dot(pick.T, back)


def solution(mesh):
    in_specs = (
        P("domain", "band"),
        P("band", "domain"),
        P("domain", None, None),
        P("domain", None),
        P("domain"),
    )
    out_specs = P("domain", "band")
    return jax.shard_map(local, mesh=mesh, in_specs=in_specs, out_specs=out_specs, check_vma=False)
```

```python
import jax
import jax.numpy as jnp
from jax import lax
from jax.sharding import PartitionSpec as P

CORE, NEAR, FAR = 1, 2, 4


def dot(left, right):
    precision = lax.Precision.HIGHEST if left.dtype == jnp.float32 else None
    return jnp.dot(left, right, precision=precision, preferred_element_type=jnp.float32)


def split(value):
    high = lax.reduce_precision(value, 8, 7)
    return high.astype(jnp.bfloat16), (value - high).astype(jnp.bfloat16)


def shifted(value, axis, steps):
    count = lax.axis_size(axis)
    leading, last = (max(0, -steps), min(count, count - steps))
    return lax.ppermute(value, axis, [(source, source + steps) for source in range(leading, last)])


def exchanged(value, axis, mask):
    return lax.ppermute(value, axis, [(source, source ^ mask) for source in range(lax.axis_size(axis))])


def rotate_square(wavefunctions, rotation):
    chip, core, band = lax.axis_index("domain") // 2, lax.axis_index("domain") % 2, lax.axis_index("band")
    first = core == 0
    half = rotation.shape[0] // 2
    start, other_start = core * half, (1 - core) * half
    keep = lax.dynamic_slice_in_dim(rotation, start, half, 0)
    received = exchanged(lax.dynamic_slice_in_dim(rotation, other_start, half, 0), "domain", CORE)
    mine = lax.dynamic_slice_in_dim(wavefunctions, start, half, 1)
    theirs = exchanged(lax.dynamic_slice_in_dim(wavefunctions, other_start, half, 1), "domain", CORE)
    onward = [(source, source ^ (NEAR if source & CORE else FAR)) for source in range(lax.axis_size("domain"))]

    def unit(shard):
        near, far = exchanged(shard, "domain", NEAR), exchanged(shard, "domain", FAR)
        both = lax.ppermute(jnp.where(first, near, far), "domain", onward)
        return shard, near, far, both

    def reduced(shards):
        swapped = [exchanged(dot(theirs, shard), "domain", CORE) for shard in shards]
        partial = jnp.stack([dot(mine, shard) + other for shard, other in zip(shards, swapped)])
        rounded = partial.astype(jnp.bfloat16)
        place = chip ^ band
        total = lax.dynamic_index_in_dim(partial, place, 0, keepdims=False)
        for mask in range(1, lax.axis_size("band")):
            sent = lax.dynamic_index_in_dim(rounded, place ^ mask, 0, keepdims=False)
            total = total + exchanged(sent, "band", mask).astype(jnp.float32)
        return total

    left = unit(jnp.where(first, keep, received))
    right = unit(jnp.where(first, received, keep))
    return jnp.concatenate([reduced(left), reduced(right)], 1)


def rotate_any(wavefunctions, rotation):
    columns = lax.all_gather(rotation, "domain", axis=1, tiled=True)
    return lax.psum_scatter(dot(wavefunctions, columns), "band", scatter_dimension=1, tiled=True)


def local(wavefunctions, rotation, cell_matrices, cell_nodes, face_map):
    cells = cell_nodes.shape[0]
    own = wavefunctions.shape[0]
    extent = own + face_map.shape[0]
    held = jnp.bfloat16 if cells == 1 else jnp.float32

    places = jax.nn.one_hot(cell_nodes, extent, dtype=held)
    assembled = jnp.zeros((extent, extent), jnp.float32)
    for cell in range(cells):
        rows = dot(places[cell].T, cell_matrices[cell].astype(held)).astype(held)
        assembled = assembled + dot(rows, places[cell])
    assembled = assembled.astype(held)
    pick = jax.nn.one_hot(face_map, own, dtype=held)
    corner = shifted(assembled[own:, own:], "domain", 1)
    returned = dot(dot(pick.T, corner).astype(held), pick).astype(held)

    chips = lax.axis_size("domain") // 2
    square = chips == FAR and chips == lax.axis_size("band")
    rotated = (rotate_square if square else rotate_any)(wavefunctions, rotation)

    high, low = split(rotated)
    if cells == 1:
        def apply(matrix):
            return dot(matrix, high) + dot(matrix, low)
    else:
        def apply(matrix):
            return dot(matrix, rotated)

    faces = dot(pick, high.astype(held)).astype(jnp.bfloat16)
    incoming = shifted(faces, "domain", -1)
    back = shifted(apply(assembled[own:, :own]), "domain", 1)
    result = apply(assembled[:own, :own]) + apply(returned) + dot(assembled[:own, own:], incoming.astype(held))
    if cells == 1:
        back_high, back_low = split(back)
        return result + dot(pick.T, back_high) + dot(pick.T, back_low)
    return result + dot(pick.T, back)


def solution(mesh):
    in_specs = (
        P("domain", "band"),
        P("band", "domain"),
        P("domain", None, None),
        P("domain", None),
        P("domain"),
    )
    out_specs = P("domain", "band")
    return jax.shard_map(local, mesh=mesh, in_specs=in_specs, out_specs=out_specs, check_vma=False)
```

```python
import functools

import jax
import jax.numpy as jnp
from jax import lax
from jax.experimental import pallas as pl
from jax.experimental.pallas import tpu as pltpu
from jax.sharding import PartitionSpec as P

CORE, NEAR, FAR = 1, 2, 4
VMEM = pl.BlockSpec(memory_space=pltpu.VMEM)
ANY = pl.BlockSpec(memory_space=pl.ANY)
SMEM = pl.BlockSpec(memory_space=pltpu.SMEM)
F32, BF16 = jnp.float32, jnp.bfloat16


def dot(left, right):
    precision = lax.Precision.HIGHEST if left.dtype == F32 else None
    return jnp.dot(left, right, precision=precision, preferred_element_type=F32)


def split(value):
    high = value.astype(BF16)
    return high, (value - high.astype(F32)).astype(BF16)


def shifted(value, axis, steps):
    count = lax.axis_size(axis)
    leading, last = (max(0, -steps), min(count, count - steps))
    return lax.ppermute(value, axis, [(source, source + steps) for source in range(leading, last)])


def exchanged(value, axis, mask, core=None):
    sources = range(lax.axis_size(axis))
    return lax.ppermute(value, axis, [(source, source ^ mask) for source in sources if core in (None, source & CORE)])


def call(kernel, outs, operands, flops=0, scalars=1, after=(), space=VMEM, scratch=()):
    size = sum(value.size * value.dtype.itemsize for value in (*operands, *outs))
    count = len(operands)

    def body(*refs):
        kernel(*refs[:count], *refs[count + len(after) :])

    return pl.pallas_call(
        body,
        out_shape=outs,
        in_specs=[SMEM] * scalars + [space] * (count - scalars) + [ANY] * len(after),
        out_specs=[VMEM] * len(outs),
        scratch_shapes=list(scratch),
        cost_estimate=pl.CostEstimate(flops=flops, bytes_accessed=size, transcendentals=0),
        compiler_params=pltpu.CompilerParams(vmem_limit_bytes=48 * 2**20),
    )(*operands, *after)


def shape(*dims, dtype=F32):
    return jax.ShapeDtypeStruct(dims, dtype)


def shard_kernel(side, place, own, other, out, done):
    half = out.shape[0]

    def fill(source):
        start = pl.multiple_of(place[0] * half, half)
        copy = pltpu.make_async_copy(source.at[pl.ds(start, half)], out, done)
        copy.start()
        copy.wait()

    pl.when(place[0] == side)(lambda: fill(own))
    pl.when(place[0] != side)(lambda: fill(other))


def product(states, place, piece):
    half = piece.shape[0]
    start = pl.multiple_of(place[0] * half, half)
    return jnp.dot(states[:, pl.ds(start, half)], piece[...], preferred_element_type=F32)


def early_kernel(count, place, states, *refs):
    pieces, out = refs[:count], refs[count]
    for slot, piece in enumerate(pieces):
        out[slot] = product(states, place, piece)


def late_kernel(place, states, even, odd, out):
    @pl.when(place[0] == 0)
    def _():
        out[...] = product(states, place, even)

    @pl.when(place[0] == 1)
    def _():
        out[...] = product(states, place, odd)


def pick_kernel(count, place, early, late, early_other, late_other, kept, *sent):
    where = place[1]
    last = early.shape[0]

    def store(slot, out):
        @pl.when(slot < last)
        def _():
            out[...] = (early[jnp.minimum(slot, last - 1)] + early_other[jnp.minimum(slot, last - 1)]).astype(out.dtype)

        @pl.when(slot == last)
        def _():
            out[...] = (late[...] + late_other[...]).astype(out.dtype)

    store(where, kept)
    for mask, out in zip(range(1, count), sent):
        store(where ^ mask, out)


def rotate_square(wavefunctions, rotation, operator):
    domain, band = lax.axis_index("domain"), lax.axis_index("band")
    bands = lax.axis_size("band")
    place = jnp.stack([domain % 2, (domain // 2) ^ band])
    rows, states = wavefunctions.shape
    width = rotation.shape[1]
    half = states // 2
    flops = 2 * rows * half * width
    swapped = exchanged(rotation, "domain", CORE)

    def shard(side, after):
        kernel, outs = functools.partial(shard_kernel, side), [shape(half, width, dtype=BF16)]
        scratch = (pltpu.SemaphoreType.DMA,)
        return call(kernel, outs, (place, rotation, swapped), after=after, space=ANY, scratch=scratch)[0]

    def early(who, pieces, after=()):
        count = len(pieces)
        kernel = functools.partial(early_kernel, count)
        return call(kernel, [shape(count, rows, width)], (place, who, *pieces), count * flops, after=after)[0]

    def late(who, even, odd, after=()):
        return call(late_kernel, [shape(rows, width)], (place, who, even, odd), flops, after=after)[0]

    def picked(early_mine, late_mine, early_other, late_other):
        outs = [shape(rows, width)] + [shape(rows, width, dtype=BF16)] * (bands - 1)
        return call(
            functools.partial(pick_kernel, bands), outs, (place, early_mine, late_mine, early_other, late_other)
        )

    def spread(kept, *sent):
        return [kept] + [exchanged(value, "band", mask) for mask, value in zip(range(1, bands), sent)]

    def gathered(piece):
        return exchanged(piece, "domain", NEAR), exchanged(piece, "domain", FAR)

    def forwarded(near, far):
        return exchanged(near, "domain", FAR, 0), exchanged(far, "domain", NEAR, CORE)

    left = shard(0, ())
    near, far = gathered(left)
    other, left = lax.optimization_barrier((wavefunctions, left))
    theirs = exchanged(other, "domain", CORE)
    assembled, pick, returned = operator()
    near, far, returned = lax.optimization_barrier((near, far, returned))
    even, odd = forwarded(near, far)
    early_theirs = early(theirs, (left, near, far))
    early_other = exchanged(early_theirs, "domain", CORE)
    right = shard(1, (early_theirs,))
    right_near, right_far = gathered(right)
    early_mine = early(wavefunctions, (left, near, far), (right,))
    late_theirs = late(theirs, even, odd)
    late_other = exchanged(late_theirs, "domain", CORE)
    late_mine = late(wavefunctions, even, odd, (late_theirs,))
    left_out = picked(early_mine, late_mine, early_other, late_other)
    left_parts = spread(*left_out)

    right_near, right_far, sent = lax.optimization_barrier((right_near, right_far, left_out[1]))
    even, odd = forwarded(right_near, right_far)
    early_theirs = early(theirs, (right, right_near, right_far), (sent,))
    early_other = exchanged(early_theirs, "domain", CORE)
    early_mine = early(wavefunctions, (right, right_near, right_far), (early_theirs,))
    late_theirs = late(theirs, even, odd)
    late_other = exchanged(late_theirs, "domain", CORE)
    late_mine = late(wavefunctions, even, odd, (late_theirs,))
    right_parts = spread(*picked(early_mine, late_mine, early_other, late_other))
    return (left_parts, right_parts), (assembled, pick, returned)


def rotate_any(wavefunctions, rotation):
    columns = lax.all_gather(rotation, "domain", axis=1, tiled=True)
    return lax.psum_scatter(dot(wavefunctions, columns), "band", scatter_dimension=1, tiled=True)


def faces_kernel(count, width, *refs):
    parts, (assembled, pick, total, faces, back) = refs[: 2 * count], refs[2 * count :]
    own = total.shape[0]
    for side in range(2):
        some = parts[side * count : (side + 1) * count]
        value = some[0][...]
        for part in some[1:]:
            value = value + part[...].astype(F32)
        columns = slice(side * width, (side + 1) * width)
        total[:, columns] = value
        high, low = split(value)
        faces[:, columns] = dot(pick[...], high).astype(BF16)
        outward = assembled[own:, :own]
        back[:, columns] = dot(outward, high) + dot(outward, low)


def inner_kernel(total, assembled, returned, out):
    own = total.shape[0]
    high, low = split(total[...])
    inner = assembled[:own, :own]
    out[...] = dot(inner, high) + dot(inner, low) + dot(returned[...], high) + dot(returned[...], low)


def final_kernel(inner, assembled, spread, incoming, back, out):
    own = inner.shape[0]
    high, low = split(back[...])
    out[...] = inner[...] + dot(assembled[:own, own:], incoming[...]) + dot(spread[...], high) + dot(spread[...], low)


def finish_square(parts, operator):
    (left, right), (assembled, pick, returned) = parts, operator
    rows, width = left[0].shape
    faces_count = pick.shape[0]
    columns = 2 * width
    total, faces, back = call(
        functools.partial(faces_kernel, len(left), width),
        [shape(rows, columns), shape(faces_count, columns, dtype=BF16), shape(faces_count, columns)],
        (*left, *right, assembled, pick),
        scalars=0,
    )
    incoming, back = shifted(faces, "domain", -1), shifted(back, "domain", 1)
    inner = call(inner_kernel, [shape(rows, columns)], (total, assembled, returned), 8 * rows * rows * columns, scalars=0)[0]
    return call(final_kernel, [shape(rows, columns)], (inner, assembled, pick.T, incoming, back), scalars=0)[0]


def finish_any(rotated, assembled, pick, returned):
    own = rotated.shape[0]
    rotated = rotated.astype(BF16).astype(assembled.dtype)
    incoming = shifted(dot(pick, rotated).astype(BF16), "domain", -1).astype(assembled.dtype)
    back = shifted(dot(assembled[own:, :own], rotated), "domain", 1)
    inner = dot(assembled[:own, :own], rotated) + dot(returned, rotated) + dot(assembled[:own, own:], incoming)
    return inner + dot(pick.T.astype(F32), back)


def assemble(cell_matrices, cell_nodes, face_map, own):
    cells = cell_nodes.shape[0]
    extent = own + face_map.shape[0]
    held = BF16 if cells == 1 else F32
    places = jax.nn.one_hot(cell_nodes, extent, dtype=held)
    assembled = jnp.zeros((extent, extent), F32)
    for cell in range(cells):
        rows = dot(places[cell].T, cell_matrices[cell].astype(held)).astype(held)
        assembled = assembled + dot(rows, places[cell])
    assembled = assembled.astype(held)
    pick = jax.nn.one_hot(face_map, own, dtype=held)
    corner = shifted(assembled[own:, own:], "domain", 1)
    returned = dot(dot(pick.T, corner).astype(held), pick).astype(held)
    return assembled, pick, returned


def local(wavefunctions, rotation, cell_matrices, cell_nodes, face_map):
    operator = functools.partial(assemble, cell_matrices, cell_nodes, face_map, wavefunctions.shape[0])
    chips = lax.axis_size("domain") // 2
    if chips == FAR and chips == lax.axis_size("band") and cell_nodes.shape[0] == 1:
        return finish_square(*rotate_square(wavefunctions, rotation, operator))
    return finish_any(rotate_any(wavefunctions, rotation), *operator())


def solution(mesh):
    in_specs = (
        P("domain", "band"),
        P("band", "domain"),
        P("domain", None, None),
        P("domain", None),
        P("domain"),
    )
    out_specs = P("domain", "band")
    return jax.shard_map(local, mesh=mesh, in_specs=in_specs, out_specs=out_specs, check_vma=False)
```

```python
import functools

import jax
import jax.numpy as jnp
from jax import lax
from jax.experimental import pallas as pl
from jax.experimental.pallas import tpu as pltpu
from jax.sharding import PartitionSpec as P

CORE, NEAR, FAR = 1, 2, 4
VMEM = pl.BlockSpec(memory_space=pltpu.VMEM)
ANY = pl.BlockSpec(memory_space=pl.ANY)
F32, BF16 = jnp.float32, jnp.bfloat16


def dot(left, right):
    precision = lax.Precision.HIGHEST if left.dtype == F32 else None
    return jnp.dot(left, right, precision=precision, preferred_element_type=F32)


def split(value):
    high = value.astype(BF16)
    return high, (value - high.astype(F32)).astype(BF16)


def shifted(value, axis, steps):
    count = lax.axis_size(axis)
    leading, last = (max(0, -steps), min(count, count - steps))
    return lax.ppermute(value, axis, [(source, source + steps) for source in range(leading, last)])


def exchanged(value, axis, mask, core=None):
    sources = range(lax.axis_size(axis))
    return lax.ppermute(value, axis, [(source, source ^ mask) for source in sources if core in (None, source & CORE)])


def call(kernel, outs, operands, after=(), spaces=None, scratch=()):
    count = len(operands)

    def body(*refs):
        kernel(*refs[:count], *refs[count + len(after) :])

    return pl.pallas_call(
        body,
        out_shape=outs,
        in_specs=[pl.BlockSpec(memory_space=space) for space in spaces or [pltpu.VMEM] * count] + [ANY] * len(after),
        out_specs=[VMEM] * len(outs),
        scratch_shapes=list(scratch),
        cost_estimate=pl.CostEstimate(flops=0, bytes_accessed=1024, transcendentals=0),
        compiler_params=pltpu.CompilerParams(vmem_limit_bytes=24 * 2**20),
    )(*operands, *after)


def shape(*dims, dtype=F32):
    return jax.ShapeDtypeStruct(dims, dtype)


def core():
    return lax.rem(lax.axis_index("domain"), 2)


def half_kernel(source, out, done):
    half = out.shape[0]
    copy = pltpu.make_async_copy(source.at[pl.ds(pl.multiple_of(core() * half, half), half)], out, done)
    copy.start()
    copy.wait()


def choose_kernel(even, odd, out):
    first = core() == 0

    @pl.when(first)
    def _():
        out[...] = even[...]

    @pl.when(jnp.logical_not(first))
    def _():
        out[...] = odd[...]


def products(states, pieces):
    half = pieces.shape[0]
    start = pl.multiple_of(core() * half, half)
    return jnp.dot(states[:, pl.ds(start, half)], pieces, preferred_element_type=F32)


def early_kernel(counts, mine, theirs, *refs):
    pieces = []
    for slot, count in enumerate(counts):
        value = refs[0][...]
        for other in refs[1:count]:
            value = jnp.where(core() == 0, value, other[...]) if slot == 0 else value + other[...]
        refs = refs[count:]
        pieces.append(value)
    own, others = refs
    width = pieces[0].shape[1]
    for first in range(0, len(pieces), 2):
        group = pieces[first : first + 2]
        wide = group[0] if len(group) == 1 else jnp.concatenate(group, 1)
        for states, out in ((theirs, others), (mine, own)):
            result = products(states, wide)
            for slot in range(len(group)):
                out[first + slot] = result[:, slot * width : (slot + 1) * width]


def late_kernel(states, even, odd, out):
    out[...] = products(states, even[...] + odd[...])


def pick_kernel(count, early, late, early_other, late_other, kept, *sent):
    where = lax.bitwise_xor(lax.div(lax.axis_index("domain"), 2), lax.axis_index("band"))
    last = early.shape[0]

    def store(slot, out):
        @pl.when(slot < last)
        def _():
            out[...] = (early[jnp.minimum(slot, last - 1)] + early_other[jnp.minimum(slot, last - 1)]).astype(out.dtype)

        @pl.when(slot == last)
        def _():
            out[...] = (late[...] + late_other[...]).astype(out.dtype)

    store(where, kept)
    for mask, out in zip(range(1, count), sent):
        store(lax.bitwise_xor(where, mask), out)


def sum_kernel(*refs):
    value = refs[0][...]
    for part in refs[1:-1]:
        value = value + part[...].astype(F32)
    refs[-1][...] = value


def rotate_square(wavefunctions, rotation, operator):
    bands = lax.axis_size("band")
    rows, states = wavefunctions.shape
    width = rotation.shape[1]
    half = states // 2
    piece = [shape(half, width, dtype=BF16)]

    def halved(value, space, after=()):
        return call(half_kernel, piece, (value,), after=after, spaces=[space], scratch=[pltpu.SemaphoreType.DMA])[0]

    def early(counts, pieces, after=()):
        outs = [shape(len(counts), rows, width)] * 2
        kernel = functools.partial(early_kernel, counts)
        own, others = call(kernel, outs, (wavefunctions, theirs, *pieces), after)
        return own, exchanged(others, "domain", CORE), others

    def late(even, odd, after=()):
        others = call(late_kernel, [shape(rows, width)], (theirs, even, odd), after)[0]
        own = call(late_kernel, [shape(rows, width)], (wavefunctions, even, odd), (others,))[0]
        return own, exchanged(others, "domain", CORE)

    def spread(early_own, early_other, late_own, late_other, after=()):
        outs = [shape(rows, width)] + [shape(rows, width, dtype=BF16)] * (bands - 1)
        kernel = functools.partial(pick_kernel, bands)
        kept, *sent = call(kernel, outs, (early_own, late_own, early_other, late_other), after=after)
        return [kept] + [exchanged(value, "band", mask) for mask, value in zip(range(1, bands), sent)], sent[0]

    swapped = exchanged(rotation, "domain", CORE)
    keep = halved(rotation, pltpu.HBM)
    near_even, far_even = exchanged(keep, "domain", NEAR, 0), exchanged(keep, "domain", FAR, 0)
    received = halved(swapped, pl.ANY, (keep,))
    near_odd, far_odd = exchanged(received, "domain", NEAR, CORE), exchanged(received, "domain", FAR, CORE)
    other, received = lax.optimization_barrier((wavefunctions, received))
    theirs = exchanged(other, "domain", CORE)
    operator = operator()
    right = call(choose_kernel, piece, (received, keep), after=operator[:1])[0]
    near, far = exchanged(right, "domain", NEAR), exchanged(right, "domain", FAR)

    near_even, far_odd, right = lax.optimization_barrier((near_even, far_odd, right))
    even, odd = exchanged(near_even, "domain", FAR, 0), exchanged(far_odd, "domain", NEAR, CORE)
    early_own, early_other, token = early((2, 2, 2), (keep, received, near_even, near_odd, far_even, far_odd))

    near, far, token = lax.optimization_barrier((near, far, token))
    right_even, right_odd = exchanged(near, "domain", FAR, 0), exchanged(far, "domain", NEAR, CORE)

    late_own, late_other = late(even, odd, (token, near, far))
    left_parts, token = spread(early_own, early_other, late_own, late_other)
    left_total = call(sum_kernel, [shape(rows, width)], left_parts)[0]

    early_own, early_other, token = early((1, 1, 1), (right, near, far), (token,))
    late_own, late_other = late(right_even, right_odd, (token,))
    right_parts, _ = spread(early_own, early_other, late_own, late_other, (left_total,))
    return left_total, right_parts, operator


def rotate_any(wavefunctions, rotation):
    columns = lax.all_gather(rotation, "domain", axis=1, tiled=True)
    return lax.psum_scatter(dot(wavefunctions, columns), "band", scatter_dimension=1, tiled=True)


def faces_kernel(width, *refs):
    left, *parts, assembled, pick, total, faces, back = refs
    own = total.shape[0]
    value = parts[0][...]
    for part in parts[1:]:
        value = value + part[...].astype(F32)
    for side, half in enumerate((left[...], value)):
        columns = slice(side * width, (side + 1) * width)
        total[:, columns] = half
        high, low = split(half)
        faces[:, columns] = dot(pick[...], high).astype(BF16)
        outward = assembled[own:, :own]
        back[:, columns] = dot(outward, high) + dot(outward, low)


def inner_kernel(total, assembled, corner, pick, spread, out):
    own = total.shape[0]
    high, low = split(total[...])
    inner = assembled[:own, :own]
    face_high, face_low = dot(pick[...], high).astype(BF16), dot(pick[...], low).astype(BF16)
    back_high, back_low = split(dot(corner[...], face_high) + dot(corner[...], face_low))
    out[...] = dot(inner, high) + dot(inner, low) + dot(spread[...], back_high) + dot(spread[...], back_low)


def final_kernel(inner, assembled, spread, incoming, back, out):
    own = inner.shape[0]
    high, low = split(back[...])
    out[...] = inner[...] + dot(assembled[:own, own:], incoming[...]) + dot(spread[...], high) + dot(spread[...], low)


def finish_square(left, parts, operator):
    assembled, corner, pick, spread = operator
    rows, width = left.shape
    faces_count = pick.shape[0]
    columns = 2 * width
    total, faces, back = call(
        functools.partial(faces_kernel, width),
        [shape(rows, columns), shape(faces_count, columns, dtype=BF16), shape(faces_count, columns)],
        (left, *parts, assembled, pick),
    )
    incoming, back = shifted(faces, "domain", -1), shifted(back, "domain", 1)
    inner = call(inner_kernel, [shape(rows, columns)], (total, assembled, corner, pick, spread))[0]
    return call(final_kernel, [shape(rows, columns)], (inner, assembled, spread, incoming, back))[0]


def finish_any(rotated, cell_matrices, cell_nodes, face_map):
    own = rotated.shape[0]
    assembled, pick, returned = assemble_any(cell_matrices, cell_nodes, face_map, own)
    rotated = rotated.astype(BF16).astype(assembled.dtype)
    incoming = shifted(dot(pick, rotated).astype(BF16), "domain", -1).astype(assembled.dtype)
    back = shifted(dot(assembled[own:, :own], rotated), "domain", 1)
    inner = dot(assembled[:own, :own], rotated) + dot(returned, rotated) + dot(assembled[:own, own:], incoming)
    return inner + dot(pick.T.astype(F32), back)


def assemble_any(cell_matrices, cell_nodes, face_map, own):
    cells = cell_nodes.shape[0]
    extent = own + face_map.shape[0]
    held = BF16 if cells == 1 else F32
    places = jax.nn.one_hot(cell_nodes, extent, dtype=held)
    assembled = jnp.zeros((extent, extent), F32)
    for cell in range(cells):
        rows = dot(places[cell].T, cell_matrices[cell].astype(held)).astype(held)
        assembled = assembled + dot(rows, places[cell])
    assembled = assembled.astype(held)
    pick = jax.nn.one_hot(face_map, own, dtype=held)
    corner = shifted(assembled[own:, own:], "domain", 1)
    returned = dot(dot(pick.T, corner).astype(held), pick).astype(held)
    return assembled, pick, returned


def assemble_kernel(matrix, nodes, faces, assembled, corner, pick, spread):
    own, extent = spread.shape[0], assembled.shape[0]
    places = jnp.where(lax.broadcasted_iota(jnp.int32, (extent, extent), 0) == nodes[...], 1.0, 0.0).astype(BF16)
    rows = dot(places, matrix[0]).astype(BF16)
    whole = lax.dot_general(rows, places, (((1,), (1,)), ((), ())), preferred_element_type=F32).astype(BF16)
    assembled[...] = whole
    corner[...] = whole[own:, own:]
    chosen = jnp.where(lax.broadcasted_iota(jnp.int32, spread.shape, 0) == faces[...], 1.0, 0.0)
    spread[...] = chosen.astype(BF16)
    pick[...] = chosen.T.astype(BF16)


def assemble(cell_matrices, cell_nodes, face_map, own):
    shared = face_map.shape[0]
    outs = [(own + shared, own + shared), (shared, shared), (shared, own), (own, shared)]
    operands = (cell_matrices, cell_nodes, face_map.reshape(1, shared))
    assembled, corner, pick, spread = call(assemble_kernel, [shape(*dims, dtype=BF16) for dims in outs], operands)
    return assembled, shifted(corner, "domain", 1), pick, spread


def local(wavefunctions, rotation, cell_matrices, cell_nodes, face_map):
    chips = lax.axis_size("domain") // 2
    if chips == FAR and chips == lax.axis_size("band") and cell_nodes.shape[0] == 1:
        operator = functools.partial(assemble, cell_matrices, cell_nodes, face_map, wavefunctions.shape[0])
        return finish_square(*rotate_square(wavefunctions, rotation, operator))
    return finish_any(rotate_any(wavefunctions, rotation), cell_matrices, cell_nodes, face_map)


def solution(mesh):
    in_specs = (
        P("domain", "band"),
        P("band", "domain"),
        P("domain", None, None),
        P("domain", None),
        P("domain"),
    )
    out_specs = P("domain", "band")
    return jax.shard_map(local, mesh=mesh, in_specs=in_specs, out_specs=out_specs, check_vma=False)
```

```python
import functools

import jax
import jax.numpy as jnp
from jax import lax
from jax.experimental import pallas as pl
from jax.experimental.pallas import tpu as pltpu
from jax.sharding import PartitionSpec as P

CORE, NEAR, FAR = 1, 2, 4
VMEM = pl.BlockSpec(memory_space=pltpu.VMEM)
ANY = pl.BlockSpec(memory_space=pl.ANY)
F32, BF16 = jnp.float32, jnp.bfloat16


def dot(left, right):
    precision = lax.Precision.HIGHEST if left.dtype == F32 else None
    return jnp.dot(left, right, precision=precision, preferred_element_type=F32)


def split(value):
    high = value.astype(BF16)
    return high, (value - high.astype(F32)).astype(BF16)


def shifted(value, axis, steps):
    count = lax.axis_size(axis)
    leading, last = (max(0, -steps), min(count, count - steps))
    return lax.ppermute(value, axis, [(source, source + steps) for source in range(leading, last)])


def exchanged(value, axis, mask, core=None):
    sources = range(lax.axis_size(axis))
    return lax.ppermute(value, axis, [(source, source ^ mask) for source in sources if core in (None, source & CORE)])


def call(kernel, outs, operands, after=(), spaces=None, scratch=()):
    count = len(operands)

    def body(*refs):
        kernel(*refs[:count], *refs[count + len(after) :])

    return pl.pallas_call(
        body,
        out_shape=outs,
        in_specs=[pl.BlockSpec(memory_space=space) for space in spaces or [pltpu.VMEM] * count] + [ANY] * len(after),
        out_specs=[VMEM] * len(outs),
        scratch_shapes=list(scratch),
        cost_estimate=pl.CostEstimate(flops=0, bytes_accessed=1024, transcendentals=0),
        compiler_params=pltpu.CompilerParams(vmem_limit_bytes=24 * 2**20),
    )(*operands, *after)


def shape(*dims, dtype=F32):
    return jax.ShapeDtypeStruct(dims, dtype)


def core():
    return lax.rem(lax.axis_index("domain"), 2)


def block_of_band():
    return lax.bitwise_xor(lax.div(lax.axis_index("domain"), 2), lax.axis_index("band"))


def multiply(mine, theirs, pieces, store):
    rows, width = mine.shape[0], pieces[0].shape[1]
    for first in range(0, len(pieces), 2):
        group = pieces[first : first + 2]
        wide = group[0] if len(group) == 1 else jnp.concatenate(group, 1)
        for side, states in enumerate((mine, theirs)):
            result = jnp.dot(states[...], wide, preferred_element_type=F32)
            for slot in range(len(group)):
                store(first + slot, slice(side * rows, (side + 1) * rows), result[:, slot * width : (slot + 1) * width])


def halves_kernel(near_even, far_even, near_odd, far_odd, top, bottom, done):
    half = top.shape[0]

    def fill(near, far):
        copies = [
            pltpu.make_async_copy(near.at[pl.ds(0, half)], top, done.at[0]),
            pltpu.make_async_copy(far.at[pl.ds(half, half)], bottom, done.at[1]),
        ]
        for copy in copies:
            copy.start()
        for copy in copies:
            copy.wait()

    pl.when(core() == 0)(lambda: fill(near_even, far_even))
    pl.when(core() != 0)(lambda: fill(near_odd, far_odd))


def early_kernel(mine, theirs, own, near_even, far_even, near_odd, far_odd, blocks):
    def store(slot, rows, value):
        blocks[slot, rows] = value

    first = core() == 0
    near, far = jnp.where(first, near_even[...], near_odd[...]), jnp.where(first, far_even[...], far_odd[...])
    multiply(mine, theirs, [own[...], near, far], store)


def late_kernel(mine, theirs, top, bottom, early, kept, *refs):
    sent, last = refs[:-1], refs[-1]
    half = top.shape[0]
    rows = mine.shape[0]
    for side, states in enumerate((mine, theirs)):
        result = jnp.dot(states[:, :half], top[...], preferred_element_type=F32)
        last[side * rows : (side + 1) * rows] = result + jnp.dot(states[:, half:], bottom[...], preferred_element_type=F32)
    count = early.shape[0]
    where = block_of_band()
    for mask, out in enumerate((kept, *sent)):
        slot = lax.bitwise_xor(where, mask)

        @pl.when(slot < count)
        def _():
            out[...] = early[jnp.minimum(slot, count - 1)].astype(out.dtype)

        @pl.when(slot == count)
        def _():
            out[...] = last[...].astype(out.dtype)


def sum_kernel(kept, *refs):
    parts, (mine, theirs) = refs[:-2], refs[-2:]
    value = kept[...]
    for part in parts:
        value = value + part[...].astype(F32)
    rows = mine.shape[0]
    mine[...] = value[:rows]
    theirs[...] = value[rows:]


def rotate_square(wavefunctions, rotation, operator):
    bands, chips = lax.axis_size("band"), lax.axis_size("domain") // 2
    rows, states = wavefunctions.shape
    width = rotation.shape[1]
    half = states // 2
    received = [exchanged(rotation, "domain", NEAR, 0), exchanged(rotation, "domain", FAR, 0)]
    theirs = exchanged(wavefunctions, "domain", CORE)
    operator = operator()
    later, _, _ = lax.optimization_barrier((rotation, theirs, operator[1]))
    received += [exchanged(later, "domain", NEAR, CORE), exchanged(later, "domain", FAR, CORE)]
    halves = [shape(half, width, dtype=BF16)] * 2
    top, bottom = call(halves_kernel, halves, received, scratch=[pltpu.SemaphoreType.DMA((2,))])
    top, bottom = exchanged(top, "domain", FAR), exchanged(bottom, "domain", NEAR)
    early = call(early_kernel, [shape(chips - 1, 2 * rows, width)], (wavefunctions, theirs, rotation, *received))[0]
    outs = [shape(2 * rows, width)] + [shape(2 * rows, width, dtype=BF16)] * (bands - 1)
    scratch = [pltpu.VMEM((2 * rows, width), F32)]
    kept, *sent = call(late_kernel, outs, (wavefunctions, theirs, top, bottom, early), scratch=scratch)
    parts = [exchanged(value, "band", mask) for mask, value in enumerate(sent, 1)]
    mine, others = call(sum_kernel, [shape(rows, width)] * 2, (kept, *parts))
    return mine, exchanged(others, "domain", CORE), operator


def rotate_any(wavefunctions, rotation):
    columns = lax.all_gather(rotation, "domain", axis=1, tiled=True)
    return lax.psum_scatter(dot(wavefunctions, columns), "band", scatter_dimension=1, tiled=True)


def faces_kernel(mine, other, assembled, pick, total, faces, back):
    own, width = mine.shape
    first = core() == 0
    for side, half in enumerate((jnp.where(first, mine[...], other[...]), jnp.where(first, other[...], mine[...]))):
        columns = slice(side * width, (side + 1) * width)
        total[:, columns] = half
        high, low = split(half)
        faces[:, columns] = dot(pick[...], high).astype(BF16)
        outward = assembled[own:, :own]
        back[:, columns] = dot(outward, high) + dot(outward, low)


def inner_kernel(total, assembled, corner, pick, spread, out):
    own = total.shape[0]
    high, low = split(total[...])
    inner = assembled[:own, :own]
    face_high, face_low = dot(pick[...], high).astype(BF16), dot(pick[...], low).astype(BF16)
    back_high, back_low = split(dot(corner[...], face_high) + dot(corner[...], face_low))
    out[...] = dot(inner, high) + dot(inner, low) + dot(spread[...], back_high) + dot(spread[...], back_low)


def final_kernel(inner, assembled, spread, incoming, back, out):
    own = inner.shape[0]
    high, low = split(back[...])
    out[...] = inner[...] + dot(assembled[:own, own:], incoming[...]) + dot(spread[...], high) + dot(spread[...], low)


def finish_square(mine, other, operator):
    assembled, corner, pick, spread = operator
    rows, width = mine.shape
    shared, columns = pick.shape[0], 2 * width
    outs = [shape(rows, columns), shape(shared, columns, dtype=BF16), shape(shared, columns)]
    total, faces, back = call(faces_kernel, outs, (mine, other, assembled, pick))
    incoming, back = shifted(faces, "domain", -1), shifted(back, "domain", 1)
    inner = call(inner_kernel, [shape(rows, columns)], (total, assembled, corner, pick, spread))[0]
    return call(final_kernel, [shape(rows, columns)], (inner, assembled, spread, incoming, back))[0]


def finish_any(rotated, cell_matrices, cell_nodes, face_map):
    own = rotated.shape[0]
    assembled, pick, returned = assemble_any(cell_matrices, cell_nodes, face_map, own)
    rotated = rotated.astype(BF16).astype(assembled.dtype)
    incoming = shifted(dot(pick, rotated).astype(BF16), "domain", -1).astype(assembled.dtype)
    back = shifted(dot(assembled[own:, :own], rotated), "domain", 1)
    inner = dot(assembled[:own, :own], rotated) + dot(returned, rotated) + dot(assembled[:own, own:], incoming)
    return inner + dot(pick.T.astype(F32), back)


def assemble_any(cell_matrices, cell_nodes, face_map, own):
    cells = cell_nodes.shape[0]
    extent = own + face_map.shape[0]
    held = BF16 if cells == 1 else F32
    places = jax.nn.one_hot(cell_nodes, extent, dtype=held)
    assembled = jnp.zeros((extent, extent), F32)
    for cell in range(cells):
        rows = dot(places[cell].T, cell_matrices[cell].astype(held)).astype(held)
        assembled = assembled + dot(rows, places[cell])
    assembled = assembled.astype(held)
    pick = jax.nn.one_hot(face_map, own, dtype=held)
    corner = shifted(assembled[own:, own:], "domain", 1)
    returned = dot(dot(pick.T, corner).astype(held), pick).astype(held)
    return assembled, pick, returned


def assemble_kernel(matrix, nodes, faces, assembled, corner, pick, spread):
    own, extent = spread.shape[0], assembled.shape[0]
    places = jnp.where(lax.broadcasted_iota(jnp.int32, (extent, extent), 0) == nodes[...], 1.0, 0.0).astype(BF16)
    rows = dot(places, matrix[0]).astype(BF16)
    whole = lax.dot_general(rows, places, (((1,), (1,)), ((), ())), preferred_element_type=F32).astype(BF16)
    assembled[...] = whole
    corner[...] = whole[own:, own:]
    chosen = jnp.where(lax.broadcasted_iota(jnp.int32, spread.shape, 0) == faces[...], 1.0, 0.0)
    spread[...] = chosen.astype(BF16)
    pick[...] = chosen.T.astype(BF16)


def assemble(cell_matrices, cell_nodes, face_map, own):
    shared = face_map.shape[0]
    outs = [(own + shared, own + shared), (shared, shared), (shared, own), (own, shared)]
    operands = (cell_matrices, cell_nodes, face_map.reshape(1, shared))
    assembled, corner, pick, spread = call(assemble_kernel, [shape(*dims, dtype=BF16) for dims in outs], operands)
    return assembled, shifted(corner, "domain", 1), pick, spread


def local(wavefunctions, rotation, cell_matrices, cell_nodes, face_map):
    chips = lax.axis_size("domain") // 2
    if chips == FAR and chips == lax.axis_size("band") and cell_nodes.shape[0] == 1:
        operator = functools.partial(assemble, cell_matrices, cell_nodes, face_map, wavefunctions.shape[0])
        return finish_square(*rotate_square(wavefunctions, rotation, operator))
    return finish_any(rotate_any(wavefunctions, rotation), cell_matrices, cell_nodes, face_map)


def solution(mesh):
    in_specs = (
        P("domain", "band"),
        P("band", "domain"),
        P("domain", None, None),
        P("domain", None),
        P("domain"),
    )
    out_specs = P("domain", "band")
    return jax.shard_map(local, mesh=mesh, in_specs=in_specs, out_specs=out_specs, check_vma=False)
```

```python
import functools

import jax
import jax.numpy as jnp
from jax import lax
from jax.experimental import pallas as pl
from jax.experimental.pallas import tpu as pltpu
from jax.sharding import PartitionSpec as P

CORE, NEAR, FAR = 1, 2, 4
VMEM = pl.BlockSpec(memory_space=pltpu.VMEM)
ANY = pl.BlockSpec(memory_space=pl.ANY)
F32, BF16 = jnp.float32, jnp.bfloat16


def dot(left, right):
    precision = lax.Precision.HIGHEST if left.dtype == F32 else None
    return jnp.dot(left, right, precision=precision, preferred_element_type=F32)


def split(value):
    high = value.astype(BF16)
    return high, (value - high.astype(F32)).astype(BF16)


def shifted(value, axis, steps):
    count = lax.axis_size(axis)
    leading, last = (max(0, -steps), min(count, count - steps))
    return lax.ppermute(value, axis, [(source, source + steps) for source in range(leading, last)])


def exchanged(value, axis, mask, core=None):
    sources = range(lax.axis_size(axis))
    return lax.ppermute(value, axis, [(source, source ^ mask) for source in sources if core in (None, source & CORE)])


def call(kernel, outs, operands, after=(), spaces=None, scratch=()):
    count = len(operands)

    def body(*refs):
        kernel(*refs[:count], *refs[count + len(after) :])

    return pl.pallas_call(
        body,
        out_shape=outs,
        in_specs=[pl.BlockSpec(memory_space=space) for space in spaces or [pltpu.VMEM] * count] + [ANY] * len(after),
        out_specs=[VMEM] * len(outs),
        scratch_shapes=list(scratch),
        cost_estimate=pl.CostEstimate(flops=0, bytes_accessed=1024, transcendentals=0),
        compiler_params=pltpu.CompilerParams(vmem_limit_bytes=24 * 2**20),
    )(*operands, *after)


def shape(*dims, dtype=F32):
    return jax.ShapeDtypeStruct(dims, dtype)


def core():
    return lax.rem(lax.axis_index("domain"), 2)


def block_of_band():
    return lax.bitwise_xor(lax.div(lax.axis_index("domain"), 2), lax.axis_index("band"))


def halves_kernel(near_even, far_even, near_odd, far_odd, top, bottom, done):
    half = top.shape[0]

    def fill(near, far):
        copies = [
            pltpu.make_async_copy(near.at[pl.ds(0, half)], top, done.at[0]),
            pltpu.make_async_copy(far.at[pl.ds(half, half)], bottom, done.at[1]),
        ]
        for copy in copies:
            copy.start()
        for copy in copies:
            copy.wait()

    pl.when(core() == 0)(lambda: fill(near_even, far_even))
    pl.when(core() != 0)(lambda: fill(near_odd, far_odd))


def own_kernel(mine, theirs, own, block):
    rows = mine.shape[0]
    for side, states in enumerate((mine, theirs)):
        block[side * rows : (side + 1) * rows] = jnp.dot(states[...], own[...], preferred_element_type=F32)


def early_kernel(mine, theirs, near_even, far_even, near_odd, far_odd, near_block, far_block):
    rows, width = mine.shape[0], near_even.shape[1]
    first = core() == 0
    near, far = jnp.where(first, near_even[...], near_odd[...]), jnp.where(first, far_even[...], far_odd[...])
    wide = jnp.concatenate([near, far], 1)
    for side, states in enumerate((mine, theirs)):
        result = jnp.dot(states[...], wide, preferred_element_type=F32)
        near_block[side * rows : (side + 1) * rows] = result[:, :width]
        far_block[side * rows : (side + 1) * rows] = result[:, width:]


def late_kernel(mine, theirs, top, bottom, own, near, far, kept, *refs):
    sent, last = refs[:-1], refs[-1]
    half = top.shape[0]
    rows = mine.shape[0]
    for side, states in enumerate((mine, theirs)):
        result = jnp.dot(states[:, :half], top[...], preferred_element_type=F32)
        last[side * rows : (side + 1) * rows] = result + jnp.dot(states[:, half:], bottom[...], preferred_element_type=F32)
    where = block_of_band()

    def store(out, slot, block):
        @pl.when(slot == lax.bitwise_xor(where, mask))
        def _():
            out[...] = block[...].astype(out.dtype)

    for mask, out in enumerate((kept, *sent)):
        for slot, block in enumerate((own, near, far, last)):
            store(out, slot, block)


def sum_kernel(kept, *refs):
    parts, (mine, theirs) = refs[:-2], refs[-2:]
    value = kept[...]
    for part in parts:
        value = value + part[...].astype(F32)
    rows = mine.shape[0]
    mine[...] = value[:rows]
    theirs[...] = value[rows:]


def rotate_square(wavefunctions, rotation, operator):
    bands, chips = lax.axis_size("band"), lax.axis_size("domain") // 2
    rows, states = wavefunctions.shape
    width = rotation.shape[1]
    half = states // 2
    received = [exchanged(rotation, "domain", NEAR, 0), exchanged(rotation, "domain", FAR, 0)]
    theirs = exchanged(wavefunctions, "domain", CORE)
    block = [shape(2 * rows, width)]
    own = call(own_kernel, block, (wavefunctions, theirs, rotation))[0]
    operator = operator(own)
    later, _ = lax.optimization_barrier((rotation, operator[0]))
    received += [exchanged(later, "domain", NEAR, CORE), exchanged(later, "domain", FAR, CORE)]
    halves = [shape(half, width, dtype=BF16)] * 2
    top, bottom = call(halves_kernel, halves, received, scratch=[pltpu.SemaphoreType.DMA((2,))])
    top, bottom = exchanged(top, "domain", FAR), exchanged(bottom, "domain", NEAR)
    early = call(early_kernel, block * 2, (wavefunctions, theirs, *received))
    outs = block + [shape(2 * rows, width, dtype=BF16)] * (bands - 1)
    scratch = [pltpu.VMEM((2 * rows, width), F32)]
    kept, *sent = call(late_kernel, outs, (wavefunctions, theirs, top, bottom, own, *early), scratch=scratch)
    parts = [exchanged(value, "band", mask) for mask, value in enumerate(sent, 1)]
    mine, others = call(sum_kernel, [shape(rows, width)] * 2, (kept, *parts))
    return mine, exchanged(others, "domain", CORE), operator


def rotate_any(wavefunctions, rotation):
    columns = lax.all_gather(rotation, "domain", axis=1, tiled=True)
    return lax.psum_scatter(dot(wavefunctions, columns), "band", scatter_dimension=1, tiled=True)


def faces_kernel(mine, other, assembled, pick, total, faces, back):
    own, width = mine.shape
    first = core() == 0
    for side, half in enumerate((jnp.where(first, mine[...], other[...]), jnp.where(first, other[...], mine[...]))):
        columns = slice(side * width, (side + 1) * width)
        total[:, columns] = half
        high, low = split(half)
        faces[:, columns] = dot(pick[...], high).astype(BF16)
        outward = assembled[own:, :own]
        back[:, columns] = dot(outward, high) + dot(outward, low)
    back[:, 2 * width :] = assembled[own:, own:].astype(F32)


def inner_kernel(total, assembled, pick, out, face_high, face_low):
    own = total.shape[0]
    high, low = split(total[...])
    inner = assembled[:own, :own]
    out[...] = dot(inner, high) + dot(inner, low)
    face_high[...] = dot(pick[...], high).astype(BF16)
    face_low[...] = dot(pick[...], low).astype(BF16)


def final_kernel(inner, face_high, face_low, assembled, spread, incoming, back, out):
    own, columns = inner.shape
    corner = back[:, columns:].astype(BF16)
    high, low = split(back[:, :columns] + dot(corner, face_high[...]) + dot(corner, face_low[...]))
    out[...] = inner[...] + dot(assembled[:own, own:], incoming[...]) + dot(spread[...], high) + dot(spread[...], low)


def finish_square(mine, other, operator):
    assembled, pick, spread = operator
    rows, width = mine.shape
    shared, columns = pick.shape[0], 2 * width
    outs = [shape(rows, columns), shape(shared, columns, dtype=BF16), shape(shared, columns + shared)]
    total, faces, back = call(faces_kernel, outs, (mine, other, assembled, pick))
    incoming, back = shifted(faces, "domain", -1), shifted(back, "domain", 1)
    outs = [shape(rows, columns)] + [shape(shared, columns, dtype=BF16)] * 2
    inner, *face = call(inner_kernel, outs, (total, assembled, pick))
    return call(final_kernel, outs[:1], (inner, *face, assembled, spread, incoming, back))[0]


def finish_any(rotated, cell_matrices, cell_nodes, face_map):
    own = rotated.shape[0]
    assembled, pick, returned = assemble_any(cell_matrices, cell_nodes, face_map, own)
    rotated = rotated.astype(BF16).astype(assembled.dtype)
    incoming = shifted(dot(pick, rotated).astype(BF16), "domain", -1).astype(assembled.dtype)
    back = shifted(dot(assembled[own:, :own], rotated), "domain", 1)
    inner = dot(assembled[:own, :own], rotated) + dot(returned, rotated) + dot(assembled[:own, own:], incoming)
    return inner + dot(pick.T.astype(F32), back)


def assemble_any(cell_matrices, cell_nodes, face_map, own):
    cells = cell_nodes.shape[0]
    extent = own + face_map.shape[0]
    held = BF16 if cells == 1 else F32
    places = jax.nn.one_hot(cell_nodes, extent, dtype=held)
    assembled = jnp.zeros((extent, extent), F32)
    for cell in range(cells):
        rows = dot(places[cell].T, cell_matrices[cell].astype(held)).astype(held)
        assembled = assembled + dot(rows, places[cell])
    assembled = assembled.astype(held)
    pick = jax.nn.one_hot(face_map, own, dtype=held)
    corner = shifted(assembled[own:, own:], "domain", 1)
    returned = dot(dot(pick.T, corner).astype(held), pick).astype(held)
    return assembled, pick, returned


def assemble_kernel(matrix, nodes, faces, assembled, pick, spread):
    extent = assembled.shape[0]
    places = jnp.where(lax.broadcasted_iota(jnp.int32, (extent, extent), 0) == nodes[...], 1.0, 0.0).astype(BF16)
    rows = dot(places, matrix[0]).astype(BF16)
    whole = lax.dot_general(rows, places, (((1,), (1,)), ((), ())), preferred_element_type=F32)
    assembled[...] = whole.astype(BF16)
    chosen = jnp.where(lax.broadcasted_iota(jnp.int32, spread.shape, 0) == faces[...], 1.0, 0.0)
    spread[...] = chosen.astype(BF16)
    pick[...] = chosen.T.astype(BF16)


def assemble(cell_matrices, cell_nodes, face_map, own, after):
    shared = face_map.shape[0]
    outs = [(own + shared, own + shared), (shared, own), (own, shared)]
    operands = (cell_matrices, cell_nodes, face_map.reshape(1, shared))
    return call(assemble_kernel, [shape(*dims, dtype=BF16) for dims in outs], operands, after=(after,))


def local(wavefunctions, rotation, cell_matrices, cell_nodes, face_map):
    chips = lax.axis_size("domain") // 2
    if chips == FAR and chips == lax.axis_size("band") and cell_nodes.shape[0] == 1:
        operator = functools.partial(assemble, cell_matrices, cell_nodes, face_map, wavefunctions.shape[0])
        return finish_square(*rotate_square(wavefunctions, rotation, operator))
    return finish_any(rotate_any(wavefunctions, rotation), cell_matrices, cell_nodes, face_map)


def solution(mesh):
    in_specs = (
        P("domain", "band"),
        P("band", "domain"),
        P("domain", None, None),
        P("domain", None),
        P("domain"),
    )
    out_specs = P("domain", "band")
    return jax.shard_map(local, mesh=mesh, in_specs=in_specs, out_specs=out_specs, check_vma=False)
```

```python
import functools

import jax
import jax.numpy as jnp
from jax import lax
from jax.experimental import pallas as pl
from jax.experimental.pallas import tpu as pltpu
from jax.sharding import PartitionSpec as P

CORE, NEAR, FAR = 1, 2, 4
VMEM = pl.BlockSpec(memory_space=pltpu.VMEM)
ANY = pl.BlockSpec(memory_space=pl.ANY)
F32, BF16 = jnp.float32, jnp.bfloat16


def dot(left, right):
    precision = lax.Precision.HIGHEST if left.dtype == F32 else None
    return jnp.dot(left, right, precision=precision, preferred_element_type=F32)


def split(value):
    high = value.astype(BF16)
    return high, (value - high.astype(F32)).astype(BF16)


def shifted(value, axis, steps):
    count = lax.axis_size(axis)
    leading, last = (max(0, -steps), min(count, count - steps))
    return lax.ppermute(value, axis, [(source, source + steps) for source in range(leading, last)])


def exchanged(value, axis, mask, core=None):
    sources = range(lax.axis_size(axis))
    return lax.ppermute(value, axis, [(source, source ^ mask) for source in sources if core in (None, source & CORE)])


def call(kernel, outs, operands, after=(), spaces=None, scratch=()):
    count = len(operands)

    def body(*refs):
        kernel(*refs[:count], *refs[count + len(after) :])

    return pl.pallas_call(
        body,
        out_shape=outs,
        in_specs=[pl.BlockSpec(memory_space=space) for space in spaces or [pltpu.VMEM] * count] + [ANY] * len(after),
        out_specs=[VMEM] * len(outs),
        scratch_shapes=list(scratch),
        cost_estimate=pl.CostEstimate(flops=0, bytes_accessed=1024, transcendentals=0),
        compiler_params=pltpu.CompilerParams(vmem_limit_bytes=24 * 2**20),
    )(*operands, *after)


def shape(*dims, dtype=F32):
    return jax.ShapeDtypeStruct(dims, dtype)


def core():
    return lax.rem(lax.axis_index("domain"), 2)


def block_of_band():
    return lax.bitwise_xor(lax.div(lax.axis_index("domain"), 2), lax.axis_index("band"))


def pieces_kernel(near_even, far_even, near_odd, far_odd, top, bottom, done):
    def fill(near, far):
        copies = [
            pltpu.make_async_copy(near.at[pl.ds(0, top.shape[0])], top, done.at[0]),
            pltpu.make_async_copy(far.at[pl.ds(top.shape[0], bottom.shape[0])], bottom, done.at[1]),
        ]
        for copy in copies:
            copy.start()
        for copy in copies:
            copy.wait()

    pl.when(core() == 0)(lambda: fill(near_even, far_even))
    pl.when(core() != 0)(lambda: fill(near_odd, far_odd))


def own_kernel(mine, theirs, own, block):
    rows = mine.shape[0]
    for side, states in enumerate((mine, theirs)):
        block[side * rows : (side + 1) * rows] = jnp.dot(states[...], own[...], preferred_element_type=F32)


def early_kernel(mine, theirs, near_even, far_even, near_odd, far_odd, near_block, far_block):
    rows, width = mine.shape[0], near_even.shape[1]
    first = core() == 0
    near, far = jnp.where(first, near_even[...], near_odd[...]), jnp.where(first, far_even[...], far_odd[...])
    wide = jnp.concatenate([near, far], 1)
    for side, states in enumerate((mine, theirs)):
        result = jnp.dot(states[...], wide, preferred_element_type=F32)
        near_block[side * rows : (side + 1) * rows] = result[:, :width]
        far_block[side * rows : (side + 1) * rows] = result[:, width:]


def late_kernel(mine, theirs, top, bottom, own, near, far, kept, *refs):
    sent, last = refs[:-1], refs[-1]
    cut = top.shape[0]
    rows = mine.shape[0]
    for side, states in enumerate((mine, theirs)):
        result = jnp.dot(states[:, :cut], top[...], preferred_element_type=F32)
        last[side * rows : (side + 1) * rows] = result + jnp.dot(states[:, cut:], bottom[...], preferred_element_type=F32)
    where = block_of_band()

    def store(out, slot, block):
        @pl.when(slot == lax.bitwise_xor(where, mask))
        def _():
            out[...] = block[...].astype(out.dtype)

    for mask, out in enumerate((kept, *sent)):
        for slot, block in enumerate((own, near, far, last)):
            store(out, slot, block)


def sum_kernel(kept, *refs):
    parts, (mine, theirs) = refs[:-2], refs[-2:]
    value = kept[...]
    for part in parts:
        value = value + part[...].astype(F32)
    rows = mine.shape[0]
    mine[...] = value[:rows]
    theirs[...] = value[rows:]


def rotate_square(wavefunctions, rotation, operator):
    bands, chips = lax.axis_size("band"), lax.axis_size("domain") // 2
    rows, states = wavefunctions.shape
    width = rotation.shape[1]
    cut = states * 9 // 16
    received = [exchanged(rotation, "domain", NEAR, 0), exchanged(rotation, "domain", FAR, 0)]
    theirs = exchanged(wavefunctions, "domain", CORE)
    block = [shape(2 * rows, width)]
    own = call(own_kernel, block, (wavefunctions, theirs, rotation))[0]
    operator = operator(own)
    later, _ = lax.optimization_barrier((rotation, operator[0]))
    received += [exchanged(later, "domain", NEAR, CORE), exchanged(later, "domain", FAR, CORE)]
    outs = [shape(count, width, dtype=BF16) for count in (cut, states - cut)]
    top, bottom = call(pieces_kernel, outs, received, scratch=[pltpu.SemaphoreType.DMA((2,))])
    top, bottom = exchanged(top, "domain", FAR), exchanged(bottom, "domain", NEAR)
    early = call(early_kernel, block * 2, (wavefunctions, theirs, *received))
    outs = block + [shape(2 * rows, width, dtype=BF16)] * (bands - 1)
    scratch = [pltpu.VMEM((2 * rows, width), F32)]
    kept, *sent = call(late_kernel, outs, (wavefunctions, theirs, top, bottom, own, *early), scratch=scratch)
    parts = [exchanged(sent[mask - 1], "band", mask) for mask in reversed(range(1, bands))]
    mine, others = call(sum_kernel, [shape(rows, width)] * 2, (kept, *parts))
    return mine, exchanged(others, "domain", CORE), operator


def rotate_any(wavefunctions, rotation):
    columns = lax.all_gather(rotation, "domain", axis=1, tiled=True)
    return lax.psum_scatter(dot(wavefunctions, columns), "band", scatter_dimension=1, tiled=True)


def faces_kernel(mine, other, assembled, pick, total, inward, outward):
    own, width = mine.shape
    columns = 2 * width
    first = core() == 0
    for side, half in enumerate((jnp.where(first, mine[...], other[...]), jnp.where(first, other[...], mine[...]))):
        total[:, side * width : (side + 1) * width] = half
    high, low = split(total[...])
    faces = dot(pick[...], high).astype(BF16)
    onward = (dot(assembled[own:, :own], high) + dot(assembled[own:, :own], low)).astype(BF16)
    corner = assembled[own:, own:]

    def store(forward, backward):
        forward[:, :columns] = onward
        forward[:, columns:] = corner
        backward[:, :columns] = faces
        backward[:, columns:] = corner

    pl.when(first)(lambda: store(inward, outward))
    pl.when(jnp.logical_not(first))(lambda: store(outward, inward))


def inner_kernel(total, assembled, pick, out, face_high, face_low):
    own = total.shape[0]
    high, low = split(total[...])
    inner = assembled[:own, :own]
    out[...] = dot(inner, high) + dot(inner, low)
    face_high[...] = dot(pick[...], high).astype(BF16)
    face_low[...] = dot(pick[...], low).astype(BF16)


def final_kernel(inner, face_high, face_low, assembled, spread, inward, outward, out):
    own, columns = inner.shape
    first = core() == 0
    incoming = jnp.where(first, inward[:, :columns], outward[:, :columns])
    back = jnp.where(first, outward[...], inward[...])
    corner = back[:, columns:]
    value = back[:, :columns].astype(F32) + dot(corner, face_high[...]) + dot(corner, face_low[...])
    high, low = split(value)
    out[...] = inner[...] + dot(assembled[:own, own:], incoming) + dot(spread[...], high) + dot(spread[...], low)


def finish_square(mine, other, operator):
    assembled, pick, spread = operator
    rows, width = mine.shape
    shared, columns = pick.shape[0], 2 * width
    outs = [shape(rows, columns)] + [shape(shared, columns + shared, dtype=BF16)] * 2
    total, inward, outward = call(faces_kernel, outs, (mine, other, assembled, pick))
    across = [(place, place + 1) for place in range(CORE, lax.axis_size("domain") - 1, 2)]
    outward = lax.ppermute(outward, "domain", across + [(target, source) for source, target in across])
    inward = exchanged(inward, "domain", CORE)
    outs = [shape(rows, columns)] + [shape(shared, columns, dtype=BF16)] * 2
    inner, *face = call(inner_kernel, outs, (total, assembled, pick))
    return call(final_kernel, outs[:1], (inner, *face, assembled, spread, inward, outward))[0]


def finish_any(rotated, cell_matrices, cell_nodes, face_map):
    own = rotated.shape[0]
    assembled, pick, returned = assemble_any(cell_matrices, cell_nodes, face_map, own)
    rotated = rotated.astype(BF16).astype(assembled.dtype)
    incoming = shifted(dot(pick, rotated).astype(BF16), "domain", -1).astype(assembled.dtype)
    back = shifted(dot(assembled[own:, :own], rotated), "domain", 1)
    inner = dot(assembled[:own, :own], rotated) + dot(returned, rotated) + dot(assembled[:own, own:], incoming)
    return inner + dot(pick.T.astype(F32), back)


def assemble_any(cell_matrices, cell_nodes, face_map, own):
    cells = cell_nodes.shape[0]
    extent = own + face_map.shape[0]
    held = BF16 if cells == 1 else F32
    places = jax.nn.one_hot(cell_nodes, extent, dtype=held)
    assembled = jnp.zeros((extent, extent), F32)
    for cell in range(cells):
        rows = dot(places[cell].T, cell_matrices[cell].astype(held)).astype(held)
        assembled = assembled + dot(rows, places[cell])
    assembled = assembled.astype(held)
    pick = jax.nn.one_hot(face_map, own, dtype=held)
    corner = shifted(assembled[own:, own:], "domain", 1)
    returned = dot(dot(pick.T, corner).astype(held), pick).astype(held)
    return assembled, pick, returned


def assemble_kernel(matrix, nodes, faces, assembled, pick, spread):
    extent = assembled.shape[0]
    places = jnp.where(lax.broadcasted_iota(jnp.int32, (extent, extent), 0) == nodes[...], 1.0, 0.0).astype(BF16)
    rows = dot(places, matrix[0]).astype(BF16)
    whole = lax.dot_general(rows, places, (((1,), (1,)), ((), ())), preferred_element_type=F32)
    assembled[...] = whole.astype(BF16)
    chosen = jnp.where(lax.broadcasted_iota(jnp.int32, spread.shape, 0) == faces[...], 1.0, 0.0)
    spread[...] = chosen.astype(BF16)
    pick[...] = chosen.T.astype(BF16)


def assemble(cell_matrices, cell_nodes, face_map, own, after):
    shared = face_map.shape[0]
    outs = [(own + shared, own + shared), (shared, own), (own, shared)]
    operands = (cell_matrices, cell_nodes, face_map.reshape(1, shared))
    return call(assemble_kernel, [shape(*dims, dtype=BF16) for dims in outs], operands, after=(after,))


def local(wavefunctions, rotation, cell_matrices, cell_nodes, face_map):
    chips = lax.axis_size("domain") // 2
    if chips == FAR and chips == lax.axis_size("band") and cell_nodes.shape[0] == 1:
        operator = functools.partial(assemble, cell_matrices, cell_nodes, face_map, wavefunctions.shape[0])
        return finish_square(*rotate_square(wavefunctions, rotation, operator))
    return finish_any(rotate_any(wavefunctions, rotation), cell_matrices, cell_nodes, face_map)


def solution(mesh):
    in_specs = (
        P("domain", "band"),
        P("band", "domain"),
        P("domain", None, None),
        P("domain", None),
        P("domain"),
    )
    out_specs = P("domain", "band")
    return jax.shard_map(local, mesh=mesh, in_specs=in_specs, out_specs=out_specs, check_vma=False)
```

```python
import functools

import jax
import jax.numpy as jnp
from jax import lax
from jax.experimental import pallas as pl
from jax.experimental.pallas import tpu as pltpu
from jax.sharding import PartitionSpec as P

CORE, NEAR, FAR = 1, 2, 4
VMEM = pl.BlockSpec(memory_space=pltpu.VMEM)
ANY = pl.BlockSpec(memory_space=pl.ANY)
F32, BF16 = jnp.float32, jnp.bfloat16


def dot(left, right):
    precision = lax.Precision.HIGHEST if left.dtype == F32 else None
    return jnp.dot(left, right, precision=precision, preferred_element_type=F32)


def split(value):
    high = value.astype(BF16)
    return high, (value - high.astype(F32)).astype(BF16)


def shifted(value, axis, steps):
    count = lax.axis_size(axis)
    leading, last = (max(0, -steps), min(count, count - steps))
    return lax.ppermute(value, axis, [(source, source + steps) for source in range(leading, last)])


def exchanged(value, axis, mask, core=None):
    sources = range(lax.axis_size(axis))
    return lax.ppermute(value, axis, [(source, source ^ mask) for source in sources if core in (None, source & CORE)])


def call(kernel, outs, operands, after=(), spaces=None, scratch=()):
    count = len(operands)

    def body(*refs):
        kernel(*refs[:count], *refs[count + len(after) :])

    return pl.pallas_call(
        body,
        out_shape=outs,
        in_specs=[pl.BlockSpec(memory_space=space) for space in spaces or [pltpu.VMEM] * count] + [ANY] * len(after),
        out_specs=[VMEM] * len(outs),
        scratch_shapes=list(scratch),
        cost_estimate=pl.CostEstimate(flops=0, bytes_accessed=1024, transcendentals=0),
        compiler_params=pltpu.CompilerParams(vmem_limit_bytes=24 * 2**20),
    )(*operands, *after)


def shape(*dims, dtype=F32):
    return jax.ShapeDtypeStruct(dims, dtype)


def core():
    return lax.rem(lax.axis_index("domain"), 2)


def pieces_kernel(near_even, far_even, near_odd, far_odd, top, bottom, done):
    def fill(near, far):
        copies = [
            pltpu.make_async_copy(near.at[pl.ds(0, top.shape[0])], top, done.at[0]),
            pltpu.make_async_copy(far.at[pl.ds(top.shape[0], bottom.shape[0])], bottom, done.at[1]),
        ]
        for copy in copies:
            copy.start()
        for copy in copies:
            copy.wait()

    pl.when(core() == 0)(lambda: fill(near_even, far_even))
    pl.when(core() != 0)(lambda: fill(near_odd, far_odd))


def own_kernel(mine, theirs, own, block):
    rows = mine.shape[0]
    for side, states in enumerate((mine, theirs)):
        block[side * rows : (side + 1) * rows] = jnp.dot(states[...], own[...], preferred_element_type=F32)


def early_kernel(mine, theirs, near_even, far_even, near_odd, far_odd, near_block, far_block):
    rows, width = mine.shape[0], near_even.shape[1]
    first = core() == 0
    near, far = jnp.where(first, near_even[...], near_odd[...]), jnp.where(first, far_even[...], far_odd[...])
    wide = jnp.concatenate([near, far], 1)
    for side, states in enumerate((mine, theirs)):
        result = jnp.dot(states[...], wide, preferred_element_type=F32)
        near_block[side * rows : (side + 1) * rows] = result[:, :width]
        far_block[side * rows : (side + 1) * rows] = result[:, width:]


def late_kernel(mine, theirs, top, bottom, own, near, far, kept, sent, last):
    cut = top.shape[0]
    rows = mine.shape[0]
    for side, states in enumerate((mine, theirs)):
        result = jnp.dot(states[:, :cut], top[...], preferred_element_type=F32)
        last[side * rows : (side + 1) * rows] = result + jnp.dot(states[:, cut:], bottom[...], preferred_element_type=F32)
    chip, band = lax.div(lax.axis_index("domain"), 2), lax.axis_index("band")

    def store(place, slot, block):
        @pl.when(place == lax.bitwise_xor(chip, slot))
        def _():
            sent[place] = block[...].astype(BF16)

        @pl.when(lax.bitwise_xor(chip, band) == slot)
        def _():
            kept[...] = block[...]

    for slot, block in enumerate((own, near, far, last)):
        for place in range(sent.shape[0]):
            store(place, slot, block)


def sum_kernel(kept, parts, mine, theirs):
    value = kept[...]
    for place in range(parts.shape[0]):
        value = value + jnp.where(place == lax.axis_index("band"), 0.0, parts[place].astype(F32))
    rows = mine.shape[0]
    mine[...] = value[:rows]
    theirs[...] = value[rows:]


def rotate_square(wavefunctions, rotation, operator):
    bands, chips = lax.axis_size("band"), lax.axis_size("domain") // 2
    rows, states = wavefunctions.shape
    width = rotation.shape[1]
    cut = states * 9 // 16
    received = [exchanged(rotation, "domain", NEAR, 0), exchanged(rotation, "domain", FAR, 0)]
    theirs = exchanged(wavefunctions, "domain", CORE)
    block = [shape(2 * rows, width)]
    own = call(own_kernel, block, (wavefunctions, theirs, rotation))[0]
    operator = operator(own)
    later, _ = lax.optimization_barrier((rotation, operator[0]))
    received += [exchanged(later, "domain", NEAR, CORE), exchanged(later, "domain", FAR, CORE)]
    outs = [shape(count, width, dtype=BF16) for count in (cut, states - cut)]
    top, bottom = call(pieces_kernel, outs, received, scratch=[pltpu.SemaphoreType.DMA((2,))])
    top, bottom = exchanged(top, "domain", FAR), exchanged(bottom, "domain", NEAR)
    early = call(early_kernel, block * 2, (wavefunctions, theirs, *received))
    outs = block + [shape(bands, 2 * rows, width, dtype=BF16)]
    scratch = [pltpu.VMEM((2 * rows, width), F32)]
    kept, sent = call(late_kernel, outs, (wavefunctions, theirs, top, bottom, own, *early), scratch=scratch)
    parts = lax.all_to_all(sent, "band", 0, 0)
    mine, others = call(sum_kernel, [shape(rows, width)] * 2, (kept, parts))
    return mine, exchanged(others, "domain", CORE), operator


def rotate_any(wavefunctions, rotation):
    columns = lax.all_gather(rotation, "domain", axis=1, tiled=True)
    return lax.psum_scatter(dot(wavefunctions, columns), "band", scatter_dimension=1, tiled=True)


def faces_kernel(mine, other, assembled, pick, total, inward, outward):
    own, width = mine.shape
    columns = 2 * width
    first = core() == 0
    for side, half in enumerate((jnp.where(first, mine[...], other[...]), jnp.where(first, other[...], mine[...]))):
        total[:, side * width : (side + 1) * width] = half
    high, low = split(total[...])
    faces = dot(pick[...], high).astype(BF16)
    onward = (dot(assembled[own:, :own], high) + dot(assembled[own:, :own], low)).astype(BF16)
    corner = assembled[own:, own:]

    def store(forward, backward):
        forward[:, :columns] = onward
        forward[:, columns:] = corner
        backward[:, :columns] = faces
        backward[:, columns:] = corner

    pl.when(first)(lambda: store(inward, outward))
    pl.when(jnp.logical_not(first))(lambda: store(outward, inward))


def inner_kernel(total, assembled, pick, out, face_high, face_low):
    own = total.shape[0]
    high, low = split(total[...])
    inner = assembled[:own, :own]
    out[...] = dot(inner, high) + dot(inner, low)
    face_high[...] = dot(pick[...], high).astype(BF16)
    face_low[...] = dot(pick[...], low).astype(BF16)


def final_kernel(inner, face_high, face_low, assembled, spread, inward, outward, out):
    own, columns = inner.shape
    first = core() == 0
    incoming = jnp.where(first, inward[:, :columns], outward[:, :columns])
    back = jnp.where(first, outward[...], inward[...])
    corner = back[:, columns:]
    value = back[:, :columns].astype(F32) + dot(corner, face_high[...]) + dot(corner, face_low[...])
    high, low = split(value)
    out[...] = inner[...] + dot(assembled[:own, own:], incoming) + dot(spread[...], high) + dot(spread[...], low)


def finish_square(mine, other, operator):
    assembled, pick, spread = operator
    rows, width = mine.shape
    shared, columns = pick.shape[0], 2 * width
    outs = [shape(rows, columns)] + [shape(shared, columns + shared, dtype=BF16)] * 2
    total, inward, outward = call(faces_kernel, outs, (mine, other, assembled, pick))
    across = [(place, place + 1) for place in range(CORE, lax.axis_size("domain") - 1, 2)]
    outward = lax.ppermute(outward, "domain", across + [(target, source) for source, target in across])
    inward = exchanged(inward, "domain", CORE)
    outs = [shape(rows, columns)] + [shape(shared, columns, dtype=BF16)] * 2
    inner, *face = call(inner_kernel, outs, (total, assembled, pick))
    return call(final_kernel, outs[:1], (inner, *face, assembled, spread, inward, outward))[0]


def finish_any(rotated, cell_matrices, cell_nodes, face_map):
    own = rotated.shape[0]
    assembled, pick, returned = assemble_any(cell_matrices, cell_nodes, face_map, own)
    rotated = rotated.astype(BF16).astype(assembled.dtype)
    incoming = shifted(dot(pick, rotated).astype(BF16), "domain", -1).astype(assembled.dtype)
    back = shifted(dot(assembled[own:, :own], rotated), "domain", 1)
    inner = dot(assembled[:own, :own], rotated) + dot(returned, rotated) + dot(assembled[:own, own:], incoming)
    return inner + dot(pick.T.astype(F32), back)


def assemble_any(cell_matrices, cell_nodes, face_map, own):
    cells = cell_nodes.shape[0]
    extent = own + face_map.shape[0]
    held = BF16 if cells == 1 else F32
    places = jax.nn.one_hot(cell_nodes, extent, dtype=held)
    assembled = jnp.zeros((extent, extent), F32)
    for cell in range(cells):
        rows = dot(places[cell].T, cell_matrices[cell].astype(held)).astype(held)
        assembled = assembled + dot(rows, places[cell])
    assembled = assembled.astype(held)
    pick = jax.nn.one_hot(face_map, own, dtype=held)
    corner = shifted(assembled[own:, own:], "domain", 1)
    returned = dot(dot(pick.T, corner).astype(held), pick).astype(held)
    return assembled, pick, returned


def assemble_kernel(matrix, nodes, faces, assembled, pick, spread):
    extent = assembled.shape[0]
    places = jnp.where(lax.broadcasted_iota(jnp.int32, (extent, extent), 0) == nodes[...], 1.0, 0.0).astype(BF16)
    rows = dot(places, matrix[0]).astype(BF16)
    whole = lax.dot_general(rows, places, (((1,), (1,)), ((), ())), preferred_element_type=F32)
    assembled[...] = whole.astype(BF16)
    chosen = jnp.where(lax.broadcasted_iota(jnp.int32, spread.shape, 0) == faces[...], 1.0, 0.0)
    spread[...] = chosen.astype(BF16)
    pick[...] = chosen.T.astype(BF16)


def assemble(cell_matrices, cell_nodes, face_map, own, after):
    shared = face_map.shape[0]
    outs = [(own + shared, own + shared), (shared, own), (own, shared)]
    operands = (cell_matrices, cell_nodes, face_map.reshape(1, shared))
    return call(assemble_kernel, [shape(*dims, dtype=BF16) for dims in outs], operands, after=(after,))


def local(wavefunctions, rotation, cell_matrices, cell_nodes, face_map):
    chips = lax.axis_size("domain") // 2
    if chips == FAR and chips == lax.axis_size("band") and cell_nodes.shape[0] == 1:
        operator = functools.partial(assemble, cell_matrices, cell_nodes, face_map, wavefunctions.shape[0])
        return finish_square(*rotate_square(wavefunctions, rotation, operator))
    return finish_any(rotate_any(wavefunctions, rotation), cell_matrices, cell_nodes, face_map)


def solution(mesh):
    in_specs = (
        P("domain", "band"),
        P("band", "domain"),
        P("domain", None, None),
        P("domain", None),
        P("domain"),
    )
    out_specs = P("domain", "band")
    return jax.shard_map(local, mesh=mesh, in_specs=in_specs, out_specs=out_specs, check_vma=False)
```

```python
import functools

import jax
import jax.numpy as jnp
from jax import lax
from jax.experimental import pallas as pl
from jax.experimental.pallas import tpu as pltpu
from jax.sharding import PartitionSpec as P

CORE, NEAR, FAR = 1, 2, 4
VMEM = pl.BlockSpec(memory_space=pltpu.VMEM)
ANY = pl.BlockSpec(memory_space=pl.ANY)
F32, BF16 = jnp.float32, jnp.bfloat16


def dot(left, right):
    precision = lax.Precision.HIGHEST if left.dtype == F32 else None
    return jnp.dot(left, right, precision=precision, preferred_element_type=F32)


def split(value):
    high = value.astype(BF16)
    return high, (value - high.astype(F32)).astype(BF16)


def shifted(value, axis, steps):
    count = lax.axis_size(axis)
    leading, last = (max(0, -steps), min(count, count - steps))
    return lax.ppermute(value, axis, [(source, source + steps) for source in range(leading, last)])


def exchanged(value, axis, mask, core=None):
    sources = range(lax.axis_size(axis))
    return lax.ppermute(value, axis, [(source, source ^ mask) for source in sources if core in (None, source & CORE)])


def call(kernel, outs, operands, after=(), spaces=None, scratch=()):
    count = len(operands)

    def body(*refs):
        kernel(*refs[:count], *refs[count + len(after) :])

    return pl.pallas_call(
        body,
        out_shape=outs,
        in_specs=[pl.BlockSpec(memory_space=space) for space in spaces or [pltpu.VMEM] * count] + [ANY] * len(after),
        out_specs=[VMEM] * len(outs),
        scratch_shapes=list(scratch),
        cost_estimate=pl.CostEstimate(flops=0, bytes_accessed=1024, transcendentals=0),
        compiler_params=pltpu.CompilerParams(vmem_limit_bytes=24 * 2**20),
    )(*operands, *after)


def shape(*dims, dtype=F32):
    return jax.ShapeDtypeStruct(dims, dtype)


def core():
    return lax.rem(lax.axis_index("domain"), 2)


def block_of_band():
    return lax.bitwise_xor(lax.div(lax.axis_index("domain"), 2), lax.axis_index("band"))


def pieces_kernel(near_even, far_even, near_odd, far_first, far_rest, top, bottom, done):
    upper, lower = pl.ds(0, top.shape[0]), pl.ds(top.shape[0], bottom.shape[0])
    rest = pl.ds(top.shape[0] - far_first.shape[0], bottom.shape[0])

    def fill(*pairs):
        copies = [pltpu.make_async_copy(source, target, done.at[number]) for number, (source, target) in enumerate(pairs)]
        for copy in copies:
            copy.start()
        for copy in copies:
            copy.wait()

    pl.when(core() == 0)(lambda: fill((near_even.at[upper], top), (far_even.at[lower], bottom)))
    pl.when(core() != 0)(lambda: fill((near_odd.at[upper], top), (far_rest.at[rest], bottom)))


def own_kernel(mine, theirs, own, block):
    rows = mine.shape[0]
    for side, states in enumerate((mine, theirs)):
        block[side * rows : (side + 1) * rows] = jnp.dot(states[...], own[...], preferred_element_type=F32)


def early_kernel(mine, theirs, near_even, far_even, near_odd, far_first, far_rest, near_block, far_block):
    rows, width = mine.shape[0], near_even.shape[1]
    first = core() == 0
    far_odd = jnp.concatenate([far_first[...], far_rest[...]], 0)
    near, far = jnp.where(first, near_even[...], near_odd[...]), jnp.where(first, far_even[...], far_odd)
    wide = jnp.concatenate([near, far], 1)
    for side, states in enumerate((mine, theirs)):
        result = jnp.dot(states[...], wide, preferred_element_type=F32)
        near_block[side * rows : (side + 1) * rows] = result[:, :width]
        far_block[side * rows : (side + 1) * rows] = result[:, width:]


def lower_kernel(mine, theirs, bottom, block):
    start, rows = mine.shape[1] - bottom.shape[0], mine.shape[0]
    for side, states in enumerate((mine, theirs)):
        result = jnp.dot(states[:, start:], bottom[...], preferred_element_type=F32)
        block[side * rows : (side + 1) * rows] = result


def late_kernel(mine, theirs, top, lower, own, near, far, kept, *refs):
    sent, last = refs[:-1], refs[-1]
    cut = top.shape[0]
    rows = mine.shape[0]
    for side, states in enumerate((mine, theirs)):
        span = slice(side * rows, (side + 1) * rows)
        last[span] = lower[span] + jnp.dot(states[:, :cut], top[...], preferred_element_type=F32)
    where = block_of_band()

    def store(out, slot, block):
        @pl.when(slot == lax.bitwise_xor(where, mask))
        def _():
            out[...] = block[...].astype(out.dtype)

    for mask, out in enumerate((kept, *sent)):
        for slot, block in enumerate((own, near, far, last)):
            store(out, slot, block)


def sum_kernel(kept, *refs):
    parts, (mine, theirs) = refs[:-2], refs[-2:]
    value = kept[...]
    for part in parts:
        value = value + part[...].astype(F32)
    rows = mine.shape[0]
    mine[...] = value[:rows]
    theirs[...] = value[rows:]


def rotate_square(wavefunctions, rotation, operator):
    bands, chips = lax.axis_size("band"), lax.axis_size("domain") // 2
    rows, states = wavefunctions.shape
    width = rotation.shape[1]
    cut, part = states // 2, states // 4
    first = exchanged(rotation[:part], "domain", FAR, CORE)
    received = [exchanged(rotation, "domain", NEAR, 0), exchanged(rotation, "domain", FAR, 0)]
    theirs = exchanged(wavefunctions, "domain", CORE)
    later, _, first = lax.optimization_barrier((rotation, theirs, first))
    received += [exchanged(later, "domain", NEAR, CORE), first, exchanged(later[part:], "domain", FAR, CORE)]
    block = [shape(2 * rows, width)]
    own = call(own_kernel, block, (wavefunctions, theirs, rotation), after=(later,))[0]
    operator = operator(own)
    outs = [shape(count, width, dtype=BF16) for count in (cut, states - cut)]
    top, bottom = call(pieces_kernel, outs, received, after=operator[:1], scratch=[pltpu.SemaphoreType.DMA((2,))])
    top, bottom = exchanged(top, "domain", FAR), exchanged(bottom, "domain", NEAR)
    early = call(early_kernel, block * 2, (wavefunctions, theirs, *received))
    outs = block + [shape(2 * rows, width, dtype=BF16)] * (bands - 1)
    scratch = [pltpu.VMEM((2 * rows, width), F32)]
    lower = call(lower_kernel, block, (wavefunctions, theirs, bottom))[0]
    kept, *sent = call(late_kernel, outs, (wavefunctions, theirs, top, lower, own, *early), scratch=scratch)
    parts = [exchanged(sent[mask - 1], "band", mask) for mask in reversed(range(1, bands))]
    mine, others = call(sum_kernel, [shape(rows, width)] * 2, (kept, *parts))
    return mine, exchanged(others, "domain", CORE), operator


def rotate_any(wavefunctions, rotation):
    columns = lax.all_gather(rotation, "domain", axis=1, tiled=True)
    return lax.psum_scatter(dot(wavefunctions, columns), "band", scatter_dimension=1, tiled=True)


def faces_kernel(mine, other, assembled, pick, total, inward, outward):
    own, width = mine.shape
    columns = 2 * width
    first = core() == 0
    for side, half in enumerate((jnp.where(first, mine[...], other[...]), jnp.where(first, other[...], mine[...]))):
        total[:, side * width : (side + 1) * width] = half
    high, low = split(total[...])
    faces = dot(pick[...], high).astype(BF16)
    onward = (dot(assembled[own:, :own], high) + dot(assembled[own:, :own], low)).astype(BF16)
    corner = assembled[own:, own:]

    def store(forward, backward):
        forward[:, :columns] = onward
        forward[:, columns:] = corner
        backward[:, :columns] = faces
        backward[:, columns:] = corner

    pl.when(first)(lambda: store(inward, outward))
    pl.when(jnp.logical_not(first))(lambda: store(outward, inward))


def inner_kernel(total, assembled, pick, out, faces):
    own, columns = total.shape
    high, low = split(total[...])
    inner = assembled[:own, :own]
    out[...] = dot(inner, high) + dot(inner, low)
    faces[:, :columns] = dot(pick[...], high).astype(BF16)
    faces[:, columns:] = dot(pick[...], low).astype(BF16)


def final_kernel(inner, faces, assembled, spread, inward, outward, out):
    own, columns = inner.shape
    first = core() == 0
    incoming = jnp.where(first, inward[:, :columns], outward[:, :columns])
    back = jnp.where(first, outward[...], inward[...])
    extra = dot(back[:, columns:], faces[...])
    high, low = split(back[:, :columns].astype(F32) + extra[:, :columns] + extra[:, columns:])
    matrix = jnp.concatenate([assembled[:own, own:], spread[...], spread[...]], 1)
    out[...] = inner[...] + dot(matrix, jnp.concatenate([incoming, high, low], 0))


def finish_square(mine, other, operator):
    assembled, pick, spread = operator
    rows, width = mine.shape
    shared, columns = pick.shape[0], 2 * width
    outs = [shape(rows, columns)] + [shape(shared, columns + shared, dtype=BF16)] * 2
    total, inward, outward = call(faces_kernel, outs, (mine, other, assembled, pick))
    across = [(place, place + 1) for place in range(CORE, lax.axis_size("domain") - 1, 2)]
    outward = lax.ppermute(outward, "domain", across + [(target, source) for source, target in across])
    inward = exchanged(inward, "domain", CORE)
    outs = [shape(rows, columns), shape(shared, 2 * columns, dtype=BF16)]
    inner, faces = call(inner_kernel, outs, (total, assembled, pick))
    return call(final_kernel, outs[:1], (inner, faces, assembled, spread, inward, outward))[0]


def finish_any(rotated, cell_matrices, cell_nodes, face_map):
    own = rotated.shape[0]
    assembled, pick, returned = assemble_any(cell_matrices, cell_nodes, face_map, own)
    rotated = rotated.astype(BF16).astype(assembled.dtype)
    incoming = shifted(dot(pick, rotated).astype(BF16), "domain", -1).astype(assembled.dtype)
    back = shifted(dot(assembled[own:, :own], rotated), "domain", 1)
    inner = dot(assembled[:own, :own], rotated) + dot(returned, rotated) + dot(assembled[:own, own:], incoming)
    return inner + dot(pick.T.astype(F32), back)


def assemble_any(cell_matrices, cell_nodes, face_map, own):
    cells = cell_nodes.shape[0]
    extent = own + face_map.shape[0]
    held = BF16 if cells == 1 else F32
    places = jax.nn.one_hot(cell_nodes, extent, dtype=held)
    assembled = jnp.zeros((extent, extent), F32)
    for cell in range(cells):
        rows = dot(places[cell].T, cell_matrices[cell].astype(held)).astype(held)
        assembled = assembled + dot(rows, places[cell])
    assembled = assembled.astype(held)
    pick = jax.nn.one_hot(face_map, own, dtype=held)
    corner = shifted(assembled[own:, own:], "domain", 1)
    returned = dot(dot(pick.T, corner).astype(held), pick).astype(held)
    return assembled, pick, returned


def assemble_kernel(matrix, nodes, faces, assembled, pick, spread):
    extent = assembled.shape[0]
    places = jnp.where(lax.broadcasted_iota(jnp.int32, (extent, extent), 0) == nodes[...], 1.0, 0.0).astype(BF16)
    rows = dot(places, matrix[0]).astype(BF16)
    whole = lax.dot_general(rows, places, (((1,), (1,)), ((), ())), preferred_element_type=F32)
    assembled[...] = whole.astype(BF16)
    chosen = jnp.where(lax.broadcasted_iota(jnp.int32, spread.shape, 0) == faces[...], 1.0, 0.0)
    spread[...] = chosen.astype(BF16)
    pick[...] = chosen.T.astype(BF16)


def assemble(cell_matrices, cell_nodes, face_map, own, after):
    shared = face_map.shape[0]
    outs = [(own + shared, own + shared), (shared, own), (own, shared)]
    operands = (cell_matrices, cell_nodes, face_map.reshape(1, shared))
    return call(assemble_kernel, [shape(*dims, dtype=BF16) for dims in outs], operands, after=(after,))


def local(wavefunctions, rotation, cell_matrices, cell_nodes, face_map):
    chips = lax.axis_size("domain") // 2
    if chips == FAR and chips == lax.axis_size("band") and cell_nodes.shape[0] == 1:
        operator = functools.partial(assemble, cell_matrices, cell_nodes, face_map, wavefunctions.shape[0])
        return finish_square(*rotate_square(wavefunctions, rotation, operator))
    return finish_any(rotate_any(wavefunctions, rotation), cell_matrices, cell_nodes, face_map)


def solution(mesh):
    in_specs = (
        P("domain", "band"),
        P("band", "domain"),
        P("domain", None, None),
        P("domain", None),
        P("domain"),
    )
    out_specs = P("domain", "band")
    return jax.shard_map(local, mesh=mesh, in_specs=in_specs, out_specs=out_specs, check_vma=False)
```

```python
import functools

import jax
import jax.numpy as jnp
from jax import lax
from jax.experimental import pallas as pl
from jax.experimental.pallas import tpu as pltpu
from jax.sharding import PartitionSpec as P

CORE, NEAR, FAR = 1, 2, 4
VMEM = pl.BlockSpec(memory_space=pltpu.VMEM)
ANY = pl.BlockSpec(memory_space=pl.ANY)
F32, BF16 = jnp.float32, jnp.bfloat16


def dot(left, right):
    precision = lax.Precision.HIGHEST if left.dtype == F32 else None
    return jnp.dot(left, right, precision=precision, preferred_element_type=F32)


def split(value):
    high = value.astype(BF16)
    return high, (value - high.astype(F32)).astype(BF16)


def shifted(value, axis, steps):
    count = lax.axis_size(axis)
    leading, last = (max(0, -steps), min(count, count - steps))
    return lax.ppermute(value, axis, [(source, source + steps) for source in range(leading, last)])


def exchanged(value, axis, mask, core=None):
    sources = range(lax.axis_size(axis))
    return lax.ppermute(value, axis, [(source, source ^ mask) for source in sources if core in (None, source & CORE)])


def call(kernel, outs, operands, after=(), spaces=None, scratch=()):
    count = len(operands)

    def body(*refs):
        kernel(*refs[:count], *refs[count + len(after) :])

    return pl.pallas_call(
        body,
        out_shape=outs,
        in_specs=[pl.BlockSpec(memory_space=space) for space in spaces or [pltpu.VMEM] * count] + [ANY] * len(after),
        out_specs=[VMEM] * len(outs),
        scratch_shapes=list(scratch),
        cost_estimate=pl.CostEstimate(flops=0, bytes_accessed=1024, transcendentals=0),
        compiler_params=pltpu.CompilerParams(vmem_limit_bytes=24 * 2**20),
    )(*operands, *after)


def shape(*dims, dtype=F32):
    return jax.ShapeDtypeStruct(dims, dtype)


def core():
    return lax.rem(lax.axis_index("domain"), 2)


def block_of_band():
    return lax.bitwise_xor(lax.div(lax.axis_index("domain"), 2), lax.axis_index("band"))


def pieces_kernel(near_even, far_even, near_odd, far_odd, top, bottom, done):
    def fill(near, far):
        copies = [
            pltpu.make_async_copy(near.at[pl.ds(0, top.shape[0])], top, done.at[0]),
            pltpu.make_async_copy(far.at[pl.ds(top.shape[0], bottom.shape[0])], bottom, done.at[1]),
        ]
        for copy in copies:
            copy.start()
        for copy in copies:
            copy.wait()

    pl.when(core() == 0)(lambda: fill(near_even, far_even))
    pl.when(core() != 0)(lambda: fill(near_odd, far_odd))


def own_kernel(mine, theirs, own, block):
    rows = mine.shape[0]
    for side, states in enumerate((mine, theirs)):
        block[side * rows : (side + 1) * rows] = jnp.dot(states[...], own[...], preferred_element_type=F32)


def early_kernel(mine, theirs, near_even, far_even, near_odd, far_odd, near_block, far_block):
    rows, width = mine.shape[0], near_even.shape[1]
    first = core() == 0
    near, far = jnp.where(first, near_even[...], near_odd[...]), jnp.where(first, far_even[...], far_odd[...])
    wide = jnp.concatenate([near, far], 1)
    for side, states in enumerate((mine, theirs)):
        result = jnp.dot(states[...], wide, preferred_element_type=F32)
        near_block[side * rows : (side + 1) * rows] = result[:, :width]
        far_block[side * rows : (side + 1) * rows] = result[:, width:]


def lower_kernel(mine, theirs, bottom, block):
    start, rows = mine.shape[1] - bottom.shape[0], mine.shape[0]
    for side, states in enumerate((mine, theirs)):
        result = jnp.dot(states[:, start:], bottom[...], preferred_element_type=F32)
        block[side * rows : (side + 1) * rows] = result


def late_kernel(mine, theirs, top, lower, own, near, far, kept, *refs):
    sent, last = refs[:-1], refs[-1]
    cut = top.shape[0]
    rows = mine.shape[0]
    for side, states in enumerate((mine, theirs)):
        span = slice(side * rows, (side + 1) * rows)
        last[span] = lower[span] + jnp.dot(states[:, :cut], top[...], preferred_element_type=F32)
    where = block_of_band()

    def store(out, slot, block):
        @pl.when(slot == lax.bitwise_xor(where, mask))
        def _():
            out[...] = block[...].astype(out.dtype)

    for mask, out in enumerate((kept, *sent)):
        for slot, block in enumerate((own, near, far, last)):
            store(out, slot, block)


def sum_kernel(kept, *refs):
    parts, (own_message, other_message, mine, swap, local, *sent) = refs[:-9], refs[-9:]
    value = kept[...]
    for part in parts:
        value = value + part[...].astype(F32)
    rows, shared = mine.shape[0], local.shape[0]
    first = core() == 0
    results = []
    for message, block in ((own_message, value[:rows]), (other_message, value[rows:])):
        high, low = split(block)
        matrix = message[:, :rows]
        result = dot(matrix, high) + dot(matrix, low)
        results += [result[:shared], result[shared:]]
    own_back, own_faces, other_back, other_faces = results
    mine[...] = value[:rows]
    swap[:rows] = value[rows:]
    swap[rows:] = jnp.where(first, own_back, own_faces)
    local[...] = jnp.where(first, other_faces, other_back)
    other_back_sent, own_back_sent, own_faces_sent, other_faces_sent = sent
    other_back_sent[...] = other_back.astype(BF16)
    own_back_sent[:, : own_back.shape[1]] = own_back.astype(BF16)
    own_back_sent[:, own_back.shape[1] : own_back.shape[1] + shared] = own_message[:shared, rows:]
    rest = own_back_sent.shape[1] - own_back.shape[1] - shared
    own_back_sent[:, -rest:] = jnp.zeros((shared, rest), BF16)
    own_faces_sent[...] = own_faces.astype(BF16)
    other_faces_sent[...] = other_faces.astype(BF16)


def rotate_square(wavefunctions, rotation, operator):
    bands, chips = lax.axis_size("band"), lax.axis_size("domain") // 2
    rows, states = wavefunctions.shape
    width = rotation.shape[1]
    cut = states * 9 // 16
    received = [exchanged(rotation, "domain", NEAR, 0), exchanged(rotation, "domain", FAR, 0)]
    theirs = exchanged(wavefunctions, "domain", CORE)
    block = [shape(2 * rows, width)]
    assembled, message, matrix = operator(theirs)
    other_message = exchanged(message, "domain", CORE)
    own = call(own_kernel, block, (wavefunctions, theirs, rotation), after=(message,))[0]
    later, _ = lax.optimization_barrier((rotation, own))
    received += [exchanged(later, "domain", NEAR, CORE), exchanged(later, "domain", FAR, CORE)]
    outs = [shape(count, width, dtype=BF16) for count in (cut, states - cut)]
    top, bottom = call(pieces_kernel, outs, received, after=(other_message,), scratch=[pltpu.SemaphoreType.DMA((2,))])
    top, bottom = exchanged(top, "domain", FAR), exchanged(bottom, "domain", NEAR)
    early = call(early_kernel, block * 2, (wavefunctions, theirs, *received))
    outs = block + [shape(2 * rows, width, dtype=BF16)] * (bands - 1)
    scratch = [pltpu.VMEM((2 * rows, width), F32)]
    lower = call(lower_kernel, block, (wavefunctions, theirs, bottom))[0]
    kept, *sent = call(late_kernel, outs, (wavefunctions, theirs, top, lower, own, *early), scratch=scratch)
    parts = [exchanged(sent[mask - 1], "band", mask) for mask in reversed(range(1, bands))]

    shared = message.shape[0] // 2
    small = shape(shared, width, dtype=BF16)
    outs = [shape(rows, width), shape(rows + shared, width), shape(shared, width)]
    outs += [small, shape(shared, 9 * width, dtype=BF16), small, small]
    mine, swap, local, *sent = call(sum_kernel, outs, (kept, *parts, message, other_message))
    chips = [2 * chip for chip in range(chips - 1)]
    back_even = lax.ppermute(sent[0], "domain", [(place, place + 2) for place in chips])
    back_odd = lax.ppermute(sent[1], "domain", [(place + 1, place + 2) for place in chips])
    faces_even = lax.ppermute(sent[2], "domain", [(place + 2, place + 1) for place in chips])
    faces_odd = lax.ppermute(sent[3], "domain", [(place + 3, place + 1) for place in chips])
    swap = exchanged(swap, "domain", CORE)
    outs = [shape(rows, width), shape(shared, width), shape(shared, 2 * width, dtype=BF16), shape(shared, 2 * width)]
    outs += [shape(shared, shared, dtype=BF16)]
    operands = (mine, assembled, message, other_message, local, back_even, back_odd, faces_even, faces_odd)
    partial = call(inner_kernel, outs, operands)
    return call(final_kernel, [shape(rows, 2 * width)], (*partial, swap, assembled, message, matrix))[0]


def rotate_any(wavefunctions, rotation):
    columns = lax.all_gather(rotation, "domain", axis=1, tiled=True)
    return lax.psum_scatter(dot(wavefunctions, columns), "band", scatter_dimension=1, tiled=True)


def own_terms(block, assembled, message, corner):
    own = block.shape[0]
    high, low = split(block)
    inner, pick = assembled[:own, :own], message[message.shape[0] // 2 :, :own]
    faces = dot(corner, dot(pick, high).astype(BF16)) + dot(corner, dot(pick, low).astype(BF16))
    return dot(inner, high) + dot(inner, low), faces


def inner_kernel(
    mine, assembled, message, other_message, local, back_even, back_odd, faces_even, faces_odd, inner, terms, faces, back, corner
):
    own, width = mine.shape
    first = core() == 0
    block = jnp.where(first, back_odd[:, width : width + corner.shape[1]], other_message[: corner.shape[0], own:])
    corner[...] = block
    inner[...], terms[...] = own_terms(mine[...], assembled, message, block)
    both = jnp.concatenate([local[...], local[...]], 1)
    faces[...] = jnp.where(first, both.astype(BF16), jnp.concatenate([faces_even[...], faces_odd[...]], 1))
    back[...] = jnp.where(first, jnp.concatenate([back_even[...], back_odd[:, :width]], 1).astype(F32), both)


def final_kernel(inner, terms, faces, back, corner, swap, assembled, message, matrix, out):
    own, width = inner.shape
    other, extra = swap[:own], swap[own:]
    other_inner, other_terms = own_terms(other, assembled, message, corner[...])
    first = core() == 0

    def half(side, block, more, incoming, sums):
        high, low = split(sums + more)
        value = block + dot(matrix[...], jnp.concatenate([incoming, high, low], 0))
        out[:, side * width : (side + 1) * width] = value

    @pl.when(first)
    def _():
        half(0, inner[...], terms[...], faces[:, :width], back[:, :width])
        half(1, other_inner, other_terms, extra.astype(BF16), back[:, width:])

    @pl.when(jnp.logical_not(first))
    def _():
        half(0, other_inner, other_terms, faces[:, :width], extra)
        half(1, inner[...], terms[...], faces[:, width:], back[:, width:])


def finish_any(rotated, cell_matrices, cell_nodes, face_map):
    own = rotated.shape[0]
    assembled, pick, returned = assemble_any(cell_matrices, cell_nodes, face_map, own)
    rotated = rotated.astype(BF16).astype(assembled.dtype)
    incoming = shifted(dot(pick, rotated).astype(BF16), "domain", -1).astype(assembled.dtype)
    back = shifted(dot(assembled[own:, :own], rotated), "domain", 1)
    inner = dot(assembled[:own, :own], rotated) + dot(returned, rotated) + dot(assembled[:own, own:], incoming)
    return inner + dot(pick.T.astype(F32), back)


def assemble_any(cell_matrices, cell_nodes, face_map, own):
    cells = cell_nodes.shape[0]
    extent = own + face_map.shape[0]
    held = BF16 if cells == 1 else F32
    places = jax.nn.one_hot(cell_nodes, extent, dtype=held)
    assembled = jnp.zeros((extent, extent), F32)
    for cell in range(cells):
        rows = dot(places[cell].T, cell_matrices[cell].astype(held)).astype(held)
        assembled = assembled + dot(rows, places[cell])
    assembled = assembled.astype(held)
    pick = jax.nn.one_hot(face_map, own, dtype=held)
    corner = shifted(assembled[own:, own:], "domain", 1)
    returned = dot(dot(pick.T, corner).astype(held), pick).astype(held)
    return assembled, pick, returned


def assemble_kernel(cell, nodes, faces, assembled, message, matrix):
    extent, shared = assembled.shape[0], faces.shape[1]
    own = extent - shared
    places = jnp.where(lax.broadcasted_iota(jnp.int32, (extent, extent), 0) == nodes[...], 1.0, 0.0).astype(BF16)
    rows = dot(places, cell[0]).astype(BF16)
    whole = lax.dot_general(rows, places, (((1,), (1,)), ((), ())), preferred_element_type=F32).astype(BF16)
    chosen = jnp.where(lax.broadcasted_iota(jnp.int32, (own, shared), 0) == faces[...], 1.0, 0.0)
    assembled[...] = whole
    message[:shared] = whole[own:]
    message[shared:, :own] = chosen.T.astype(BF16)
    message[shared:, own:] = jnp.zeros((shared, shared), BF16)
    matrix[:, :shared] = whole[:own, own:]
    matrix[:, shared : 2 * shared] = chosen.astype(BF16)
    matrix[:, 2 * shared :] = chosen.astype(BF16)


def assemble(cell_matrices, cell_nodes, face_map, own, after):
    shared = face_map.shape[0]
    extent = own + shared
    outs = [shape(*dims, dtype=BF16) for dims in ((extent, extent), (2 * shared, extent), (own, 3 * shared))]
    operands = (cell_matrices, cell_nodes, face_map.reshape(1, shared))
    return call(assemble_kernel, outs, operands, after=(after,))


def local(wavefunctions, rotation, cell_matrices, cell_nodes, face_map):
    chips = lax.axis_size("domain") // 2
    if chips == FAR and chips == lax.axis_size("band") and cell_nodes.shape[0] == 1:
        operator = functools.partial(assemble, cell_matrices, cell_nodes, face_map, wavefunctions.shape[0])
        return rotate_square(wavefunctions, rotation, operator)
    return finish_any(rotate_any(wavefunctions, rotation), cell_matrices, cell_nodes, face_map)


def solution(mesh):
    in_specs = (
        P("domain", "band"),
        P("band", "domain"),
        P("domain", None, None),
        P("domain", None),
        P("domain"),
    )
    out_specs = P("domain", "band")
    return jax.shard_map(local, mesh=mesh, in_specs=in_specs, out_specs=out_specs, check_vma=False)
```

```python
import functools

import jax
import jax.numpy as jnp
from jax import lax
from jax.experimental import pallas as pl
from jax.experimental.pallas import tpu as pltpu
from jax.sharding import PartitionSpec as P

CORE, NEAR, FAR = 1, 2, 4
VMEM = pl.BlockSpec(memory_space=pltpu.VMEM)
ANY = pl.BlockSpec(memory_space=pl.ANY)
F32, BF16 = jnp.float32, jnp.bfloat16


def dot(left, right):
    precision = lax.Precision.HIGHEST if left.dtype == F32 else None
    return jnp.dot(left, right, precision=precision, preferred_element_type=F32)


def split(value):
    high = value.astype(BF16)
    return high, (value - high.astype(F32)).astype(BF16)


def shifted(value, axis, steps):
    count = lax.axis_size(axis)
    leading, last = (max(0, -steps), min(count, count - steps))
    return lax.ppermute(value, axis, [(source, source + steps) for source in range(leading, last)])


def exchanged(value, axis, mask, core=None):
    sources = range(lax.axis_size(axis))
    return lax.ppermute(value, axis, [(source, source ^ mask) for source in sources if core in (None, source & CORE)])


def call(kernel, outs, operands, after=(), spaces=None, scratch=()):
    after = tuple(after)
    count = len(operands)

    def body(*refs):
        kernel(*refs[:count], *refs[count + len(after) :])

    return pl.pallas_call(
        body,
        out_shape=outs,
        in_specs=[pl.BlockSpec(memory_space=space) for space in spaces or [pltpu.VMEM] * count] + [ANY] * len(after),
        out_specs=[VMEM] * len(outs),
        scratch_shapes=list(scratch),
        cost_estimate=pl.CostEstimate(flops=0, bytes_accessed=1024, transcendentals=0),
        compiler_params=pltpu.CompilerParams(vmem_limit_bytes=24 * 2**20),
    )(*operands, *after)


def shape(*dims, dtype=F32):
    return jax.ShapeDtypeStruct(dims, dtype)


def core():
    return lax.rem(lax.axis_index("domain"), 2)


def block_of_band():
    return lax.bitwise_xor(lax.div(lax.axis_index("domain"), 2), lax.axis_index("band"))


def pieces_kernel(near_even, far_even, near_odd, far_odd, top, bottom, done):
    def fill(near, far):
        copies = [
            pltpu.make_async_copy(near.at[pl.ds(0, top.shape[0])], top, done.at[0]),
            pltpu.make_async_copy(far.at[pl.ds(top.shape[0], bottom.shape[0])], bottom, done.at[1]),
        ]
        for copy in copies:
            copy.start()
        for copy in copies:
            copy.wait()

    pl.when(core() == 0)(lambda: fill(near_even, far_even))
    pl.when(core() != 0)(lambda: fill(near_odd, far_odd))


def own_kernel(mine, theirs, own, block):
    rows = mine.shape[0]
    for side, states in enumerate((mine, theirs)):
        block[side * rows : (side + 1) * rows] = jnp.dot(states[...], own[...], preferred_element_type=F32)


def early_kernel(mine, theirs, own, near_even, far_even, near_odd, far_odd, near_block, far_block, *sent):
    rows, width = mine.shape[0], near_even.shape[1]
    first = core() == 0
    near, far = jnp.where(first, near_even[...], near_odd[...]), jnp.where(first, far_even[...], far_odd[...])
    wide = jnp.concatenate([near, far], 1)
    for side, states in enumerate((mine, theirs)):
        result = jnp.dot(states[...], wide, preferred_element_type=F32)
        near_block[side * rows : (side + 1) * rows] = result[:, :width]
        far_block[side * rows : (side + 1) * rows] = result[:, width:]
    where = block_of_band()

    def store(out, slot, block):
        @pl.when(slot == lax.bitwise_xor(where, mask))
        def _():
            out[...] = block[...].astype(out.dtype)

    for mask, out in enumerate(sent, 1):
        for slot, block in enumerate((own, near_block, far_block)):
            store(out, slot, block)


def late_kernel(mine, theirs, top, bottom, own, near, far, kept, *refs):
    sent, last = refs[:-1], refs[-1]
    cut = top.shape[0]
    rows = mine.shape[0]
    for side, states in enumerate((mine, theirs)):
        result = jnp.dot(states[:, :cut], top[...], preferred_element_type=F32)
        last[side * rows : (side + 1) * rows] = result + jnp.dot(states[:, cut:], bottom[...], preferred_element_type=F32)
    where = block_of_band()

    def store(out, slot, block):
        @pl.when(slot == lax.bitwise_xor(where, mask))
        def _():
            out[...] = block[...].astype(out.dtype)

    for mask, out in enumerate((kept, *sent)):
        for slot, block in enumerate((own, near, far, last)):
            store(out, slot, block)


def sum_kernel(kept, *refs):
    parts, (mine, theirs) = refs[:-2], refs[-2:]
    value = kept[...]
    for part in parts:
        value = value + part[...].astype(F32)
    rows = mine.shape[0]
    mine[...] = value[:rows]
    theirs[...] = value[rows:]


def rotate_square(wavefunctions, rotation, operator):
    bands, chips = lax.axis_size("band"), lax.axis_size("domain") // 2
    rows, states = wavefunctions.shape
    width = rotation.shape[1]

    def across(value, mask, ahead):
        pairs = []
        for chip in range(chips):
            for band in range(bands):
                place = 2 * chip * bands
                if ((chip ^ band ^ mask) != chips - 1) == ahead:
                    pairs.append((place + band, place + (band ^ mask)))
                if not ahead:
                    pairs.append((place + bands + band, place + bands + (band ^ mask)))
        return lax.ppermute(value, ("domain", "band"), pairs)

    cut = states * 9 // 16
    received = [exchanged(rotation, "domain", NEAR, 0), exchanged(rotation, "domain", FAR, 0)]
    theirs = exchanged(wavefunctions, "domain", CORE)
    block = [shape(2 * rows, width)]
    operator = operator(theirs)
    later, _ = lax.optimization_barrier((rotation, operator[0]))
    received += [exchanged(later, "domain", NEAR, CORE), exchanged(later, "domain", FAR, CORE)]
    own = call(own_kernel, block, (wavefunctions, theirs, rotation), after=(later,))[0]
    outs = [shape(count, width, dtype=BF16) for count in (cut, states - cut)]
    top, bottom = call(pieces_kernel, outs, received, after=(own,), scratch=[pltpu.SemaphoreType.DMA((2,))])
    top, bottom = exchanged(top, "domain", FAR), exchanged(bottom, "domain", NEAR)
    messages = [shape(2 * rows, width, dtype=BF16)] * (bands - 1)
    near, far, *sent = call(early_kernel, block * 2 + messages, (wavefunctions, theirs, own, *received))
    masks = range(1, bands)[::-1]
    parts = [across(sent[mask - 1], mask, True) for mask in masks]
    scratch = [pltpu.VMEM((2 * rows, width), F32)]
    operands = (wavefunctions, theirs, top, bottom, own, near, far)
    kept, *sent = call(late_kernel, block + messages, operands, after=parts, scratch=scratch)
    parts += [across(sent[mask - 1], mask, False) for mask in masks]
    mine, others = call(sum_kernel, [shape(rows, width)] * 2, (kept, *parts))
    return mine, exchanged(others, "domain", CORE), operator


def rotate_any(wavefunctions, rotation):
    columns = lax.all_gather(rotation, "domain", axis=1, tiled=True)
    return lax.psum_scatter(dot(wavefunctions, columns), "band", scatter_dimension=1, tiled=True)


def faces_kernel(mine, other, assembled, pick, total, inward, outward):
    own, width = mine.shape
    columns = 2 * width
    first = core() == 0
    for side, half in enumerate((jnp.where(first, mine[...], other[...]), jnp.where(first, other[...], mine[...]))):
        total[:, side * width : (side + 1) * width] = half
    high, low = split(total[...])
    faces = dot(pick[...], high).astype(BF16)
    onward = (dot(assembled[own:, :own], high) + dot(assembled[own:, :own], low)).astype(BF16)
    corner = assembled[own:, own:]

    def store(forward, backward):
        forward[:, :columns] = onward
        forward[:, columns:] = corner
        backward[:, :columns] = faces
        backward[:, columns:] = corner

    pl.when(first)(lambda: store(inward, outward))
    pl.when(jnp.logical_not(first))(lambda: store(outward, inward))


def inner_kernel(total, assembled, pick, out, face_high, face_low):
    own = total.shape[0]
    high, low = split(total[...])
    inner = assembled[:own, :own]
    out[...] = dot(inner, high) + dot(inner, low)
    face_high[...] = dot(pick[...], high).astype(BF16)
    face_low[...] = dot(pick[...], low).astype(BF16)


def final_kernel(inner, face_high, face_low, assembled, spread, inward, outward, out):
    own, columns = inner.shape
    first = core() == 0
    incoming = jnp.where(first, inward[:, :columns], outward[:, :columns])
    back = jnp.where(first, outward[...], inward[...])
    corner = back[:, columns:]
    value = back[:, :columns].astype(F32) + dot(corner, face_high[...]) + dot(corner, face_low[...])
    high, low = split(value)
    out[...] = inner[...] + dot(assembled[:own, own:], incoming) + dot(spread[...], high) + dot(spread[...], low)


def finish_square(mine, other, operator):
    assembled, pick, spread = operator
    rows, width = mine.shape
    shared, columns = pick.shape[0], 2 * width
    outs = [shape(rows, columns)] + [shape(shared, columns + shared, dtype=BF16)] * 2
    total, inward, outward = call(faces_kernel, outs, (mine, other, assembled, pick))
    across = [(place, place + 1) for place in range(CORE, lax.axis_size("domain") - 1, 2)]
    outward = lax.ppermute(outward, "domain", across + [(target, source) for source, target in across])
    inward = exchanged(inward, "domain", CORE)
    outs = [shape(rows, columns)] + [shape(shared, columns, dtype=BF16)] * 2
    inner, *face = call(inner_kernel, outs, (total, assembled, pick))
    return call(final_kernel, outs[:1], (inner, *face, assembled, spread, inward, outward))[0]


def finish_any(rotated, cell_matrices, cell_nodes, face_map):
    own = rotated.shape[0]
    assembled, pick, returned = assemble_any(cell_matrices, cell_nodes, face_map, own)
    rotated = rotated.astype(BF16).astype(assembled.dtype)
    incoming = shifted(dot(pick, rotated).astype(BF16), "domain", -1).astype(assembled.dtype)
    back = shifted(dot(assembled[own:, :own], rotated), "domain", 1)
    inner = dot(assembled[:own, :own], rotated) + dot(returned, rotated) + dot(assembled[:own, own:], incoming)
    return inner + dot(pick.T.astype(F32), back)


def assemble_any(cell_matrices, cell_nodes, face_map, own):
    cells = cell_nodes.shape[0]
    extent = own + face_map.shape[0]
    held = BF16 if cells == 1 else F32
    places = jax.nn.one_hot(cell_nodes, extent, dtype=held)
    assembled = jnp.zeros((extent, extent), F32)
    for cell in range(cells):
        rows = dot(places[cell].T, cell_matrices[cell].astype(held)).astype(held)
        assembled = assembled + dot(rows, places[cell])
    assembled = assembled.astype(held)
    pick = jax.nn.one_hot(face_map, own, dtype=held)
    corner = shifted(assembled[own:, own:], "domain", 1)
    returned = dot(dot(pick.T, corner).astype(held), pick).astype(held)
    return assembled, pick, returned


def assemble_kernel(matrix, nodes, faces, assembled, pick, spread):
    extent = assembled.shape[0]
    places = jnp.where(lax.broadcasted_iota(jnp.int32, (extent, extent), 0) == nodes[...], 1.0, 0.0).astype(BF16)
    rows = dot(places, matrix[0]).astype(BF16)
    whole = lax.dot_general(rows, places, (((1,), (1,)), ((), ())), preferred_element_type=F32)
    assembled[...] = whole.astype(BF16)
    chosen = jnp.where(lax.broadcasted_iota(jnp.int32, spread.shape, 0) == faces[...], 1.0, 0.0)
    spread[...] = chosen.astype(BF16)
    pick[...] = chosen.T.astype(BF16)


def assemble(cell_matrices, cell_nodes, face_map, own, after):
    shared = face_map.shape[0]
    outs = [(own + shared, own + shared), (shared, own), (own, shared)]
    operands = (cell_matrices, cell_nodes, face_map.reshape(1, shared))
    return call(assemble_kernel, [shape(*dims, dtype=BF16) for dims in outs], operands, after=(after,))


def local(wavefunctions, rotation, cell_matrices, cell_nodes, face_map):
    chips = lax.axis_size("domain") // 2
    if chips == FAR and chips == lax.axis_size("band") and cell_nodes.shape[0] == 1:
        operator = functools.partial(assemble, cell_matrices, cell_nodes, face_map, wavefunctions.shape[0])
        return finish_square(*rotate_square(wavefunctions, rotation, operator))
    return finish_any(rotate_any(wavefunctions, rotation), cell_matrices, cell_nodes, face_map)


def solution(mesh):
    in_specs = (
        P("domain", "band"),
        P("band", "domain"),
        P("domain", None, None),
        P("domain", None),
        P("domain"),
    )
    out_specs = P("domain", "band")
    return jax.shard_map(local, mesh=mesh, in_specs=in_specs, out_specs=out_specs, check_vma=False)
```

```python
import functools

import jax
import jax.numpy as jnp
from jax import lax
from jax.experimental import pallas as pl
from jax.experimental.pallas import tpu as pltpu
from jax.sharding import PartitionSpec as P

CORE, NEAR, FAR = 1, 2, 4
VMEM = pl.BlockSpec(memory_space=pltpu.VMEM)
ANY = pl.BlockSpec(memory_space=pl.ANY)
F32, BF16 = jnp.float32, jnp.bfloat16


def dot(left, right):
    precision = lax.Precision.HIGHEST if left.dtype == F32 else None
    return jnp.dot(left, right, precision=precision, preferred_element_type=F32)


def split(value):
    high = value.astype(BF16)
    return high, (value - high.astype(F32)).astype(BF16)


def shifted(value, axis, steps):
    count = lax.axis_size(axis)
    leading, last = (max(0, -steps), min(count, count - steps))
    return lax.ppermute(value, axis, [(source, source + steps) for source in range(leading, last)])


def exchanged(value, axis, mask, core=None):
    sources = range(lax.axis_size(axis))
    return lax.ppermute(value, axis, [(source, source ^ mask) for source in sources if core in (None, source & CORE)])


def call(kernel, outs, operands, after=(), spaces=None, scratch=()):
    after = tuple(after)
    count = len(operands)

    def body(*refs):
        kernel(*refs[:count], *refs[count + len(after) :])

    return pl.pallas_call(
        body,
        out_shape=outs,
        in_specs=[pl.BlockSpec(memory_space=space) for space in spaces or [pltpu.VMEM] * count] + [ANY] * len(after),
        out_specs=[VMEM] * len(outs),
        scratch_shapes=list(scratch),
        cost_estimate=pl.CostEstimate(flops=0, bytes_accessed=1024, transcendentals=0),
        compiler_params=pltpu.CompilerParams(vmem_limit_bytes=24 * 2**20),
    )(*operands, *after)


def shape(*dims, dtype=F32):
    return jax.ShapeDtypeStruct(dims, dtype)


def core():
    return lax.rem(lax.axis_index("domain"), 2)


def block_of_band():
    return lax.bitwise_xor(lax.div(lax.axis_index("domain"), 2), lax.axis_index("band"))


def pieces_kernel(far, near, top, bottom, done):
    cut, rest = top.shape[0], bottom.shape[0]
    copies = [
        pltpu.make_async_copy(near.at[pl.ds(0, cut)], top, done.at[0]),
        pltpu.make_async_copy(far.at[pl.ds(cut, rest)], bottom, done.at[1]),
    ]
    for copy in copies:
        copy.start()
    for copy in copies:
        copy.wait()


def own_kernel(mine, theirs, own, block):
    rows = mine.shape[0]
    for side, states in enumerate((mine, theirs)):
        block[side * rows : (side + 1) * rows] = jnp.dot(states[...], own[...], preferred_element_type=F32)


def early_kernel(mine, theirs, near_even, far_even, near_odd, far_odd, near_block, far_block):
    rows, width = mine.shape[0], near_even.shape[1]
    first = core() == 0
    near, far = jnp.where(first, near_even[...], near_odd[...]), jnp.where(first, far_even[...], far_odd[...])
    wide = jnp.concatenate([near, far], 1)
    for side, states in enumerate((mine, theirs)):
        result = jnp.dot(states[...], wide, preferred_element_type=F32)
        near_block[side * rows : (side + 1) * rows] = result[:, :width]
        far_block[side * rows : (side + 1) * rows] = result[:, width:]


def late_kernel(mine, theirs, top_even, bottom_even, top_odd, bottom_odd, own, near, far, kept, *refs):
    sent, last = refs[:-1], refs[-1]
    rows = mine.shape[0]

    def multiply(top, bottom):
        cut = top.shape[0]
        for side, states in enumerate((mine, theirs)):
            result = jnp.dot(states[:, :cut], top[...], preferred_element_type=F32)
            last[side * rows : (side + 1) * rows] = result + jnp.dot(states[:, cut:], bottom[...], preferred_element_type=F32)

    pl.when(core() == 0)(lambda: multiply(top_even, bottom_even))
    pl.when(core() != 0)(lambda: multiply(top_odd, bottom_odd))
    where = block_of_band()

    def store(out, slot, block):
        @pl.when(slot == lax.bitwise_xor(where, mask))
        def _():
            out[...] = block[...].astype(out.dtype)

    for mask, out in enumerate((kept, *sent)):
        for slot, block in enumerate((own, near, far, last)):
            store(out, slot, block)


def sum_kernel(kept, *refs):
    parts, (mine, theirs) = refs[:-2], refs[-2:]
    value = kept[...]
    for part in parts:
        value = value + part[...].astype(F32)
    rows = mine.shape[0]
    mine[...] = value[:rows]
    theirs[...] = value[rows:]


def rotate_square(wavefunctions, rotation, operator):
    bands, chips = lax.axis_size("band"), lax.axis_size("domain") // 2
    rows, states = wavefunctions.shape
    width = rotation.shape[1]
    received = [exchanged(rotation, "domain", NEAR, 0), exchanged(rotation, "domain", FAR, 0)]
    theirs = exchanged(wavefunctions, "domain", CORE)
    block = [shape(2 * rows, width)]
    own = call(own_kernel, block, (wavefunctions, theirs, rotation))[0]
    operator = operator(own)
    later, _ = lax.optimization_barrier((rotation, operator[0]))
    received += [exchanged(later, "domain", NEAR, CORE), exchanged(later, "domain", FAR, CORE)]
    passed, previous = [], []
    for one, share in ((0, 21), (CORE, 17)):
        cut = states * share // 32
        outs = [shape(count, width, dtype=BF16) for count in (cut, states - cut)]
        pair = received[2 * one : 2 * one + 2][::-1]
        top, bottom = call(pieces_kernel, outs, pair, after=previous, scratch=[pltpu.SemaphoreType.DMA((2,))])
        previous = [bottom]
        passed += [exchanged(top, "domain", FAR, one), exchanged(bottom, "domain", NEAR, one)]
    early = call(early_kernel, block * 2, (wavefunctions, theirs, *received))
    outs = block + [shape(2 * rows, width, dtype=BF16)] * (bands - 1)
    scratch = [pltpu.VMEM((2 * rows, width), F32)]
    kept, *sent = call(late_kernel, outs, (wavefunctions, theirs, *passed, own, *early), scratch=scratch)
    parts = [exchanged(sent[mask - 1], "band", mask) for mask in (1, *reversed(range(2, bands)))]
    mine, others = call(sum_kernel, [shape(rows, width)] * 2, (kept, *parts))
    return mine, exchanged(others, "domain", CORE), operator


def rotate_any(wavefunctions, rotation):
    columns = lax.all_gather(rotation, "domain", axis=1, tiled=True)
    return lax.psum_scatter(dot(wavefunctions, columns), "band", scatter_dimension=1, tiled=True)


def faces_kernel(mine, other, assembled, pick, total, inward, outward):
    own, width = mine.shape
    columns = 2 * width
    first = core() == 0
    for side, half in enumerate((jnp.where(first, mine[...], other[...]), jnp.where(first, other[...], mine[...]))):
        total[:, side * width : (side + 1) * width] = half
    high, low = split(total[...])
    faces = dot(pick[...], high).astype(BF16)
    onward = (dot(assembled[own:, :own], high) + dot(assembled[own:, :own], low)).astype(BF16)
    corner = assembled[own:, own:]

    def store(forward, backward):
        forward[:, :columns] = onward
        forward[:, columns:] = corner
        backward[:, :columns] = faces
        backward[:, columns:] = corner

    pl.when(first)(lambda: store(inward, outward))
    pl.when(jnp.logical_not(first))(lambda: store(outward, inward))


def inner_kernel(total, assembled, pick, out, face_high, face_low):
    own = total.shape[0]
    high, low = split(total[...])
    inner = assembled[:own, :own]
    out[...] = dot(inner, high) + dot(inner, low)
    face_high[...] = dot(pick[...], high).astype(BF16)
    face_low[...] = dot(pick[...], low).astype(BF16)


def final_kernel(inner, face_high, face_low, assembled, spread, inward, outward, out):
    own, columns = inner.shape
    first = core() == 0
    incoming = jnp.where(first, inward[:, :columns], outward[:, :columns])
    back = jnp.where(first, outward[...], inward[...])
    corner = back[:, columns:]
    value = back[:, :columns].astype(F32) + dot(corner, face_high[...]) + dot(corner, face_low[...])
    high, low = split(value)
    out[...] = inner[...] + dot(assembled[:own, own:], incoming) + dot(spread[...], high) + dot(spread[...], low)


def finish_square(mine, other, operator):
    assembled, pick, spread = operator
    rows, width = mine.shape
    shared, columns = pick.shape[0], 2 * width
    outs = [shape(rows, columns)] + [shape(shared, columns + shared, dtype=BF16)] * 2
    total, inward, outward = call(faces_kernel, outs, (mine, other, assembled, pick))
    across = [(place, place + 1) for place in range(CORE, lax.axis_size("domain") - 1, 2)]
    outward = lax.ppermute(outward, "domain", across + [(target, source) for source, target in across])
    inward = exchanged(inward, "domain", CORE)
    outs = [shape(rows, columns)] + [shape(shared, columns, dtype=BF16)] * 2
    inner, *face = call(inner_kernel, outs, (total, assembled, pick))
    return call(final_kernel, outs[:1], (inner, *face, assembled, spread, inward, outward))[0]


def finish_any(rotated, cell_matrices, cell_nodes, face_map):
    own = rotated.shape[0]
    assembled, pick, returned = assemble_any(cell_matrices, cell_nodes, face_map, own)
    rotated = rotated.astype(BF16).astype(assembled.dtype)
    incoming = shifted(dot(pick, rotated).astype(BF16), "domain", -1).astype(assembled.dtype)
    back = shifted(dot(assembled[own:, :own], rotated), "domain", 1)
    inner = dot(assembled[:own, :own], rotated) + dot(returned, rotated) + dot(assembled[:own, own:], incoming)
    return inner + dot(pick.T.astype(F32), back)


def assemble_any(cell_matrices, cell_nodes, face_map, own):
    cells = cell_nodes.shape[0]
    extent = own + face_map.shape[0]
    held = BF16 if cells == 1 else F32
    places = jax.nn.one_hot(cell_nodes, extent, dtype=held)
    assembled = jnp.zeros((extent, extent), F32)
    for cell in range(cells):
        rows = dot(places[cell].T, cell_matrices[cell].astype(held)).astype(held)
        assembled = assembled + dot(rows, places[cell])
    assembled = assembled.astype(held)
    pick = jax.nn.one_hot(face_map, own, dtype=held)
    corner = shifted(assembled[own:, own:], "domain", 1)
    returned = dot(dot(pick.T, corner).astype(held), pick).astype(held)
    return assembled, pick, returned


def assemble_kernel(matrix, nodes, faces, assembled, pick, spread):
    extent = assembled.shape[0]
    places = jnp.where(lax.broadcasted_iota(jnp.int32, (extent, extent), 0) == nodes[...], 1.0, 0.0).astype(BF16)
    rows = dot(places, matrix[0]).astype(BF16)
    whole = lax.dot_general(rows, places, (((1,), (1,)), ((), ())), preferred_element_type=F32)
    assembled[...] = whole.astype(BF16)
    chosen = jnp.where(lax.broadcasted_iota(jnp.int32, spread.shape, 0) == faces[...], 1.0, 0.0)
    spread[...] = chosen.astype(BF16)
    pick[...] = chosen.T.astype(BF16)


def assemble(cell_matrices, cell_nodes, face_map, own, after):
    shared = face_map.shape[0]
    outs = [(own + shared, own + shared), (shared, own), (own, shared)]
    operands = (cell_matrices, cell_nodes, face_map.reshape(1, shared))
    return call(assemble_kernel, [shape(*dims, dtype=BF16) for dims in outs], operands, after=(after,))


def local(wavefunctions, rotation, cell_matrices, cell_nodes, face_map):
    chips = lax.axis_size("domain") // 2
    if chips == FAR and chips == lax.axis_size("band") and cell_nodes.shape[0] == 1:
        operator = functools.partial(assemble, cell_matrices, cell_nodes, face_map, wavefunctions.shape[0])
        return finish_square(*rotate_square(wavefunctions, rotation, operator))
    return finish_any(rotate_any(wavefunctions, rotation), cell_matrices, cell_nodes, face_map)


def solution(mesh):
    in_specs = (
        P("domain", "band"),
        P("band", "domain"),
        P("domain", None, None),
        P("domain", None),
        P("domain"),
    )
    out_specs = P("domain", "band")
    return jax.shard_map(local, mesh=mesh, in_specs=in_specs, out_specs=out_specs, check_vma=False)
```

```python
import functools

import jax
import jax.numpy as jnp
from jax import lax
from jax.experimental import pallas as pl
from jax.experimental.pallas import tpu as pltpu
from jax.sharding import PartitionSpec as P

CORE, NEAR, FAR = 1, 2, 4
VMEM = pl.BlockSpec(memory_space=pltpu.VMEM)
ANY = pl.BlockSpec(memory_space=pl.ANY)
F32, BF16 = jnp.float32, jnp.bfloat16


def dot(left, right):
    precision = lax.Precision.HIGHEST if left.dtype == F32 else None
    return jnp.dot(left, right, precision=precision, preferred_element_type=F32)


def split(value):
    high = value.astype(BF16)
    return high, (value - high.astype(F32)).astype(BF16)


def shifted(value, axis, steps):
    count = lax.axis_size(axis)
    leading, last = (max(0, -steps), min(count, count - steps))
    return lax.ppermute(value, axis, [(source, source + steps) for source in range(leading, last)])


def exchanged(value, axis, mask, core=None):
    sources = range(lax.axis_size(axis))
    return lax.ppermute(value, axis, [(source, source ^ mask) for source in sources if core in (None, source & CORE)])


def call(kernel, outs, operands, after=(), spaces=None, scratch=()):
    after = tuple(after)
    count = len(operands)

    def body(*refs):
        kernel(*refs[:count], *refs[count + len(after) :])

    return pl.pallas_call(
        body,
        out_shape=outs,
        in_specs=[pl.BlockSpec(memory_space=space) for space in spaces or [pltpu.VMEM] * count] + [ANY] * len(after),
        out_specs=[VMEM] * len(outs),
        scratch_shapes=list(scratch),
        cost_estimate=pl.CostEstimate(flops=0, bytes_accessed=1024, transcendentals=0),
        compiler_params=pltpu.CompilerParams(vmem_limit_bytes=24 * 2**20),
    )(*operands, *after)


def shape(*dims, dtype=F32):
    return jax.ShapeDtypeStruct(dims, dtype)


def core():
    return lax.rem(lax.axis_index("domain"), 2)


def block_of_band():
    return lax.bitwise_xor(lax.div(lax.axis_index("domain"), 2), lax.axis_index("band"))


def piece_kernel(start, shard, out, done):
    copy = pltpu.make_async_copy(shard.at[pl.ds(start, out.shape[0])], out, done)
    copy.start()
    copy.wait()


def own_kernel(mine, theirs, own, block):
    rows = mine.shape[0]
    for side, states in enumerate((mine, theirs)):
        block[side * rows : (side + 1) * rows] = jnp.dot(states[...], own[...], preferred_element_type=F32)


def early_kernel(mine, theirs, near_even, far_even, near_odd, far_odd, near_block, far_block):
    rows, width = mine.shape[0], near_even.shape[1]
    first = core() == 0
    near, far = jnp.where(first, near_even[...], near_odd[...]), jnp.where(first, far_even[...], far_odd[...])
    wide = jnp.concatenate([near, far], 1)
    for side, states in enumerate((mine, theirs)):
        result = jnp.dot(states[...], wide, preferred_element_type=F32)
        near_block[side * rows : (side + 1) * rows] = result[:, :width]
        far_block[side * rows : (side + 1) * rows] = result[:, width:]


def lower_kernel(mine, theirs, bottom_even, bottom_odd, block):
    rows = mine.shape[0]

    def multiply(bottom):
        start = mine.shape[1] - bottom.shape[0]
        for side, states in enumerate((mine, theirs)):
            result = jnp.dot(states[:, start:], bottom[...], preferred_element_type=F32)
            block[side * rows : (side + 1) * rows] = result

    pl.when(core() == 0)(lambda: multiply(bottom_even))
    pl.when(core() != 0)(lambda: multiply(bottom_odd))


def late_kernel(mine, theirs, top_even, top_odd, lower, own, near, far, kept, *refs):
    sent, last = refs[:-1], refs[-1]
    rows = mine.shape[0]

    def finish(top):
        cut = top.shape[0]
        for side, states in enumerate((mine, theirs)):
            span = slice(side * rows, (side + 1) * rows)
            last[span] = lower[span] + jnp.dot(states[:, :cut], top[...], preferred_element_type=F32)

    pl.when(core() == 0)(lambda: finish(top_even))
    pl.when(core() != 0)(lambda: finish(top_odd))
    where = block_of_band()

    def store(out, slot, block):
        @pl.when(slot == lax.bitwise_xor(where, mask))
        def _():
            out[...] = block[...].astype(out.dtype)

    for mask, out in enumerate((kept, *sent)):
        for slot, block in enumerate((own, near, far, last)):
            store(out, slot, block)


def sum_kernel(kept, *refs):
    parts, (mine, theirs) = refs[:-2], refs[-2:]
    value = kept[...]
    for part in parts:
        value = value + part[...].astype(F32)
    rows = mine.shape[0]
    mine[...] = value[:rows]
    theirs[...] = value[rows:]


def rotate_square(wavefunctions, rotation, operator):
    bands, chips = lax.axis_size("band"), lax.axis_size("domain") // 2
    rows, states = wavefunctions.shape
    width = rotation.shape[1]
    received = [exchanged(rotation, "domain", NEAR, 0), exchanged(rotation, "domain", FAR, 0)]
    theirs = exchanged(wavefunctions, "domain", CORE)
    block = [shape(2 * rows, width)]
    own = call(own_kernel, block, (wavefunctions, theirs, rotation))[0]
    operator = operator(own)
    later, _ = lax.optimization_barrier((rotation, operator[0]))
    received += [exchanged(later, "domain", NEAR, CORE), exchanged(later, "domain", FAR, CORE)]
    tops, bottoms, previous = [], [], []
    for one, share in ((0, 17), (CORE, 13)):
        cut = states * share // 32
        near, far = received[2 * one : 2 * one + 2]
        for parts, shard, start, count, mask in ((bottoms, far, cut, states - cut, NEAR), (tops, near, 0, cut, FAR)):
            kernel, outs = functools.partial(piece_kernel, start), [shape(count, width, dtype=BF16)]
            previous = call(kernel, outs, (shard,), after=previous, scratch=[pltpu.SemaphoreType.DMA])
            parts.append(exchanged(previous[0], "domain", mask, one))
    early = call(early_kernel, block * 2, (wavefunctions, theirs, *received))
    lower = call(lower_kernel, block, (wavefunctions, theirs, *bottoms), after=early[:1])[0]
    outs = block + [shape(2 * rows, width, dtype=BF16)] * (bands - 1)
    scratch = [pltpu.VMEM((2 * rows, width), F32)]
    kept, *sent = call(late_kernel, outs, (wavefunctions, theirs, *tops, lower, own, *early), scratch=scratch)
    parts = [exchanged(sent[mask - 1], "band", mask) for mask in (1, *reversed(range(2, bands)))]
    mine, others = call(sum_kernel, [shape(rows, width)] * 2, (kept, *parts))
    return mine, exchanged(others, "domain", CORE), operator


def rotate_any(wavefunctions, rotation):
    columns = lax.all_gather(rotation, "domain", axis=1, tiled=True)
    return lax.psum_scatter(dot(wavefunctions, columns), "band", scatter_dimension=1, tiled=True)


def faces_kernel(mine, other, assembled, pick, total, inward, outward):
    own, width = mine.shape
    columns = 2 * width
    first = core() == 0
    for side, half in enumerate((jnp.where(first, mine[...], other[...]), jnp.where(first, other[...], mine[...]))):
        total[:, side * width : (side + 1) * width] = half
    high, low = split(total[...])
    faces = dot(pick[...], high).astype(BF16)
    onward = (dot(assembled[own:, :own], high) + dot(assembled[own:, :own], low)).astype(BF16)
    corner = assembled[own:, own:]

    def store(forward, backward):
        forward[:, :columns] = onward
        forward[:, columns:] = corner
        backward[:, :columns] = faces
        backward[:, columns:] = corner

    pl.when(first)(lambda: store(inward, outward))
    pl.when(jnp.logical_not(first))(lambda: store(outward, inward))


def inner_kernel(total, assembled, pick, out, face_high, face_low):
    own = total.shape[0]
    high, low = split(total[...])
    inner = assembled[:own, :own]
    out[...] = dot(inner, high) + dot(inner, low)
    face_high[...] = dot(pick[...], high).astype(BF16)
    face_low[...] = dot(pick[...], low).astype(BF16)


def final_kernel(inner, face_high, face_low, assembled, spread, inward, outward, out):
    own, columns = inner.shape
    first = core() == 0
    incoming = jnp.where(first, inward[:, :columns], outward[:, :columns])
    back = jnp.where(first, outward[...], inward[...])
    corner = back[:, columns:]
    value = back[:, :columns].astype(F32) + dot(corner, face_high[...]) + dot(corner, face_low[...])
    high, low = split(value)
    out[...] = inner[...] + dot(assembled[:own, own:], incoming) + dot(spread[...], high) + dot(spread[...], low)


def finish_square(mine, other, operator):
    assembled, pick, spread = operator
    rows, width = mine.shape
    shared, columns = pick.shape[0], 2 * width
    outs = [shape(rows, columns)] + [shape(shared, columns + shared, dtype=BF16)] * 2
    total, inward, outward = call(faces_kernel, outs, (mine, other, assembled, pick))
    across = [(place, place + 1) for place in range(CORE, lax.axis_size("domain") - 1, 2)]
    outward = lax.ppermute(outward, "domain", across + [(target, source) for source, target in across])
    inward = exchanged(inward, "domain", CORE)
    outs = [shape(rows, columns)] + [shape(shared, columns, dtype=BF16)] * 2
    inner, *face = call(inner_kernel, outs, (total, assembled, pick))
    return call(final_kernel, outs[:1], (inner, *face, assembled, spread, inward, outward))[0]


def finish_any(rotated, cell_matrices, cell_nodes, face_map):
    own = rotated.shape[0]
    assembled, pick, returned = assemble_any(cell_matrices, cell_nodes, face_map, own)
    rotated = rotated.astype(BF16).astype(assembled.dtype)
    incoming = shifted(dot(pick, rotated).astype(BF16), "domain", -1).astype(assembled.dtype)
    back = shifted(dot(assembled[own:, :own], rotated), "domain", 1)
    inner = dot(assembled[:own, :own], rotated) + dot(returned, rotated) + dot(assembled[:own, own:], incoming)
    return inner + dot(pick.T.astype(F32), back)


def assemble_any(cell_matrices, cell_nodes, face_map, own):
    cells = cell_nodes.shape[0]
    extent = own + face_map.shape[0]
    held = BF16 if cells == 1 else F32
    places = jax.nn.one_hot(cell_nodes, extent, dtype=held)
    assembled = jnp.zeros((extent, extent), F32)
    for cell in range(cells):
        rows = dot(places[cell].T, cell_matrices[cell].astype(held)).astype(held)
        assembled = assembled + dot(rows, places[cell])
    assembled = assembled.astype(held)
    pick = jax.nn.one_hot(face_map, own, dtype=held)
    corner = shifted(assembled[own:, own:], "domain", 1)
    returned = dot(dot(pick.T, corner).astype(held), pick).astype(held)
    return assembled, pick, returned


def assemble_kernel(matrix, nodes, faces, assembled, pick, spread):
    extent = assembled.shape[0]
    places = jnp.where(lax.broadcasted_iota(jnp.int32, (extent, extent), 0) == nodes[...], 1.0, 0.0).astype(BF16)
    rows = dot(places, matrix[0]).astype(BF16)
    whole = lax.dot_general(rows, places, (((1,), (1,)), ((), ())), preferred_element_type=F32)
    assembled[...] = whole.astype(BF16)
    chosen = jnp.where(lax.broadcasted_iota(jnp.int32, spread.shape, 0) == faces[...], 1.0, 0.0)
    spread[...] = chosen.astype(BF16)
    pick[...] = chosen.T.astype(BF16)


def assemble(cell_matrices, cell_nodes, face_map, own, after):
    shared = face_map.shape[0]
    outs = [(own + shared, own + shared), (shared, own), (own, shared)]
    operands = (cell_matrices, cell_nodes, face_map.reshape(1, shared))
    return call(assemble_kernel, [shape(*dims, dtype=BF16) for dims in outs], operands, after=(after,))


def local(wavefunctions, rotation, cell_matrices, cell_nodes, face_map):
    chips = lax.axis_size("domain") // 2
    if chips == FAR and chips == lax.axis_size("band") and cell_nodes.shape[0] == 1:
        operator = functools.partial(assemble, cell_matrices, cell_nodes, face_map, wavefunctions.shape[0])
        return finish_square(*rotate_square(wavefunctions, rotation, operator))
    return finish_any(rotate_any(wavefunctions, rotation), cell_matrices, cell_nodes, face_map)


def solution(mesh):
    in_specs = (
        P("domain", "band"),
        P("band", "domain"),
        P("domain", None, None),
        P("domain", None),
        P("domain"),
    )
    out_specs = P("domain", "band")
    return jax.shard_map(local, mesh=mesh, in_specs=in_specs, out_specs=out_specs, check_vma=False)
```

```python
import functools

import jax
import jax.numpy as jnp
from jax import lax
from jax.experimental import pallas as pl
from jax.experimental.pallas import tpu as pltpu
from jax.sharding import PartitionSpec as P

CORE, NEAR, FAR = 1, 2, 4
VMEM = pl.BlockSpec(memory_space=pltpu.VMEM)
ANY = pl.BlockSpec(memory_space=pl.ANY)
F32, BF16 = jnp.float32, jnp.bfloat16


def dot(left, right):
    precision = lax.Precision.HIGHEST if left.dtype == F32 else None
    return jnp.dot(left, right, precision=precision, preferred_element_type=F32)


def split(value):
    high = value.astype(BF16)
    return high, (value - high.astype(F32)).astype(BF16)


def shifted(value, axis, steps):
    count = lax.axis_size(axis)
    leading, last = (max(0, -steps), min(count, count - steps))
    return lax.ppermute(value, axis, [(source, source + steps) for source in range(leading, last)])


def exchanged(value, axis, mask, core=None):
    sources = range(lax.axis_size(axis))
    pairs = [(source, source ^ mask if core in (None, source & CORE) else source) for source in sources]
    return lax.ppermute(value, axis, pairs)


def call(kernel, outs, operands, after=(), spaces=None, scratch=()):
    after = tuple(after)
    count = len(operands)

    def body(*refs):
        kernel(*refs[:count], *refs[count + len(after) :])

    return pl.pallas_call(
        body,
        out_shape=outs,
        in_specs=[pl.BlockSpec(memory_space=space) for space in spaces or [pltpu.VMEM] * count] + [ANY] * len(after),
        out_specs=[VMEM] * len(outs),
        scratch_shapes=list(scratch),
        cost_estimate=pl.CostEstimate(flops=0, bytes_accessed=1024, transcendentals=0),
        compiler_params=pltpu.CompilerParams(vmem_limit_bytes=24 * 2**20),
    )(*operands, *after)


def shape(*dims, dtype=F32):
    return jax.ShapeDtypeStruct(dims, dtype)


def core():
    return lax.rem(lax.axis_index("domain"), 2)


def block_of_band():
    return lax.bitwise_xor(lax.div(lax.axis_index("domain"), 2), lax.axis_index("band"))


def pieces_kernel(far, near, top, bottom, done):
    cut, rest = top.shape[0], bottom.shape[0]
    copies = [
        pltpu.make_async_copy(near.at[pl.ds(0, cut)], top, done.at[0]),
        pltpu.make_async_copy(far.at[pl.ds(cut, rest)], bottom, done.at[1]),
    ]
    for copy in copies:
        copy.start()
    for copy in copies:
        copy.wait()


def own_kernel(mine, theirs, own, block):
    rows = mine.shape[0]
    for side, states in enumerate((mine, theirs)):
        block[side * rows : (side + 1) * rows] = jnp.dot(states[...], own[...], preferred_element_type=F32)


def early_kernel(mine, theirs, near_even, far_even, near_odd, far_odd, near_block, far_block):
    rows, width = mine.shape[0], near_even.shape[1]
    first = core() == 0
    near, far = jnp.where(first, near_even[...], near_odd[...]), jnp.where(first, far_even[...], far_odd[...])
    wide = jnp.concatenate([near, far], 1)
    for side, states in enumerate((mine, theirs)):
        result = jnp.dot(states[...], wide, preferred_element_type=F32)
        near_block[side * rows : (side + 1) * rows] = result[:, :width]
        far_block[side * rows : (side + 1) * rows] = result[:, width:]


def late_kernel(mine, theirs, top_even, bottom_even, top_odd, bottom_odd, own, near, far, kept, *refs):
    sent, last = refs[:-1], refs[-1]
    rows = mine.shape[0]

    def multiply(top, bottom):
        cut = top.shape[0]
        for side, states in enumerate((mine, theirs)):
            result = jnp.dot(states[:, :cut], top[...], preferred_element_type=F32)
            last[side * rows : (side + 1) * rows] = result + jnp.dot(states[:, cut:], bottom[...], preferred_element_type=F32)

    pl.when(core() == 0)(lambda: multiply(top_even, bottom_even))
    pl.when(core() != 0)(lambda: multiply(top_odd, bottom_odd))
    where = block_of_band()

    def store(out, slot, block):
        @pl.when(slot == lax.bitwise_xor(where, mask))
        def _():
            out[...] = block[...].astype(out.dtype)

    for mask, out in enumerate((kept, *sent)):
        for slot, block in enumerate((own, near, far, last)):
            store(out, slot, block)


def sum_kernel(kept, *refs):
    parts, (mine, theirs) = refs[:-2], refs[-2:]
    value = kept[...]
    for part in parts:
        value = value + part[...].astype(F32)
    rows = mine.shape[0]
    mine[...] = value[:rows]
    theirs[...] = value[rows:]


def rotate_square(wavefunctions, rotation, operator):
    bands, chips = lax.axis_size("band"), lax.axis_size("domain") // 2
    rows, states = wavefunctions.shape
    width = rotation.shape[1]
    received = [exchanged(rotation, "domain", NEAR, 0), exchanged(rotation, "domain", FAR, 0)]
    theirs = exchanged(wavefunctions, "domain", CORE)
    block = [shape(2 * rows, width)]
    own = call(own_kernel, block, (wavefunctions, theirs, rotation))[0]
    operator = operator(own)
    later, _ = lax.optimization_barrier((rotation, operator[0]))
    received += [exchanged(later, "domain", NEAR, CORE), exchanged(later, "domain", FAR, CORE)]
    passed, previous = [], []
    for one, share in ((0, 21), (CORE, 17)):
        cut = states * share // 32
        outs = [shape(count, width, dtype=BF16) for count in (cut, states - cut)]
        pair = received[2 * one : 2 * one + 2][::-1]
        top, bottom = call(pieces_kernel, outs, pair, after=previous, scratch=[pltpu.SemaphoreType.DMA((2,))])
        previous = [bottom]
        passed += [exchanged(top, "domain", FAR, one), exchanged(bottom, "domain", NEAR, one)]
    early = call(early_kernel, block * 2, (wavefunctions, theirs, *received))
    outs = block + [shape(2 * rows, width, dtype=BF16)] * (bands - 1)
    scratch = [pltpu.VMEM((2 * rows, width), F32)]
    kept, *sent = call(late_kernel, outs, (wavefunctions, theirs, *passed, own, *early), scratch=scratch)
    parts = [exchanged(sent[mask - 1], "band", mask) for mask in (1, *reversed(range(2, bands)))]
    mine, others = call(sum_kernel, [shape(rows, width)] * 2, (kept, *parts))
    return mine, exchanged(others, "domain", CORE), operator


def rotate_any(wavefunctions, rotation):
    columns = lax.all_gather(rotation, "domain", axis=1, tiled=True)
    return lax.psum_scatter(dot(wavefunctions, columns), "band", scatter_dimension=1, tiled=True)


def faces_kernel(mine, other, assembled, pick, total, inward, outward):
    own, width = mine.shape
    columns = 2 * width
    first = core() == 0
    for side, half in enumerate((jnp.where(first, mine[...], other[...]), jnp.where(first, other[...], mine[...]))):
        total[:, side * width : (side + 1) * width] = half
    high, low = split(total[...])
    faces = dot(pick[...], high).astype(BF16)
    onward = (dot(assembled[own:, :own], high) + dot(assembled[own:, :own], low)).astype(BF16)
    corner = assembled[own:, own:]

    def store(forward, backward):
        forward[:, :columns] = onward
        forward[:, columns:] = corner
        backward[:, :columns] = faces
        backward[:, columns:] = corner

    pl.when(first)(lambda: store(inward, outward))
    pl.when(jnp.logical_not(first))(lambda: store(outward, inward))


def inner_kernel(total, assembled, pick, out, face_high, face_low):
    own = total.shape[0]
    high, low = split(total[...])
    inner = assembled[:own, :own]
    out[...] = dot(inner, high) + dot(inner, low)
    face_high[...] = dot(pick[...], high).astype(BF16)
    face_low[...] = dot(pick[...], low).astype(BF16)


def final_kernel(inner, face_high, face_low, assembled, spread, inward, outward, out):
    own, columns = inner.shape
    first = core() == 0
    incoming = jnp.where(first, inward[:, :columns], outward[:, :columns])
    back = jnp.where(first, outward[...], inward[...])
    corner = back[:, columns:]
    value = back[:, :columns].astype(F32) + dot(corner, face_high[...]) + dot(corner, face_low[...])
    high, low = split(value)
    out[...] = inner[...] + dot(assembled[:own, own:], incoming) + dot(spread[...], high) + dot(spread[...], low)


def finish_square(mine, other, operator):
    assembled, pick, spread = operator
    rows, width = mine.shape
    shared, columns = pick.shape[0], 2 * width
    outs = [shape(rows, columns)] + [shape(shared, columns + shared, dtype=BF16)] * 2
    total, inward, outward = call(faces_kernel, outs, (mine, other, assembled, pick))
    across = [(place, place + 1) for place in range(CORE, lax.axis_size("domain") - 1, 2)]
    outward = lax.ppermute(outward, "domain", across + [(target, source) for source, target in across])
    inward = exchanged(inward, "domain", CORE)
    outs = [shape(rows, columns)] + [shape(shared, columns, dtype=BF16)] * 2
    inner, *face = call(inner_kernel, outs, (total, assembled, pick))
    return call(final_kernel, outs[:1], (inner, *face, assembled, spread, inward, outward))[0]


def finish_any(rotated, cell_matrices, cell_nodes, face_map):
    own = rotated.shape[0]
    assembled, pick, returned = assemble_any(cell_matrices, cell_nodes, face_map, own)
    rotated = rotated.astype(BF16).astype(assembled.dtype)
    incoming = shifted(dot(pick, rotated).astype(BF16), "domain", -1).astype(assembled.dtype)
    back = shifted(dot(assembled[own:, :own], rotated), "domain", 1)
    inner = dot(assembled[:own, :own], rotated) + dot(returned, rotated) + dot(assembled[:own, own:], incoming)
    return inner + dot(pick.T.astype(F32), back)


def assemble_any(cell_matrices, cell_nodes, face_map, own):
    cells = cell_nodes.shape[0]
    extent = own + face_map.shape[0]
    held = BF16 if cells == 1 else F32
    places = jax.nn.one_hot(cell_nodes, extent, dtype=held)
    assembled = jnp.zeros((extent, extent), F32)
    for cell in range(cells):
        rows = dot(places[cell].T, cell_matrices[cell].astype(held)).astype(held)
        assembled = assembled + dot(rows, places[cell])
    assembled = assembled.astype(held)
    pick = jax.nn.one_hot(face_map, own, dtype=held)
    corner = shifted(assembled[own:, own:], "domain", 1)
    returned = dot(dot(pick.T, corner).astype(held), pick).astype(held)
    return assembled, pick, returned


def assemble_kernel(matrix, nodes, faces, assembled, pick, spread):
    extent = assembled.shape[0]
    places = jnp.where(lax.broadcasted_iota(jnp.int32, (extent, extent), 0) == nodes[...], 1.0, 0.0).astype(BF16)
    rows = dot(places, matrix[0]).astype(BF16)
    whole = lax.dot_general(rows, places, (((1,), (1,)), ((), ())), preferred_element_type=F32)
    assembled[...] = whole.astype(BF16)
    chosen = jnp.where(lax.broadcasted_iota(jnp.int32, spread.shape, 0) == faces[...], 1.0, 0.0)
    spread[...] = chosen.astype(BF16)
    pick[...] = chosen.T.astype(BF16)


def assemble(cell_matrices, cell_nodes, face_map, own, after):
    shared = face_map.shape[0]
    outs = [(own + shared, own + shared), (shared, own), (own, shared)]
    operands = (cell_matrices, cell_nodes, face_map.reshape(1, shared))
    return call(assemble_kernel, [shape(*dims, dtype=BF16) for dims in outs], operands, after=(after,))


def local(wavefunctions, rotation, cell_matrices, cell_nodes, face_map):
    chips = lax.axis_size("domain") // 2
    if chips == FAR and chips == lax.axis_size("band") and cell_nodes.shape[0] == 1:
        operator = functools.partial(assemble, cell_matrices, cell_nodes, face_map, wavefunctions.shape[0])
        return finish_square(*rotate_square(wavefunctions, rotation, operator))
    return finish_any(rotate_any(wavefunctions, rotation), cell_matrices, cell_nodes, face_map)


def solution(mesh):
    in_specs = (
        P("domain", "band"),
        P("band", "domain"),
        P("domain", None, None),
        P("domain", None),
        P("domain"),
    )
    out_specs = P("domain", "band")
    return jax.shard_map(local, mesh=mesh, in_specs=in_specs, out_specs=out_specs, check_vma=False)
```

```python
import functools

import jax
import jax.numpy as jnp
from jax import lax
from jax.experimental import pallas as pl
from jax.experimental.pallas import tpu as pltpu
from jax.sharding import PartitionSpec as P

CORE, NEAR, FAR = 1, 2, 4
VMEM = pl.BlockSpec(memory_space=pltpu.VMEM)
ANY = pl.BlockSpec(memory_space=pl.ANY)
F32, BF16 = jnp.float32, jnp.bfloat16


def dot(left, right):
    precision = lax.Precision.HIGHEST if left.dtype == F32 else None
    return jnp.dot(left, right, precision=precision, preferred_element_type=F32)


def split(value):
    high = value.astype(BF16)
    return high, (value - high.astype(F32)).astype(BF16)


def shifted(value, axis, steps):
    count = lax.axis_size(axis)
    leading, last = (max(0, -steps), min(count, count - steps))
    return lax.ppermute(value, axis, [(source, source + steps) for source in range(leading, last)])


def exchanged(value, axis, mask, core=None):
    sources = range(lax.axis_size(axis))
    return lax.ppermute(value, axis, [(source, source ^ mask) for source in sources if core in (None, source & CORE)])


def call(kernel, outs, operands, after=(), spaces=None, scratch=()):
    after = tuple(after)
    count = len(operands)

    def body(*refs):
        kernel(*refs[:count], *refs[count + len(after) :])

    return pl.pallas_call(
        body,
        out_shape=outs,
        in_specs=[pl.BlockSpec(memory_space=space) for space in spaces or [pltpu.VMEM] * count] + [ANY] * len(after),
        out_specs=[VMEM] * len(outs),
        scratch_shapes=list(scratch),
        cost_estimate=pl.CostEstimate(flops=0, bytes_accessed=1024, transcendentals=0),
        compiler_params=pltpu.CompilerParams(vmem_limit_bytes=24 * 2**20),
    )(*operands, *after)


def shape(*dims, dtype=F32):
    return jax.ShapeDtypeStruct(dims, dtype)


def core():
    return lax.rem(lax.axis_index("domain"), 2)


def block_of_band():
    return lax.bitwise_xor(lax.div(lax.axis_index("domain"), 2), lax.axis_index("band"))


def pieces_kernel(one, far, near, top, bottom, done):
    cut, rest = top.shape[0], bottom.shape[0]

    @pl.when(core() == one)
    def _():
        copies = [
            pltpu.make_async_copy(near.at[pl.ds(0, cut)], top, done.at[0]),
            pltpu.make_async_copy(far.at[pl.ds(cut, rest)], bottom, done.at[1]),
        ]
        for copy in copies:
            copy.start()
        for copy in copies:
            copy.wait()


def own_kernel(mine, theirs, own, block):
    rows = mine.shape[0]
    for side, states in enumerate((mine, theirs)):
        block[side * rows : (side + 1) * rows] = jnp.dot(states[...], own[...], preferred_element_type=F32)


def early_kernel(mine, theirs, near_even, far_even, near_odd, far_odd, near_block, far_block):
    rows, width = mine.shape[0], near_even.shape[1]
    first = core() == 0
    near, far = jnp.where(first, near_even[...], near_odd[...]), jnp.where(first, far_even[...], far_odd[...])
    wide = jnp.concatenate([near, far], 1)
    for side, states in enumerate((mine, theirs)):
        result = jnp.dot(states[...], wide, preferred_element_type=F32)
        near_block[side * rows : (side + 1) * rows] = result[:, :width]
        far_block[side * rows : (side + 1) * rows] = result[:, width:]


def late_kernel(mine, theirs, top_even, bottom_even, top_odd, bottom_odd, own, near, far, kept, *refs):
    sent, last = refs[:-1], refs[-1]
    rows = mine.shape[0]

    def multiply(top, bottom):
        cut = top.shape[0]
        for side, states in enumerate((mine, theirs)):
            result = jnp.dot(states[:, :cut], top[...], preferred_element_type=F32)
            last[side * rows : (side + 1) * rows] = result + jnp.dot(states[:, cut:], bottom[...], preferred_element_type=F32)

    pl.when(core() == 0)(lambda: multiply(top_even, bottom_even))
    pl.when(core() != 0)(lambda: multiply(top_odd, bottom_odd))
    where = block_of_band()

    def store(out, slot, block):
        @pl.when(slot == lax.bitwise_xor(where, mask))
        def _():
            out[...] = block[...].astype(out.dtype)

    for mask, out in enumerate((kept, *sent)):
        for slot, block in enumerate((own, near, far, last)):
            store(out, slot, block)


def sum_kernel(kept, *refs):
    parts, (mine, theirs) = refs[:-2], refs[-2:]
    value = kept[...]
    for part in parts:
        value = value + part[...].astype(F32)
    rows = mine.shape[0]
    mine[...] = value[:rows]
    theirs[...] = value[rows:]


def rotate_square(wavefunctions, rotation, operator):
    bands, chips = lax.axis_size("band"), lax.axis_size("domain") // 2
    rows, states = wavefunctions.shape
    width = rotation.shape[1]
    received = [exchanged(rotation, "domain", NEAR, 0), exchanged(rotation, "domain", FAR, 0)]
    theirs = exchanged(wavefunctions, "domain", CORE)
    block = [shape(2 * rows, width)]
    own = call(own_kernel, block, (wavefunctions, theirs, rotation))[0]
    operator = operator(own)
    later, _ = lax.optimization_barrier((rotation, operator[0]))
    received += [exchanged(later, "domain", NEAR, CORE), exchanged(later, "domain", FAR, CORE)]
    passed, previous = [], []
    for one, share in ((0, 21), (CORE, 19)):
        cut = states * share // 32
        outs = [shape(count, width, dtype=BF16) for count in (cut, states - cut)]
        pair = received[2 * one : 2 * one + 2][::-1]
        kernel = functools.partial(pieces_kernel, one)
        top, bottom = call(kernel, outs, pair, after=previous, scratch=[pltpu.SemaphoreType.DMA((2,))])
        previous = [bottom]
        passed += [exchanged(top, "domain", FAR, one), exchanged(bottom, "domain", NEAR, one)]
    early = call(early_kernel, block * 2, (wavefunctions, theirs, *received))
    outs = block + [shape(2 * rows, width, dtype=BF16)] * (bands - 1)
    scratch = [pltpu.VMEM((2 * rows, width), F32)]
    kept, *sent = call(late_kernel, outs, (wavefunctions, theirs, *passed, own, *early), scratch=scratch)
    parts = [exchanged(sent[mask - 1], "band", mask) for mask in (1, *reversed(range(2, bands)))]
    mine, others = call(sum_kernel, [shape(rows, width)] * 2, (kept, *parts))
    return mine, exchanged(others, "domain", CORE), operator


def rotate_any(wavefunctions, rotation):
    columns = lax.all_gather(rotation, "domain", axis=1, tiled=True)
    return lax.psum_scatter(dot(wavefunctions, columns), "band", scatter_dimension=1, tiled=True)


def faces_kernel(mine, other, assembled, pick, total, inward, outward):
    own, width = mine.shape
    columns = 2 * width
    first = core() == 0
    for side, half in enumerate((jnp.where(first, mine[...], other[...]), jnp.where(first, other[...], mine[...]))):
        total[:, side * width : (side + 1) * width] = half
    high, low = split(total[...])
    faces = dot(pick[...], high).astype(BF16)
    onward = (dot(assembled[own:, :own], high) + dot(assembled[own:, :own], low)).astype(BF16)
    corner = assembled[own:, own:]

    def store(forward, backward):
        forward[:, :columns] = onward
        forward[:, columns:] = corner
        backward[:, :columns] = faces
        backward[:, columns:] = corner

    pl.when(first)(lambda: store(inward, outward))
    pl.when(jnp.logical_not(first))(lambda: store(outward, inward))


def inner_kernel(total, assembled, pick, out, faces):
    own, columns = total.shape
    high, low = split(total[...])
    inner = assembled[:own, :own]
    out[...] = dot(inner, high) + dot(inner, low)
    faces[:, :columns] = dot(pick[...], high).astype(BF16)
    faces[:, columns:] = dot(pick[...], low).astype(BF16)


def final_kernel(inner, faces, assembled, spread, inward, outward, out):
    own, columns = inner.shape
    first = core() == 0
    incoming = jnp.where(first, inward[:, :columns], outward[:, :columns])
    back = jnp.where(first, outward[...], inward[...])
    extra = dot(back[:, columns:], faces[...])
    high, low = split(back[:, :columns].astype(F32) + extra[:, :columns] + extra[:, columns:])
    matrix = jnp.concatenate([assembled[:own, own:], spread[...], spread[...]], 1)
    out[...] = inner[...] + dot(matrix, jnp.concatenate([incoming, high, low], 0))


def finish_square(mine, other, operator):
    assembled, pick, spread = operator
    rows, width = mine.shape
    shared, columns = pick.shape[0], 2 * width
    outs = [shape(rows, columns)] + [shape(shared, columns + shared, dtype=BF16)] * 2
    total, inward, outward = call(faces_kernel, outs, (mine, other, assembled, pick))
    across = [(place, place + 1) for place in range(CORE, lax.axis_size("domain") - 1, 2)]
    outward = lax.ppermute(outward, "domain", across + [(target, source) for source, target in across])
    inward = exchanged(inward, "domain", CORE)
    outs = [shape(rows, columns), shape(shared, 2 * columns, dtype=BF16)]
    inner, faces = call(inner_kernel, outs, (total, assembled, pick))
    return call(final_kernel, outs[:1], (inner, faces, assembled, spread, inward, outward))[0]


def finish_any(rotated, cell_matrices, cell_nodes, face_map):
    own = rotated.shape[0]
    assembled, pick, returned = assemble_any(cell_matrices, cell_nodes, face_map, own)
    rotated = rotated.astype(BF16).astype(assembled.dtype)
    incoming = shifted(dot(pick, rotated).astype(BF16), "domain", -1).astype(assembled.dtype)
    back = shifted(dot(assembled[own:, :own], rotated), "domain", 1)
    inner = dot(assembled[:own, :own], rotated) + dot(returned, rotated) + dot(assembled[:own, own:], incoming)
    return inner + dot(pick.T.astype(F32), back)


def assemble_any(cell_matrices, cell_nodes, face_map, own):
    cells = cell_nodes.shape[0]
    extent = own + face_map.shape[0]
    held = BF16 if cells == 1 else F32
    places = jax.nn.one_hot(cell_nodes, extent, dtype=held)
    assembled = jnp.zeros((extent, extent), F32)
    for cell in range(cells):
        rows = dot(places[cell].T, cell_matrices[cell].astype(held)).astype(held)
        assembled = assembled + dot(rows, places[cell])
    assembled = assembled.astype(held)
    pick = jax.nn.one_hot(face_map, own, dtype=held)
    corner = shifted(assembled[own:, own:], "domain", 1)
    returned = dot(dot(pick.T, corner).astype(held), pick).astype(held)
    return assembled, pick, returned


def assemble_kernel(matrix, nodes, faces, assembled, pick, spread):
    extent = assembled.shape[0]
    places = jnp.where(lax.broadcasted_iota(jnp.int32, (extent, extent), 0) == nodes[...], 1.0, 0.0).astype(BF16)
    rows = dot(places, matrix[0]).astype(BF16)
    whole = lax.dot_general(rows, places, (((1,), (1,)), ((), ())), preferred_element_type=F32)
    assembled[...] = whole.astype(BF16)
    chosen = jnp.where(lax.broadcasted_iota(jnp.int32, spread.shape, 0) == faces[...], 1.0, 0.0)
    spread[...] = chosen.astype(BF16)
    pick[...] = chosen.T.astype(BF16)


def assemble(cell_matrices, cell_nodes, face_map, own, after):
    shared = face_map.shape[0]
    outs = [(own + shared, own + shared), (shared, own), (own, shared)]
    operands = (cell_matrices, cell_nodes, face_map.reshape(1, shared))
    return call(assemble_kernel, [shape(*dims, dtype=BF16) for dims in outs], operands, after=(after,))


def local(wavefunctions, rotation, cell_matrices, cell_nodes, face_map):
    chips = lax.axis_size("domain") // 2
    if chips == FAR and chips == lax.axis_size("band") and cell_nodes.shape[0] == 1:
        operator = functools.partial(assemble, cell_matrices, cell_nodes, face_map, wavefunctions.shape[0])
        return finish_square(*rotate_square(wavefunctions, rotation, operator))
    return finish_any(rotate_any(wavefunctions, rotation), cell_matrices, cell_nodes, face_map)


def solution(mesh):
    in_specs = (
        P("domain", "band"),
        P("band", "domain"),
        P("domain", None, None),
        P("domain", None),
        P("domain"),
    )
    out_specs = P("domain", "band")
    return jax.shard_map(local, mesh=mesh, in_specs=in_specs, out_specs=out_specs, check_vma=False)
```

```python
import functools

import jax
import jax.numpy as jnp
from jax import lax
from jax.experimental import pallas as pl
from jax.experimental.pallas import tpu as pltpu
from jax.sharding import PartitionSpec as P

CORE, NEAR, FAR = 1, 2, 4
VMEM = pl.BlockSpec(memory_space=pltpu.VMEM)
ANY = pl.BlockSpec(memory_space=pl.ANY)
F32, BF16 = jnp.float32, jnp.bfloat16


def dot(left, right):
    precision = lax.Precision.HIGHEST if left.dtype == F32 else None
    return jnp.dot(left, right, precision=precision, preferred_element_type=F32)


def split(value):
    high = value.astype(BF16)
    return high, (value - high.astype(F32)).astype(BF16)


def shifted(value, axis, steps):
    count = lax.axis_size(axis)
    leading, last = (max(0, -steps), min(count, count - steps))
    return lax.ppermute(value, axis, [(source, source + steps) for source in range(leading, last)])


def exchanged(value, axis, mask, core=None):
    sources = range(lax.axis_size(axis))
    return lax.ppermute(value, axis, [(source, source ^ mask) for source in sources if core in (None, source & CORE)])


def call(kernel, outs, operands, after=(), spaces=None, scratch=()):
    after = tuple(after)
    count = len(operands)

    def body(*refs):
        kernel(*refs[:count], *refs[count + len(after) :])

    return pl.pallas_call(
        body,
        out_shape=outs,
        in_specs=[pl.BlockSpec(memory_space=space) for space in spaces or [pltpu.VMEM] * count] + [ANY] * len(after),
        out_specs=[VMEM] * len(outs),
        scratch_shapes=list(scratch),
        cost_estimate=pl.CostEstimate(flops=0, bytes_accessed=1024, transcendentals=0),
        compiler_params=pltpu.CompilerParams(vmem_limit_bytes=24 * 2**20),
    )(*operands, *after)


def shape(*dims, dtype=F32):
    return jax.ShapeDtypeStruct(dims, dtype)


def core():
    return lax.rem(lax.axis_index("domain"), 2)


def block_of_band():
    return lax.bitwise_xor(lax.div(lax.axis_index("domain"), 2), lax.axis_index("band"))


def only(one):
    return pl.when(core() == one)


def pieces_kernel(one, *refs):
    (*shards, done), count = refs, (len(refs) - 1) // 2

    @only(one)
    def _():
        start = 0
        for number in range(count):
            out = shards[count + number]
            rows = out.shape[0]
            copy = pltpu.make_async_copy(shards[number].at[pl.ds(start, rows)], out, done)
            copy.start()
            copy.wait()
            start += rows


def part_kernel(start, one, shard, out, done):
    @only(one)
    def _():
        copy = pltpu.make_async_copy(shard.at[pl.ds(start, out.shape[0])], out, done)
        copy.start()
        copy.wait()


def multiply(mine, theirs, right, blocks, start=0, add=None):
    rows, width = mine.shape[0], right.shape[1] // len(blocks)
    for side, states in enumerate((mine, theirs)):
        span = slice(side * rows, (side + 1) * rows)
        result = jnp.dot(states[:, start : start + right.shape[0]], right, preferred_element_type=F32)
        for slot, block in enumerate(blocks):
            value = result[:, slot * width : (slot + 1) * width]
            block[span] = value if add is None else value + add[span]


def send(blocks, outs, masks):
    where = block_of_band()
    for mask, out in zip(masks, outs):
        for slot, block in blocks:

            @pl.when(slot == lax.bitwise_xor(where, mask))
            def _():
                out[...] = block[...].astype(out.dtype)


def own_kernel(mine, theirs, own, block):
    multiply(mine, theirs, own[...], [block])


def far_kernel(mine, theirs, far, own, block, *sent):
    @only(0)
    def _():
        multiply(mine, theirs, far[...], [block])
        send([(0, own), (2, block)], sent, range(1, len(sent) + 1))


def near_kernel(mine, theirs, near, block):
    only(0)(lambda: multiply(mine, theirs, near[...], [block]))


def first_late_kernel(mine, theirs, top, bottom, own, near, far, kept, *refs):
    sent, last = refs[:-1], refs[-1]

    @only(0)
    def _():
        multiply(mine, theirs, top[...], [last])
        multiply(mine, theirs, bottom[...], [last], top.shape[0], last)
        send([(0, own), (1, near), (2, far), (3, last)], [kept], [0])
        send([(1, near), (3, last)], sent, range(1, len(sent) + 1))


def early_kernel(mine, theirs, near, far, near_block, far_block):
    only(CORE)(lambda: multiply(mine, theirs, jnp.concatenate([near[...], far[...]], 1), [near_block, far_block]))


def lower_kernel(mine, theirs, bottom, block):
    only(CORE)(lambda: multiply(mine, theirs, bottom[...], [block], mine.shape[1] - bottom.shape[0]))


def late_kernel(mine, theirs, top, lower, own, near, far, kept, *refs):
    sent, last = refs[:-1], refs[-1]

    @only(CORE)
    def _():
        multiply(mine, theirs, top[...], [last], 0, lower)
        send([(0, own), (1, near), (2, far), (3, last)], [kept, *sent], range(len(sent) + 1))


def total_of(kept, parts):
    value = kept[...]
    for part in parts:
        value = value + part[...].astype(F32)
    return value


def first_sum_kernel(kept, *refs):
    parts, out = refs[:-1], refs[-1]

    @only(0)
    def _():
        out[...] = total_of(kept, parts)


def sum_kernel(other_total, kept, *refs):
    parts, (mine, theirs) = refs[:-2], refs[-2:]
    rows = mine.shape[0]

    def store(value):
        mine[...] = value[:rows]
        theirs[...] = value[rows:]

    only(0)(lambda: store(other_total[...]))
    only(CORE)(lambda: store(total_of(kept, parts)))


def rotate_square(wavefunctions, rotation, operator):
    bands, chips = lax.axis_size("band"), lax.axis_size("domain") // 2
    rows, states = wavefunctions.shape
    width = rotation.shape[1]
    block = [shape(2 * rows, width)]
    messages = [shape(2 * rows, width, dtype=BF16)] * (bands - 1)
    masks = range(1, bands)[::-1]
    scratch = [pltpu.VMEM((2 * rows, width), F32)]
    semaphore = [pltpu.SemaphoreType.DMA]

    def across(sent, one, slots):
        results = []
        for mask in masks:
            pairs = []
            for chip in range(chips):
                for band in range(bands):
                    if chip ^ band ^ mask in slots:
                        place = (2 * chip + one) * bands
                        pairs.append((place + band, place + (band ^ mask)))
            results.append(lax.ppermute(sent[mask - 1], ("domain", "band"), pairs))
        return results

    near, far = exchanged(rotation, "domain", NEAR, 0), exchanged(rotation, "domain", FAR, 0)
    theirs = exchanged(wavefunctions, "domain", CORE)
    both = (wavefunctions, theirs)
    own = call(own_kernel, block, (*both, rotation))[0]
    far_block, *sent = call(far_kernel, block + messages, (*both, far, own))
    parts = across(sent, 0, (0, 2))
    cut = states * 17 // 32
    outs = [shape(count, width, dtype=BF16) for count in (cut, states - cut)]
    top, bottom = call(functools.partial(pieces_kernel, 0), outs, (near, far), after=(far_block,), scratch=semaphore)
    top, bottom = exchanged(top, "domain", FAR, 0), exchanged(bottom, "domain", NEAR, 0)
    near_block = call(near_kernel, block, (*both, near))[0]
    operands = (*both, top, bottom, own, near_block, far_block)
    kept, *sent = call(first_late_kernel, block + messages, operands, after=parts, scratch=scratch)
    parts += across(sent, 0, (1, 3))
    first_total = call(first_sum_kernel, block, (kept, *parts))[0]

    later, _ = lax.optimization_barrier((rotation, first_total))
    near, far = exchanged(later, "domain", NEAR, CORE), exchanged(later, "domain", FAR, CORE)
    operator = operator(later)
    cut = states * 13 // 32
    outs = [shape(states - cut, width, dtype=BF16), shape(cut, width, dtype=BF16)]
    after = operator[:1]
    bottom = call(functools.partial(part_kernel, cut, CORE), outs[:1], (far,), after=after, scratch=semaphore)[0]
    top = call(functools.partial(part_kernel, 0, CORE), outs[1:], (near,), after=(bottom,), scratch=semaphore)[0]
    bottom, top = exchanged(bottom, "domain", NEAR, CORE), exchanged(top, "domain", FAR, CORE)
    early = call(early_kernel, block * 2, (*both, near, far))
    lower = call(lower_kernel, block, (*both, bottom), after=early[:1])[0]
    kept, *sent = call(late_kernel, block + messages, (*both, top, lower, own, *early), scratch=scratch)
    parts = across(sent, 1, range(chips))
    mine, others = call(sum_kernel, [shape(rows, width)] * 2, (first_total, kept, *parts))
    return mine, exchanged(others, "domain", CORE), operator


def rotate_any(wavefunctions, rotation):
    columns = lax.all_gather(rotation, "domain", axis=1, tiled=True)
    return lax.psum_scatter(dot(wavefunctions, columns), "band", scatter_dimension=1, tiled=True)


def faces_kernel(mine, other, assembled, pick, total, inward, outward):
    own, width = mine.shape
    columns = 2 * width
    first = core() == 0
    for side, half in enumerate((jnp.where(first, mine[...], other[...]), jnp.where(first, other[...], mine[...]))):
        total[:, side * width : (side + 1) * width] = half
    high, low = split(total[...])
    faces = dot(pick[...], high).astype(BF16)
    onward = (dot(assembled[own:, :own], high) + dot(assembled[own:, :own], low)).astype(BF16)
    corner = assembled[own:, own:]

    def store(forward, backward):
        forward[:, :columns] = onward
        forward[:, columns:] = corner
        backward[:, :columns] = faces
        backward[:, columns:] = corner

    pl.when(first)(lambda: store(inward, outward))
    pl.when(jnp.logical_not(first))(lambda: store(outward, inward))


def inner_kernel(total, assembled, pick, out, faces):
    own, columns = total.shape
    high, low = split(total[...])
    inner = assembled[:own, :own]
    out[...] = dot(inner, high) + dot(inner, low)
    faces[:, :columns] = dot(pick[...], high).astype(BF16)
    faces[:, columns:] = dot(pick[...], low).astype(BF16)


def final_kernel(inner, faces, assembled, spread, inward, outward, out):
    own, columns = inner.shape
    first = core() == 0
    incoming = jnp.where(first, inward[:, :columns], outward[:, :columns])
    back = jnp.where(first, outward[...], inward[...])
    extra = dot(back[:, columns:], faces[...])
    high, low = split(back[:, :columns].astype(F32) + extra[:, :columns] + extra[:, columns:])
    matrix = jnp.concatenate([assembled[:own, own:], spread[...], spread[...]], 1)
    out[...] = inner[...] + dot(matrix, jnp.concatenate([incoming, high, low], 0))


def finish_square(mine, other, operator):
    assembled, pick, spread = operator
    rows, width = mine.shape
    shared, columns = pick.shape[0], 2 * width
    outs = [shape(rows, columns)] + [shape(shared, columns + shared, dtype=BF16)] * 2
    total, inward, outward = call(faces_kernel, outs, (mine, other, assembled, pick))
    across = [(place, place + 1) for place in range(CORE, lax.axis_size("domain") - 1, 2)]
    outward = lax.ppermute(outward, "domain", across + [(target, source) for source, target in across])
    inward = exchanged(inward, "domain", CORE)
    outs = [shape(rows, columns), shape(shared, 2 * columns, dtype=BF16)]
    inner, faces = call(inner_kernel, outs, (total, assembled, pick))
    return call(final_kernel, outs[:1], (inner, faces, assembled, spread, inward, outward))[0]


def finish_any(rotated, cell_matrices, cell_nodes, face_map):
    own = rotated.shape[0]
    assembled, pick, returned = assemble_any(cell_matrices, cell_nodes, face_map, own)
    rotated = rotated.astype(BF16).astype(assembled.dtype)
    incoming = shifted(dot(pick, rotated).astype(BF16), "domain", -1).astype(assembled.dtype)
    back = shifted(dot(assembled[own:, :own], rotated), "domain", 1)
    inner = dot(assembled[:own, :own], rotated) + dot(returned, rotated) + dot(assembled[:own, own:], incoming)
    return inner + dot(pick.T.astype(F32), back)


def assemble_any(cell_matrices, cell_nodes, face_map, own):
    cells = cell_nodes.shape[0]
    extent = own + face_map.shape[0]
    held = BF16 if cells == 1 else F32
    places = jax.nn.one_hot(cell_nodes, extent, dtype=held)
    assembled = jnp.zeros((extent, extent), F32)
    for cell in range(cells):
        rows = dot(places[cell].T, cell_matrices[cell].astype(held)).astype(held)
        assembled = assembled + dot(rows, places[cell])
    assembled = assembled.astype(held)
    pick = jax.nn.one_hot(face_map, own, dtype=held)
    corner = shifted(assembled[own:, own:], "domain", 1)
    returned = dot(dot(pick.T, corner).astype(held), pick).astype(held)
    return assembled, pick, returned


def assemble_kernel(matrix, nodes, faces, assembled, pick, spread):
    extent = assembled.shape[0]
    places = jnp.where(lax.broadcasted_iota(jnp.int32, (extent, extent), 0) == nodes[...], 1.0, 0.0).astype(BF16)
    rows = dot(places, matrix[0]).astype(BF16)
    whole = lax.dot_general(rows, places, (((1,), (1,)), ((), ())), preferred_element_type=F32)
    assembled[...] = whole.astype(BF16)
    chosen = jnp.where(lax.broadcasted_iota(jnp.int32, spread.shape, 0) == faces[...], 1.0, 0.0)
    spread[...] = chosen.astype(BF16)
    pick[...] = chosen.T.astype(BF16)


def assemble(cell_matrices, cell_nodes, face_map, own, after):
    shared = face_map.shape[0]
    outs = [(own + shared, own + shared), (shared, own), (own, shared)]
    operands = (cell_matrices, cell_nodes, face_map.reshape(1, shared))
    return call(assemble_kernel, [shape(*dims, dtype=BF16) for dims in outs], operands, after=(after,))


def local(wavefunctions, rotation, cell_matrices, cell_nodes, face_map):
    chips = lax.axis_size("domain") // 2
    if chips == FAR and chips == lax.axis_size("band") and cell_nodes.shape[0] == 1:
        operator = functools.partial(assemble, cell_matrices, cell_nodes, face_map, wavefunctions.shape[0])
        return finish_square(*rotate_square(wavefunctions, rotation, operator))
    return finish_any(rotate_any(wavefunctions, rotation), cell_matrices, cell_nodes, face_map)


def solution(mesh):
    in_specs = (
        P("domain", "band"),
        P("band", "domain"),
        P("domain", None, None),
        P("domain", None),
        P("domain"),
    )
    out_specs = P("domain", "band")
    return jax.shard_map(local, mesh=mesh, in_specs=in_specs, out_specs=out_specs, check_vma=False)
```

```python
import functools

import jax
import jax.numpy as jnp
from jax import lax
from jax.experimental import pallas as pl
from jax.experimental.pallas import tpu as pltpu
from jax.sharding import PartitionSpec as P

CORE, NEAR, FAR = 1, 2, 4
VMEM = pl.BlockSpec(memory_space=pltpu.VMEM)
ANY = pl.BlockSpec(memory_space=pl.ANY)
F32, BF16 = jnp.float32, jnp.bfloat16


def dot(left, right):
    precision = lax.Precision.HIGHEST if left.dtype == F32 else None
    return jnp.dot(left, right, precision=precision, preferred_element_type=F32)


def split(value):
    high = value.astype(BF16)
    return high, (value - high.astype(F32)).astype(BF16)


def shifted(value, axis, steps):
    count = lax.axis_size(axis)
    leading, last = (max(0, -steps), min(count, count - steps))
    return lax.ppermute(value, axis, [(source, source + steps) for source in range(leading, last)])


def exchanged(value, axis, mask, core=None):
    sources = range(lax.axis_size(axis))
    return lax.ppermute(value, axis, [(source, source ^ mask) for source in sources if core in (None, source & CORE)])


def call(kernel, outs, operands, after=(), spaces=None, scratch=()):
    after = tuple(after)
    count = len(operands)

    def body(*refs):
        kernel(*refs[:count], *refs[count + len(after) :])

    return pl.pallas_call(
        body,
        out_shape=outs,
        in_specs=[pl.BlockSpec(memory_space=space) for space in spaces or [pltpu.VMEM] * count] + [ANY] * len(after),
        out_specs=[VMEM] * len(outs),
        scratch_shapes=list(scratch),
        cost_estimate=pl.CostEstimate(flops=0, bytes_accessed=1024, transcendentals=0),
        compiler_params=pltpu.CompilerParams(vmem_limit_bytes=24 * 2**20),
    )(*operands, *after)


def shape(*dims, dtype=F32):
    return jax.ShapeDtypeStruct(dims, dtype)


def core():
    return lax.rem(lax.axis_index("domain"), 2)


def block_of_band():
    return lax.bitwise_xor(lax.div(lax.axis_index("domain"), 2), lax.axis_index("band"))


def pieces_kernel(one, far, near, top, bottom, done):
    cut, rest = top.shape[0], bottom.shape[0]

    @pl.when(core() == one)
    def _():
        copies = [
            pltpu.make_async_copy(near.at[pl.ds(0, cut)], top, done.at[0]),
            pltpu.make_async_copy(far.at[pl.ds(cut, rest)], bottom, done.at[1]),
        ]
        for copy in copies:
            copy.start()
        for copy in copies:
            copy.wait()


def own_kernel(mine, theirs, own, block):
    rows = mine.shape[0]
    for side, states in enumerate((mine, theirs)):
        block[side * rows : (side + 1) * rows] = jnp.dot(states[...], own[...], preferred_element_type=F32)


def early_kernel(mine, theirs, near_even, far_even, near_odd, far_odd, near_block, far_block):
    rows, width = mine.shape[0], near_even.shape[1]
    first = core() == 0
    near, far = jnp.where(first, near_even[...], near_odd[...]), jnp.where(first, far_even[...], far_odd[...])
    wide = jnp.concatenate([near, far], 1)
    for side, states in enumerate((mine, theirs)):
        result = jnp.dot(states[...], wide, preferred_element_type=F32)
        near_block[side * rows : (side + 1) * rows] = result[:, :width]
        far_block[side * rows : (side + 1) * rows] = result[:, width:]


def late_kernel(mine, theirs, top_even, bottom_even, top_odd, bottom_odd, own, near, far, kept, *refs):
    sent, last = refs[:-1], refs[-1]
    rows = mine.shape[0]

    def multiply(top, bottom):
        cut = top.shape[0]
        for side, states in enumerate((mine, theirs)):
            result = jnp.dot(states[:, :cut], top[...], preferred_element_type=F32)
            last[side * rows : (side + 1) * rows] = result + jnp.dot(states[:, cut:], bottom[...], preferred_element_type=F32)

    pl.when(core() == 0)(lambda: multiply(top_even, bottom_even))
    pl.when(core() != 0)(lambda: multiply(top_odd, bottom_odd))
    where = block_of_band()

    def store(out, slot, block):
        @pl.when(slot == lax.bitwise_xor(where, mask))
        def _():
            out[...] = block[...].astype(out.dtype)

    for mask, out in enumerate((kept, *sent)):
        for slot, block in enumerate((own, near, far, last)):
            store(out, slot, block)


def sum_kernel(kept, *refs):
    parts, (mine, theirs) = refs[:-2], refs[-2:]
    value = kept[...]
    for part in parts:
        value = value + part[...].astype(F32)
    rows = mine.shape[0]
    mine[...] = value[:rows]
    theirs[...] = value[rows:]


def rotate_square(wavefunctions, rotation, operator):
    bands, chips = lax.axis_size("band"), lax.axis_size("domain") // 2
    rows, states = wavefunctions.shape
    width = rotation.shape[1]
    received = [exchanged(rotation, "domain", NEAR, 0), exchanged(rotation, "domain", FAR, 0)]
    theirs = exchanged(wavefunctions, "domain", CORE)
    block = [shape(2 * rows, width)]
    own = call(own_kernel, block, (wavefunctions, theirs, rotation))[0]
    operator = operator(own)
    later, _ = lax.optimization_barrier((rotation, operator[0]))
    received += [exchanged(later, "domain", NEAR, CORE), exchanged(later, "domain", FAR, CORE)]
    passed, previous = [], []
    for one, share in ((0, 21), (CORE, 18)):
        cut = states * share // 32
        outs = [shape(count, width, dtype=BF16) for count in (cut, states - cut)]
        pair = received[2 * one : 2 * one + 2][::-1]
        kernel = functools.partial(pieces_kernel, one)
        top, bottom = call(kernel, outs, pair, after=previous, scratch=[pltpu.SemaphoreType.DMA((2,))])
        previous = [bottom]
        passed += [exchanged(top, "domain", FAR, one), exchanged(bottom, "domain", NEAR, one)]
    early = call(early_kernel, block * 2, (wavefunctions, theirs, *received))
    outs = block + [shape(2 * rows, width, dtype=BF16)] * (bands - 1)
    scratch = [pltpu.VMEM((2 * rows, width), F32)]
    kept, *sent = call(late_kernel, outs, (wavefunctions, theirs, *passed, own, *early), scratch=scratch)
    parts = [exchanged(sent[mask - 1], "band", mask) for mask in (1, *reversed(range(2, bands)))]
    mine, others = call(sum_kernel, [shape(rows, width)] * 2, (kept, *parts))
    return mine, exchanged(others, "domain", CORE), operator


def rotate_any(wavefunctions, rotation):
    columns = lax.all_gather(rotation, "domain", axis=1, tiled=True)
    return lax.psum_scatter(dot(wavefunctions, columns), "band", scatter_dimension=1, tiled=True)


def faces_kernel(mine, other, assembled, pick, total, inward, outward):
    own, width = mine.shape
    columns = 2 * width
    first = core() == 0
    for side, half in enumerate((jnp.where(first, mine[...], other[...]), jnp.where(first, other[...], mine[...]))):
        total[:, side * width : (side + 1) * width] = half
    high, low = split(total[...])
    faces = dot(pick[...], high).astype(BF16)
    onward = (dot(assembled[own:, :own], high) + dot(assembled[own:, :own], low)).astype(BF16)
    corner = assembled[own:, own:]

    def store(forward, backward):
        forward[:, :columns] = onward
        forward[:, columns:] = corner
        backward[:, :columns] = faces
        backward[:, columns:] = corner

    pl.when(first)(lambda: store(inward, outward))
    pl.when(jnp.logical_not(first))(lambda: store(outward, inward))


def inner_kernel(total, assembled, pick, out, faces):
    own, columns = total.shape
    high, low = split(total[...])
    inner = assembled[:own, :own]
    out[...] = dot(inner, high) + dot(inner, low)
    faces[:, :columns] = dot(pick[...], high).astype(BF16)
    faces[:, columns:] = dot(pick[...], low).astype(BF16)


def final_kernel(inner, faces, assembled, spread, inward, one_hop, two_hops, out):
    own, columns = inner.shape
    domain, count = lax.axis_index("domain"), lax.axis_size("domain")
    first = core() == 0
    outward = jnp.where(lax.div(domain + 1, 2) == count // 4, two_hops[...], one_hop[...])
    outward = jnp.where((domain == 0) | (domain == count - 1), jnp.zeros_like(outward), outward)
    incoming = jnp.where(first, inward[:, :columns], outward[:, :columns])
    back = jnp.where(first, outward, inward[...])
    extra = dot(back[:, columns:], faces[...])
    high, low = split(back[:, :columns].astype(F32) + extra[:, :columns] + extra[:, columns:])
    matrix = jnp.concatenate([assembled[:own, own:], spread[...], spread[...]], 1)
    out[...] = inner[...] + dot(matrix, jnp.concatenate([incoming, high, low], 0))


def finish_square(mine, other, operator):
    assembled, pick, spread = operator
    rows, width = mine.shape
    shared, columns = pick.shape[0], 2 * width
    outs = [shape(rows, columns)] + [shape(shared, columns + shared, dtype=BF16)] * 2
    total, inward, outward = call(faces_kernel, outs, (mine, other, assembled, pick))
    outward = [exchanged(outward, "domain", mask) for mask in (CORE | NEAR, CORE | NEAR | FAR)]
    inward = exchanged(inward, "domain", CORE)
    outs = [shape(rows, columns), shape(shared, 2 * columns, dtype=BF16)]
    inner, faces = call(inner_kernel, outs, (total, assembled, pick))
    return call(final_kernel, outs[:1], (inner, faces, assembled, spread, inward, *outward))[0]


def finish_any(rotated, cell_matrices, cell_nodes, face_map):
    own = rotated.shape[0]
    assembled, pick, returned = assemble_any(cell_matrices, cell_nodes, face_map, own)
    rotated = rotated.astype(BF16).astype(assembled.dtype)
    incoming = shifted(dot(pick, rotated).astype(BF16), "domain", -1).astype(assembled.dtype)
    back = shifted(dot(assembled[own:, :own], rotated), "domain", 1)
    inner = dot(assembled[:own, :own], rotated) + dot(returned, rotated) + dot(assembled[:own, own:], incoming)
    return inner + dot(pick.T.astype(F32), back)


def assemble_any(cell_matrices, cell_nodes, face_map, own):
    cells = cell_nodes.shape[0]
    extent = own + face_map.shape[0]
    held = BF16 if cells == 1 else F32
    places = jax.nn.one_hot(cell_nodes, extent, dtype=held)
    assembled = jnp.zeros((extent, extent), F32)
    for cell in range(cells):
        rows = dot(places[cell].T, cell_matrices[cell].astype(held)).astype(held)
        assembled = assembled + dot(rows, places[cell])
    assembled = assembled.astype(held)
    pick = jax.nn.one_hot(face_map, own, dtype=held)
    corner = shifted(assembled[own:, own:], "domain", 1)
    returned = dot(dot(pick.T, corner).astype(held), pick).astype(held)
    return assembled, pick, returned


def assemble_kernel(matrix, nodes, faces, assembled, pick, spread):
    extent = assembled.shape[0]
    places = jnp.where(lax.broadcasted_iota(jnp.int32, (extent, extent), 0) == nodes[...], 1.0, 0.0).astype(BF16)
    rows = dot(places, matrix[0]).astype(BF16)
    whole = lax.dot_general(rows, places, (((1,), (1,)), ((), ())), preferred_element_type=F32)
    assembled[...] = whole.astype(BF16)
    chosen = jnp.where(lax.broadcasted_iota(jnp.int32, spread.shape, 0) == faces[...], 1.0, 0.0)
    spread[...] = chosen.astype(BF16)
    pick[...] = chosen.T.astype(BF16)


def assemble(cell_matrices, cell_nodes, face_map, own, after):
    shared = face_map.shape[0]
    outs = [(own + shared, own + shared), (shared, own), (own, shared)]
    operands = (cell_matrices, cell_nodes, face_map.reshape(1, shared))
    return call(assemble_kernel, [shape(*dims, dtype=BF16) for dims in outs], operands, after=(after,))


def local(wavefunctions, rotation, cell_matrices, cell_nodes, face_map):
    chips = lax.axis_size("domain") // 2
    if chips == FAR and chips == lax.axis_size("band") and cell_nodes.shape[0] == 1:
        operator = functools.partial(assemble, cell_matrices, cell_nodes, face_map, wavefunctions.shape[0])
        return finish_square(*rotate_square(wavefunctions, rotation, operator))
    return finish_any(rotate_any(wavefunctions, rotation), cell_matrices, cell_nodes, face_map)


def solution(mesh):
    in_specs = (
        P("domain", "band"),
        P("band", "domain"),
        P("domain", None, None),
        P("domain", None),
        P("domain"),
    )
    out_specs = P("domain", "band")
    return jax.shard_map(local, mesh=mesh, in_specs=in_specs, out_specs=out_specs, check_vma=False)
```

```python
import functools

import jax
import jax.numpy as jnp
from jax import lax
from jax.experimental import pallas as pl
from jax.experimental.pallas import tpu as pltpu
from jax.sharding import PartitionSpec as P

CORE, NEAR, FAR = 1, 2, 4
VMEM = pl.BlockSpec(memory_space=pltpu.VMEM)
ANY = pl.BlockSpec(memory_space=pl.ANY)
F32, BF16 = jnp.float32, jnp.bfloat16


def dot(left, right):
    precision = lax.Precision.HIGHEST if left.dtype == F32 else None
    return jnp.dot(left, right, precision=precision, preferred_element_type=F32)


def split(value):
    high = value.astype(BF16)
    return high, (value - high.astype(F32)).astype(BF16)


def shifted(value, axis, steps):
    count = lax.axis_size(axis)
    leading, last = (max(0, -steps), min(count, count - steps))
    return lax.ppermute(value, axis, [(source, source + steps) for source in range(leading, last)])


def exchanged(value, axis, mask, core=None):
    sources = range(lax.axis_size(axis))
    return lax.ppermute(value, axis, [(source, source ^ mask) for source in sources if core in (None, source & CORE)])


def call(kernel, outs, operands, after=(), spaces=None, scratch=()):
    after = tuple(after)
    count = len(operands)

    def body(*refs):
        kernel(*refs[:count], *refs[count + len(after) :])

    return pl.pallas_call(
        body,
        out_shape=outs,
        in_specs=[pl.BlockSpec(memory_space=space) for space in spaces or [pltpu.VMEM] * count] + [ANY] * len(after),
        out_specs=[VMEM] * len(outs),
        scratch_shapes=list(scratch),
        cost_estimate=pl.CostEstimate(flops=0, bytes_accessed=1024, transcendentals=0),
        compiler_params=pltpu.CompilerParams(vmem_limit_bytes=24 * 2**20),
    )(*operands, *after)


def shape(*dims, dtype=F32):
    return jax.ShapeDtypeStruct(dims, dtype)


def core():
    return lax.rem(lax.axis_index("domain"), 2)


def block_of_band():
    return lax.bitwise_xor(lax.div(lax.axis_index("domain"), 2), lax.axis_index("band"))


def pieces_kernel(one, far, near, top, bottom, done):
    cut, rest = top.shape[0], bottom.shape[0]

    @pl.when(core() == one)
    def _():
        copies = [
            pltpu.make_async_copy(near.at[pl.ds(0, cut)], top, done.at[0]),
            pltpu.make_async_copy(far.at[pl.ds(cut, rest)], bottom, done.at[1]),
        ]
        for copy in copies:
            copy.start()
        for copy in copies:
            copy.wait()


def own_kernel(mine, theirs, own, block):
    rows = mine.shape[0]
    for side, states in enumerate((mine, theirs)):
        block[side * rows : (side + 1) * rows] = jnp.dot(states[...], own[...], preferred_element_type=F32)


def early_kernel(mine, theirs, near_even, far_even, near_odd, far_odd, near_block, far_block):
    rows, width = mine.shape[0], near_even.shape[1]
    first = core() == 0
    near, far = jnp.where(first, near_even[...], near_odd[...]), jnp.where(first, far_even[...], far_odd[...])
    wide = jnp.concatenate([near, far], 1)
    for side, states in enumerate((mine, theirs)):
        result = jnp.dot(states[...], wide, preferred_element_type=F32)
        near_block[side * rows : (side + 1) * rows] = result[:, :width]
        far_block[side * rows : (side + 1) * rows] = result[:, width:]


def late_kernel(mine, theirs, top_even, bottom_even, top_odd, bottom_odd, own, near, far, kept, *refs):
    sent, last = refs[:-1], refs[-1]
    rows = mine.shape[0]

    def multiply(top, bottom):
        cut = top.shape[0]
        for side, states in enumerate((mine, theirs)):
            result = jnp.dot(states[:, :cut], top[...], preferred_element_type=F32)
            last[side * rows : (side + 1) * rows] = result + jnp.dot(states[:, cut:], bottom[...], preferred_element_type=F32)

    pl.when(core() == 0)(lambda: multiply(top_even, bottom_even))
    pl.when(core() != 0)(lambda: multiply(top_odd, bottom_odd))
    where = block_of_band()

    def store(out, slot, block):
        @pl.when(slot == lax.bitwise_xor(where, mask))
        def _():
            out[...] = block[...].astype(out.dtype)

    for mask, out in enumerate((kept, *sent)):
        for slot, block in enumerate((own, near, far, last)):
            store(out, slot, block)


def sum_kernel(kept, *refs):
    parts, (mine, theirs) = refs[:-2], refs[-2:]
    value = kept[...]
    for part in parts:
        value = value + part[...].astype(F32)
    rows = mine.shape[0]
    mine[...] = value[:rows]
    theirs[...] = value[rows:]


def rotate_square(wavefunctions, rotation, operator):
    bands, chips = lax.axis_size("band"), lax.axis_size("domain") // 2
    rows, states = wavefunctions.shape
    width = rotation.shape[1]
    received = [exchanged(rotation, "domain", NEAR, 0), exchanged(rotation, "domain", FAR, 0)]
    theirs = exchanged(wavefunctions, "domain", CORE)
    block = [shape(2 * rows, width)]
    own = call(own_kernel, block, (wavefunctions, theirs, rotation))[0]
    operator = operator(own)
    later, _ = lax.optimization_barrier((rotation, operator[0]))
    received += [exchanged(later, "domain", NEAR, CORE), exchanged(later, "domain", FAR, CORE)]
    passed, previous = [], []
    for one, share in ((0, 21), (CORE, 18)):
        cut = states * share // 32
        outs = [shape(count, width, dtype=BF16) for count in (cut, states - cut)]
        pair = received[2 * one : 2 * one + 2][::-1]
        kernel = functools.partial(pieces_kernel, one)
        top, bottom = call(kernel, outs, pair, after=previous, scratch=[pltpu.SemaphoreType.DMA((2,))])
        previous = [bottom]
        passed += [exchanged(top, "domain", FAR, one), exchanged(bottom, "domain", NEAR, one)]
    early = call(early_kernel, block * 2, (wavefunctions, theirs, *received))
    outs = block + [shape(2 * rows, width, dtype=BF16)] * (bands - 1)
    scratch = [pltpu.VMEM((2 * rows, width), F32)]
    kept, *sent = call(late_kernel, outs, (wavefunctions, theirs, *passed, own, *early), scratch=scratch)
    parts = [exchanged(sent[mask - 1], "band", mask) for mask in (1, *reversed(range(2, bands)))]
    mine, others = call(sum_kernel, [shape(rows, width)] * 2, (kept, *parts))
    return mine, exchanged(others, "domain", CORE), operator


def rotate_any(wavefunctions, rotation):
    columns = lax.all_gather(rotation, "domain", axis=1, tiled=True)
    return lax.psum_scatter(dot(wavefunctions, columns), "band", scatter_dimension=1, tiled=True)


def faces_kernel(mine, other, assembled, pick, total, faces, onward):
    own, width = mine.shape
    columns = 2 * width
    first = core() == 0
    for side, half in enumerate((jnp.where(first, mine[...], other[...]), jnp.where(first, other[...], mine[...]))):
        total[:, side * width : (side + 1) * width] = half
    high, low = split(total[...])
    faces[...] = dot(pick[...], high).astype(BF16)
    onward[:, :columns] = (dot(assembled[own:, :own], high) + dot(assembled[own:, :own], low)).astype(BF16)
    onward[:, columns:] = assembled[own:, own:]


def inner_kernel(total, assembled, pick, out, faces):
    own, columns = total.shape
    high, low = split(total[...])
    inner = assembled[:own, :own]
    out[...] = dot(inner, high) + dot(inner, low)
    faces[:, :columns] = dot(pick[...], high).astype(BF16)
    faces[:, columns:] = dot(pick[...], low).astype(BF16)


def final_kernel(inner, faces, assembled, spread, incoming, back, out):
    own, columns = inner.shape
    domain, count = lax.axis_index("domain"), lax.axis_size("domain")
    incoming = jnp.where(domain == count - 1, jnp.zeros(incoming.shape, BF16), incoming[...])
    back = jnp.where(domain == 0, jnp.zeros(back.shape, BF16), back[...])
    extra = dot(back[:, columns:], faces[...])
    high, low = split(back[:, :columns].astype(F32) + extra[:, :columns] + extra[:, columns:])
    matrix = jnp.concatenate([assembled[:own, own:], spread[...], spread[...]], 1)
    out[...] = inner[...] + dot(matrix, jnp.concatenate([incoming, high, low], 0))


def rotated(value, axis, steps):
    count = lax.axis_size(axis)
    return lax.ppermute(value, axis, [(source, (source + steps) % count) for source in range(count)])


def finish_square(mine, other, operator):
    assembled, pick, spread = operator
    rows, width = mine.shape
    shared, columns = pick.shape[0], 2 * width
    outs = [shape(rows, columns), shape(shared, columns, dtype=BF16), shape(shared, columns + shared, dtype=BF16)]
    total, faces, onward = call(faces_kernel, outs, (mine, other, assembled, pick))
    back, incoming = rotated(onward, "domain", 1), rotated(faces, "domain", -1)
    outs = [shape(rows, columns), shape(shared, 2 * columns, dtype=BF16)]
    inner, faces = call(inner_kernel, outs, (total, assembled, pick))
    return call(final_kernel, outs[:1], (inner, faces, assembled, spread, incoming, back))[0]


def finish_any(rotated, cell_matrices, cell_nodes, face_map):
    own = rotated.shape[0]
    assembled, pick, returned = assemble_any(cell_matrices, cell_nodes, face_map, own)
    rotated = rotated.astype(BF16).astype(assembled.dtype)
    incoming = shifted(dot(pick, rotated).astype(BF16), "domain", -1).astype(assembled.dtype)
    back = shifted(dot(assembled[own:, :own], rotated), "domain", 1)
    inner = dot(assembled[:own, :own], rotated) + dot(returned, rotated) + dot(assembled[:own, own:], incoming)
    return inner + dot(pick.T.astype(F32), back)


def assemble_any(cell_matrices, cell_nodes, face_map, own):
    cells = cell_nodes.shape[0]
    extent = own + face_map.shape[0]
    held = BF16 if cells == 1 else F32
    places = jax.nn.one_hot(cell_nodes, extent, dtype=held)
    assembled = jnp.zeros((extent, extent), F32)
    for cell in range(cells):
        rows = dot(places[cell].T, cell_matrices[cell].astype(held)).astype(held)
        assembled = assembled + dot(rows, places[cell])
    assembled = assembled.astype(held)
    pick = jax.nn.one_hot(face_map, own, dtype=held)
    corner = shifted(assembled[own:, own:], "domain", 1)
    returned = dot(dot(pick.T, corner).astype(held), pick).astype(held)
    return assembled, pick, returned


def assemble_kernel(matrix, nodes, faces, assembled, pick, spread):
    extent = assembled.shape[0]
    places = jnp.where(lax.broadcasted_iota(jnp.int32, (extent, extent), 0) == nodes[...], 1.0, 0.0).astype(BF16)
    rows = dot(places, matrix[0]).astype(BF16)
    whole = lax.dot_general(rows, places, (((1,), (1,)), ((), ())), preferred_element_type=F32)
    assembled[...] = whole.astype(BF16)
    chosen = jnp.where(lax.broadcasted_iota(jnp.int32, spread.shape, 0) == faces[...], 1.0, 0.0)
    spread[...] = chosen.astype(BF16)
    pick[...] = chosen.T.astype(BF16)


def assemble(cell_matrices, cell_nodes, face_map, own, after):
    shared = face_map.shape[0]
    outs = [(own + shared, own + shared), (shared, own), (own, shared)]
    operands = (cell_matrices, cell_nodes, face_map.reshape(1, shared))
    return call(assemble_kernel, [shape(*dims, dtype=BF16) for dims in outs], operands, after=(after,))


def local(wavefunctions, rotation, cell_matrices, cell_nodes, face_map):
    chips = lax.axis_size("domain") // 2
    if chips == FAR and chips == lax.axis_size("band") and cell_nodes.shape[0] == 1:
        operator = functools.partial(assemble, cell_matrices, cell_nodes, face_map, wavefunctions.shape[0])
        return finish_square(*rotate_square(wavefunctions, rotation, operator))
    return finish_any(rotate_any(wavefunctions, rotation), cell_matrices, cell_nodes, face_map)


def solution(mesh):
    in_specs = (
        P("domain", "band"),
        P("band", "domain"),
        P("domain", None, None),
        P("domain", None),
        P("domain"),
    )
    out_specs = P("domain", "band")
    return jax.shard_map(local, mesh=mesh, in_specs=in_specs, out_specs=out_specs, check_vma=False)
```

```python
import functools

import jax
import jax.numpy as jnp
from jax import lax
from jax.experimental import pallas as pl
from jax.experimental.pallas import tpu as pltpu
from jax.sharding import PartitionSpec as P

CORE, NEAR, FAR = 1, 2, 4
VMEM = pl.BlockSpec(memory_space=pltpu.VMEM)
ANY = pl.BlockSpec(memory_space=pl.ANY)
F32, BF16 = jnp.float32, jnp.bfloat16


def dot(left, right):
    precision = lax.Precision.HIGHEST if left.dtype == F32 else None
    return jnp.dot(left, right, precision=precision, preferred_element_type=F32)


def split(value):
    high = value.astype(BF16)
    return high, (value - high.astype(F32)).astype(BF16)


def shifted(value, axis, steps):
    count = lax.axis_size(axis)
    leading, last = (max(0, -steps), min(count, count - steps))
    return lax.ppermute(value, axis, [(source, source + steps) for source in range(leading, last)])


def exchanged(value, axis, mask, core=None):
    sources = range(lax.axis_size(axis))
    return lax.ppermute(value, axis, [(source, source ^ mask) for source in sources if core in (None, source & CORE)])


def call(kernel, outs, operands, after=(), spaces=None, scratch=()):
    after = tuple(after)
    count = len(operands)

    def body(*refs):
        kernel(*refs[:count], *refs[count + len(after) :])

    return pl.pallas_call(
        body,
        out_shape=outs,
        in_specs=[pl.BlockSpec(memory_space=space) for space in spaces or [pltpu.VMEM] * count] + [ANY] * len(after),
        out_specs=[VMEM] * len(outs),
        scratch_shapes=list(scratch),
        cost_estimate=pl.CostEstimate(flops=0, bytes_accessed=1024, transcendentals=0),
        compiler_params=pltpu.CompilerParams(vmem_limit_bytes=24 * 2**20),
    )(*operands, *after)


def shape(*dims, dtype=F32):
    return jax.ShapeDtypeStruct(dims, dtype)


def core():
    return lax.rem(lax.axis_index("domain"), 2)


def block_of_band():
    return lax.bitwise_xor(lax.div(lax.axis_index("domain"), 2), lax.axis_index("band"))


def pieces_kernel(one, far, near, top, bottom, done):
    cut, rest = top.shape[0], bottom.shape[0]

    @pl.when(core() == one)
    def _():
        copies = [
            pltpu.make_async_copy(near.at[pl.ds(0, cut)], top, done.at[0]),
            pltpu.make_async_copy(far.at[pl.ds(cut, rest)], bottom, done.at[1]),
        ]
        for copy in copies:
            copy.start()
        for copy in copies:
            copy.wait()


def own_kernel(mine, theirs, own, block):
    rows = mine.shape[0]
    for side, states in enumerate((mine, theirs)):
        block[side * rows : (side + 1) * rows] = jnp.dot(states[...], own[...], preferred_element_type=F32)


def early_kernel(mine, theirs, near_even, far_even, near_odd, far_odd, near_block, far_block):
    rows, width = mine.shape[0], near_even.shape[1]
    first = core() == 0
    near, far = jnp.where(first, near_even[...], near_odd[...]), jnp.where(first, far_even[...], far_odd[...])
    wide = jnp.concatenate([near, far], 1)
    for side, states in enumerate((mine, theirs)):
        result = jnp.dot(states[...], wide, preferred_element_type=F32)
        near_block[side * rows : (side + 1) * rows] = result[:, :width]
        far_block[side * rows : (side + 1) * rows] = result[:, width:]


def upper_kernel(mine, theirs, top_even, top_odd, block):
    rows = mine.shape[0]

    def multiply(top):
        for side, states in enumerate((mine, theirs)):
            result = jnp.dot(states[:, : top.shape[0]], top[...], preferred_element_type=F32)
            block[side * rows : (side + 1) * rows] = result

    pl.when(core() == 0)(lambda: multiply(top_even))
    pl.when(core() != 0)(lambda: multiply(top_odd))


def late_kernel(mine, theirs, bottom_even, bottom_odd, upper, own, near, far, kept, *refs):
    sent, last = refs[:-1], refs[-1]
    rows = mine.shape[0]

    def multiply(bottom):
        start = mine.shape[1] - bottom.shape[0]
        for side, states in enumerate((mine, theirs)):
            span = slice(side * rows, (side + 1) * rows)
            last[span] = upper[span] + jnp.dot(states[:, start:], bottom[...], preferred_element_type=F32)

    pl.when(core() == 0)(lambda: multiply(bottom_even))
    pl.when(core() != 0)(lambda: multiply(bottom_odd))
    where = block_of_band()

    def store(out, slot, block):
        @pl.when(slot == lax.bitwise_xor(where, mask))
        def _():
            out[...] = block[...].astype(out.dtype)

    for mask, out in enumerate((kept, *sent)):
        for slot, block in enumerate((own, near, far, last)):
            store(out, slot, block)


def sum_kernel(kept, *refs):
    parts, (mine, theirs) = refs[:-2], refs[-2:]
    value = kept[...]
    for part in parts:
        value = value + part[...].astype(F32)
    rows = mine.shape[0]
    mine[...] = value[:rows]
    theirs[...] = value[rows:]


def rotate_square(wavefunctions, rotation, operator):
    bands, chips = lax.axis_size("band"), lax.axis_size("domain") // 2
    rows, states = wavefunctions.shape
    width = rotation.shape[1]
    received = [exchanged(rotation, "domain", NEAR, 0), exchanged(rotation, "domain", FAR, 0)]
    theirs = exchanged(wavefunctions, "domain", CORE)
    block = [shape(2 * rows, width)]
    own = call(own_kernel, block, (wavefunctions, theirs, rotation))[0]
    operator = operator(own)
    later, _ = lax.optimization_barrier((rotation, operator[0]))
    received += [exchanged(later, "domain", NEAR, CORE), exchanged(later, "domain", FAR, CORE)]
    passed, previous = [], []
    for one, share in ((0, 21), (CORE, 18)):
        cut = states * share // 32
        outs = [shape(count, width, dtype=BF16) for count in (cut, states - cut)]
        pair = received[2 * one : 2 * one + 2][::-1]
        kernel = functools.partial(pieces_kernel, one)
        top, bottom = call(kernel, outs, pair, after=previous, scratch=[pltpu.SemaphoreType.DMA((2,))])
        previous = [bottom]
        passed += [exchanged(top, "domain", FAR, one), exchanged(bottom, "domain", NEAR, one)]
    early = call(early_kernel, block * 2, (wavefunctions, theirs, *received))
    outs = block + [shape(2 * rows, width, dtype=BF16)] * (bands - 1)
    scratch = [pltpu.VMEM((2 * rows, width), F32)]
    upper = call(upper_kernel, block, (wavefunctions, theirs, *passed[::2]), after=early[:1])[0]
    operands = (wavefunctions, theirs, *passed[1::2], upper, own, *early)
    kept, *sent = call(late_kernel, outs, operands, scratch=scratch)
    parts = [exchanged(sent[mask - 1], "band", mask) for mask in (1, *reversed(range(2, bands)))]
    mine, others = call(sum_kernel, [shape(rows, width)] * 2, (kept, *parts))
    return mine, exchanged(others, "domain", CORE), operator


def rotate_any(wavefunctions, rotation):
    columns = lax.all_gather(rotation, "domain", axis=1, tiled=True)
    return lax.psum_scatter(dot(wavefunctions, columns), "band", scatter_dimension=1, tiled=True)


def faces_kernel(mine, other, assembled, pick, total, faces, onward):
    own, width = mine.shape
    columns = 2 * width
    first = core() == 0
    for side, half in enumerate((jnp.where(first, mine[...], other[...]), jnp.where(first, other[...], mine[...]))):
        total[:, side * width : (side + 1) * width] = half
    high, low = split(total[...])
    faces[...] = dot(pick[...], high).astype(BF16)
    onward[:, :columns] = (dot(assembled[own:, :own], high) + dot(assembled[own:, :own], low)).astype(BF16)
    onward[:, columns:] = assembled[own:, own:]


def inner_kernel(total, assembled, pick, out, faces):
    own, columns = total.shape
    high, low = split(total[...])
    inner = assembled[:own, :own]
    out[...] = dot(inner, high) + dot(inner, low)
    faces[:, :columns] = dot(pick[...], high).astype(BF16)
    faces[:, columns:] = dot(pick[...], low).astype(BF16)


def final_kernel(inner, faces, assembled, spread, incoming, back, out):
    own, columns = inner.shape
    domain, count = lax.axis_index("domain"), lax.axis_size("domain")
    incoming = jnp.where(domain == count - 1, jnp.zeros(incoming.shape, BF16), incoming[...])
    back = jnp.where(domain == 0, jnp.zeros(back.shape, BF16), back[...])
    extra = dot(back[:, columns:], faces[...])
    high, low = split(back[:, :columns].astype(F32) + extra[:, :columns] + extra[:, columns:])
    matrix = jnp.concatenate([assembled[:own, own:], spread[...], spread[...]], 1)
    out[...] = inner[...] + dot(matrix, jnp.concatenate([incoming, high, low], 0))


def rotated(value, axis, steps):
    count = lax.axis_size(axis)
    return lax.ppermute(value, axis, [(source, (source + steps) % count) for source in range(count)])


def finish_square(mine, other, operator):
    assembled, pick, spread = operator
    rows, width = mine.shape
    shared, columns = pick.shape[0], 2 * width
    outs = [shape(rows, columns), shape(shared, columns, dtype=BF16), shape(shared, columns + shared, dtype=BF16)]
    total, faces, onward = call(faces_kernel, outs, (mine, other, assembled, pick))
    back, incoming = rotated(onward, "domain", 1), rotated(faces, "domain", -1)
    outs = [shape(rows, columns), shape(shared, 2 * columns, dtype=BF16)]
    inner, faces = call(inner_kernel, outs, (total, assembled, pick))
    return call(final_kernel, outs[:1], (inner, faces, assembled, spread, incoming, back))[0]


def finish_any(rotated, cell_matrices, cell_nodes, face_map):
    own = rotated.shape[0]
    assembled, pick, returned = assemble_any(cell_matrices, cell_nodes, face_map, own)
    rotated = rotated.astype(BF16).astype(assembled.dtype)
    incoming = shifted(dot(pick, rotated).astype(BF16), "domain", -1).astype(assembled.dtype)
    back = shifted(dot(assembled[own:, :own], rotated), "domain", 1)
    inner = dot(assembled[:own, :own], rotated) + dot(returned, rotated) + dot(assembled[:own, own:], incoming)
    return inner + dot(pick.T.astype(F32), back)


def assemble_any(cell_matrices, cell_nodes, face_map, own):
    cells = cell_nodes.shape[0]
    extent = own + face_map.shape[0]
    held = BF16 if cells == 1 else F32
    places = jax.nn.one_hot(cell_nodes, extent, dtype=held)
    assembled = jnp.zeros((extent, extent), F32)
    for cell in range(cells):
        rows = dot(places[cell].T, cell_matrices[cell].astype(held)).astype(held)
        assembled = assembled + dot(rows, places[cell])
    assembled = assembled.astype(held)
    pick = jax.nn.one_hot(face_map, own, dtype=held)
    corner = shifted(assembled[own:, own:], "domain", 1)
    returned = dot(dot(pick.T, corner).astype(held), pick).astype(held)
    return assembled, pick, returned


def assemble_kernel(matrix, nodes, faces, assembled, pick, spread):
    extent = assembled.shape[0]
    places = jnp.where(lax.broadcasted_iota(jnp.int32, (extent, extent), 0) == nodes[...], 1.0, 0.0).astype(BF16)
    rows = dot(places, matrix[0]).astype(BF16)
    whole = lax.dot_general(rows, places, (((1,), (1,)), ((), ())), preferred_element_type=F32)
    assembled[...] = whole.astype(BF16)
    chosen = jnp.where(lax.broadcasted_iota(jnp.int32, spread.shape, 0) == faces[...], 1.0, 0.0)
    spread[...] = chosen.astype(BF16)
    pick[...] = chosen.T.astype(BF16)


def assemble(cell_matrices, cell_nodes, face_map, own, after):
    shared = face_map.shape[0]
    outs = [(own + shared, own + shared), (shared, own), (own, shared)]
    operands = (cell_matrices, cell_nodes, face_map.reshape(1, shared))
    return call(assemble_kernel, [shape(*dims, dtype=BF16) for dims in outs], operands, after=(after,))


def local(wavefunctions, rotation, cell_matrices, cell_nodes, face_map):
    chips = lax.axis_size("domain") // 2
    if chips == FAR and chips == lax.axis_size("band") and cell_nodes.shape[0] == 1:
        operator = functools.partial(assemble, cell_matrices, cell_nodes, face_map, wavefunctions.shape[0])
        return finish_square(*rotate_square(wavefunctions, rotation, operator))
    return finish_any(rotate_any(wavefunctions, rotation), cell_matrices, cell_nodes, face_map)


def solution(mesh):
    in_specs = (
        P("domain", "band"),
        P("band", "domain"),
        P("domain", None, None),
        P("domain", None),
        P("domain"),
    )
    out_specs = P("domain", "band")
    return jax.shard_map(local, mesh=mesh, in_specs=in_specs, out_specs=out_specs, check_vma=False)
```

```python
import functools

import jax
import jax.numpy as jnp
from jax import lax
from jax.experimental import pallas as pl
from jax.experimental.pallas import tpu as pltpu
from jax.sharding import PartitionSpec as P

CORE, NEAR, FAR = 1, 2, 4
VMEM = pl.BlockSpec(memory_space=pltpu.VMEM)
ANY = pl.BlockSpec(memory_space=pl.ANY)
F32, BF16 = jnp.float32, jnp.bfloat16


def dot(left, right):
    precision = lax.Precision.HIGHEST if left.dtype == F32 else None
    return jnp.dot(left, right, precision=precision, preferred_element_type=F32)


def split(value):
    high = value.astype(BF16)
    return high, (value - high.astype(F32)).astype(BF16)


def shifted(value, axis, steps):
    count = lax.axis_size(axis)
    leading, last = (max(0, -steps), min(count, count - steps))
    return lax.ppermute(value, axis, [(source, source + steps) for source in range(leading, last)])


def exchanged(value, axis, mask, core=None):
    sources = range(lax.axis_size(axis))
    return lax.ppermute(value, axis, [(source, source ^ mask) for source in sources if core in (None, source & CORE)])


def paired(value, mask, one):
    count, bands = lax.axis_size("domain"), lax.axis_size("band")
    pairs = []
    for place in range(count):
        for band in range(bands):
            partner = (place ^ mask, band) if place & CORE == one else (place, band ^ 1)
            pairs.append((place * bands + band, partner[0] * bands + partner[1]))
    return lax.ppermute(value, ("domain", "band"), pairs)


def call(kernel, outs, operands, after=(), spaces=None, scratch=()):
    after = tuple(after)
    count = len(operands)

    def body(*refs):
        kernel(*refs[:count], *refs[count + len(after) :])

    return pl.pallas_call(
        body,
        out_shape=outs,
        in_specs=[pl.BlockSpec(memory_space=space) for space in spaces or [pltpu.VMEM] * count] + [ANY] * len(after),
        out_specs=[VMEM] * len(outs),
        scratch_shapes=list(scratch),
        cost_estimate=pl.CostEstimate(flops=0, bytes_accessed=1024, transcendentals=0),
        compiler_params=pltpu.CompilerParams(vmem_limit_bytes=24 * 2**20),
    )(*operands, *after)


def shape(*dims, dtype=F32):
    return jax.ShapeDtypeStruct(dims, dtype)


def core():
    return lax.rem(lax.axis_index("domain"), 2)


def block_of_band():
    return lax.bitwise_xor(lax.div(lax.axis_index("domain"), 2), lax.axis_index("band"))


def pieces_kernel(one, far, near, top, bottom, done):
    cut, rest = top.shape[0], bottom.shape[0]

    @pl.when(core() == one)
    def _():
        copies = [
            pltpu.make_async_copy(near.at[pl.ds(0, cut)], top, done.at[0]),
            pltpu.make_async_copy(far.at[pl.ds(cut, rest)], bottom, done.at[1]),
        ]
        for copy in copies:
            copy.start()
        for copy in copies:
            copy.wait()


def own_kernel(mine, theirs, own, block):
    rows = mine.shape[0]
    for side, states in enumerate((mine, theirs)):
        block[side * rows : (side + 1) * rows] = jnp.dot(states[...], own[...], preferred_element_type=F32)


def early_kernel(mine, theirs, near_even, far_even, near_odd, far_odd, near_block, far_block):
    rows, width = mine.shape[0], near_even.shape[1]
    first = core() == 0
    near, far = jnp.where(first, near_even[...], near_odd[...]), jnp.where(first, far_even[...], far_odd[...])
    wide = jnp.concatenate([near, far], 1)
    for side, states in enumerate((mine, theirs)):
        result = jnp.dot(states[...], wide, preferred_element_type=F32)
        near_block[side * rows : (side + 1) * rows] = result[:, :width]
        far_block[side * rows : (side + 1) * rows] = result[:, width:]


def upper_kernel(mine, theirs, top_even, top_odd, block):
    rows = mine.shape[0]

    def multiply(top):
        for side, states in enumerate((mine, theirs)):
            result = jnp.dot(states[:, : top.shape[0]], top[...], preferred_element_type=F32)
            block[side * rows : (side + 1) * rows] = result

    pl.when(core() == 0)(lambda: multiply(top_even))
    pl.when(core() != 0)(lambda: multiply(top_odd))


def late_kernel(mine, theirs, bottom_even, bottom_odd, upper, own, near, far, kept, *refs):
    sent, last = refs[:-1], refs[-1]
    rows = mine.shape[0]

    def multiply(bottom):
        start = mine.shape[1] - bottom.shape[0]
        for side, states in enumerate((mine, theirs)):
            span = slice(side * rows, (side + 1) * rows)
            last[span] = upper[span] + jnp.dot(states[:, start:], bottom[...], preferred_element_type=F32)

    pl.when(core() == 0)(lambda: multiply(bottom_even))
    pl.when(core() != 0)(lambda: multiply(bottom_odd))
    where = block_of_band()

    def store(out, slot, block):
        @pl.when(slot == lax.bitwise_xor(where, mask))
        def _():
            out[...] = block[...].astype(out.dtype)

    for mask, out in enumerate((kept, *sent)):
        for slot, block in enumerate((own, near, far, last)):
            store(out, slot, block)


def sum_kernel(kept, *refs):
    parts, (mine, theirs) = refs[:-2], refs[-2:]
    value = kept[...]
    for part in parts:
        value = value + part[...].astype(F32)
    rows = mine.shape[0]
    mine[...] = value[:rows]
    theirs[...] = value[rows:]


def rotate_square(wavefunctions, rotation, operator):
    bands, chips = lax.axis_size("band"), lax.axis_size("domain") // 2
    rows, states = wavefunctions.shape
    width = rotation.shape[1]
    received = [paired(rotation, NEAR, 0), paired(rotation, FAR, 0)]
    theirs = exchanged(wavefunctions, "domain", CORE)
    block = [shape(2 * rows, width)]
    own = call(own_kernel, block, (wavefunctions, theirs, rotation))[0]
    operator = operator(own)
    later, _ = lax.optimization_barrier((rotation, operator[0]))
    received += [exchanged(later, "domain", NEAR, CORE), exchanged(later, "domain", FAR, CORE)]
    passed, previous = [], []
    for one, share in ((0, 21), (CORE, 18)):
        cut = states * share // 32
        outs = [shape(count, width, dtype=BF16) for count in (cut, states - cut)]
        pair = received[2 * one : 2 * one + 2][::-1]
        kernel = functools.partial(pieces_kernel, one)
        top, bottom = call(kernel, outs, pair, after=previous, scratch=[pltpu.SemaphoreType.DMA((2,))])
        previous = [bottom]
        passed += [exchanged(top, "domain", FAR, one), exchanged(bottom, "domain", NEAR, one)]
    early = call(early_kernel, block * 2, (wavefunctions, theirs, *received))
    outs = block + [shape(2 * rows, width, dtype=BF16)] * (bands - 1)
    scratch = [pltpu.VMEM((2 * rows, width), F32)]
    upper = call(upper_kernel, block, (wavefunctions, theirs, *passed[::2]), after=early[:1])[0]
    operands = (wavefunctions, theirs, *passed[1::2], upper, own, *early)
    kept, *sent = call(late_kernel, outs, operands, scratch=scratch)
    parts = [exchanged(sent[mask - 1], "band", mask) for mask in (1, *reversed(range(2, bands)))]
    mine, others = call(sum_kernel, [shape(rows, width)] * 2, (kept, *parts))
    return mine, exchanged(others, "domain", CORE), operator


def rotate_any(wavefunctions, rotation):
    columns = lax.all_gather(rotation, "domain", axis=1, tiled=True)
    return lax.psum_scatter(dot(wavefunctions, columns), "band", scatter_dimension=1, tiled=True)


def faces_kernel(mine, other, assembled, pick, total, faces, onward):
    own, width = mine.shape
    columns = 2 * width
    first = core() == 0
    for side, half in enumerate((jnp.where(first, mine[...], other[...]), jnp.where(first, other[...], mine[...]))):
        total[:, side * width : (side + 1) * width] = half
    high, low = split(total[...])
    faces[...] = dot(pick[...], high).astype(BF16)
    onward[:, :columns] = (dot(assembled[own:, :own], high) + dot(assembled[own:, :own], low)).astype(BF16)
    onward[:, columns:] = assembled[own:, own:]


def inner_kernel(total, assembled, pick, out, faces):
    own, columns = total.shape
    high, low = split(total[...])
    inner = assembled[:own, :own]
    out[...] = dot(inner, high) + dot(inner, low)
    faces[:, :columns] = dot(pick[...], high).astype(BF16)
    faces[:, columns:] = dot(pick[...], low).astype(BF16)


def final_kernel(inner, faces, assembled, spread, incoming, back, out):
    own, columns = inner.shape
    domain, count = lax.axis_index("domain"), lax.axis_size("domain")
    incoming = jnp.where(domain == count - 1, jnp.zeros(incoming.shape, BF16), incoming[...])
    back = jnp.where(domain == 0, jnp.zeros(back.shape, BF16), back[...])
    extra = dot(back[:, columns:], faces[...])
    high, low = split(back[:, :columns].astype(F32) + extra[:, :columns] + extra[:, columns:])
    matrix = jnp.concatenate([assembled[:own, own:], spread[...], spread[...]], 1)
    out[...] = inner[...] + dot(matrix, jnp.concatenate([incoming, high, low], 0))


def rotated(value, axis, steps):
    count = lax.axis_size(axis)
    return lax.ppermute(value, axis, [(source, (source + steps) % count) for source in range(count)])


def finish_square(mine, other, operator):
    assembled, pick, spread = operator
    rows, width = mine.shape
    shared, columns = pick.shape[0], 2 * width
    outs = [shape(rows, columns), shape(shared, columns, dtype=BF16), shape(shared, columns + shared, dtype=BF16)]
    total, faces, onward = call(faces_kernel, outs, (mine, other, assembled, pick))
    back, incoming = rotated(onward, "domain", 1), rotated(faces, "domain", -1)
    outs = [shape(rows, columns), shape(shared, 2 * columns, dtype=BF16)]
    inner, faces = call(inner_kernel, outs, (total, assembled, pick))
    return call(final_kernel, outs[:1], (inner, faces, assembled, spread, incoming, back))[0]


def finish_any(rotated, cell_matrices, cell_nodes, face_map):
    own = rotated.shape[0]
    assembled, pick, returned = assemble_any(cell_matrices, cell_nodes, face_map, own)
    rotated = rotated.astype(BF16).astype(assembled.dtype)
    incoming = shifted(dot(pick, rotated).astype(BF16), "domain", -1).astype(assembled.dtype)
    back = shifted(dot(assembled[own:, :own], rotated), "domain", 1)
    inner = dot(assembled[:own, :own], rotated) + dot(returned, rotated) + dot(assembled[:own, own:], incoming)
    return inner + dot(pick.T.astype(F32), back)


def assemble_any(cell_matrices, cell_nodes, face_map, own):
    cells = cell_nodes.shape[0]
    extent = own + face_map.shape[0]
    held = BF16 if cells == 1 else F32
    places = jax.nn.one_hot(cell_nodes, extent, dtype=held)
    assembled = jnp.zeros((extent, extent), F32)
    for cell in range(cells):
        rows = dot(places[cell].T, cell_matrices[cell].astype(held)).astype(held)
        assembled = assembled + dot(rows, places[cell])
    assembled = assembled.astype(held)
    pick = jax.nn.one_hot(face_map, own, dtype=held)
    corner = shifted(assembled[own:, own:], "domain", 1)
    returned = dot(dot(pick.T, corner).astype(held), pick).astype(held)
    return assembled, pick, returned


def assemble_kernel(matrix, nodes, faces, assembled, pick, spread):
    extent = assembled.shape[0]
    places = jnp.where(lax.broadcasted_iota(jnp.int32, (extent, extent), 0) == nodes[...], 1.0, 0.0).astype(BF16)
    rows = dot(places, matrix[0]).astype(BF16)
    whole = lax.dot_general(rows, places, (((1,), (1,)), ((), ())), preferred_element_type=F32)
    assembled[...] = whole.astype(BF16)
    chosen = jnp.where(lax.broadcasted_iota(jnp.int32, spread.shape, 0) == faces[...], 1.0, 0.0)
    spread[...] = chosen.astype(BF16)
    pick[...] = chosen.T.astype(BF16)


def assemble(cell_matrices, cell_nodes, face_map, own, after):
    shared = face_map.shape[0]
    outs = [(own + shared, own + shared), (shared, own), (own, shared)]
    operands = (cell_matrices, cell_nodes, face_map.reshape(1, shared))
    return call(assemble_kernel, [shape(*dims, dtype=BF16) for dims in outs], operands, after=(after,))


def local(wavefunctions, rotation, cell_matrices, cell_nodes, face_map):
    chips = lax.axis_size("domain") // 2
    if chips == FAR and chips == lax.axis_size("band") and cell_nodes.shape[0] == 1:
        operator = functools.partial(assemble, cell_matrices, cell_nodes, face_map, wavefunctions.shape[0])
        return finish_square(*rotate_square(wavefunctions, rotation, operator))
    return finish_any(rotate_any(wavefunctions, rotation), cell_matrices, cell_nodes, face_map)


def solution(mesh):
    in_specs = (
        P("domain", "band"),
        P("band", "domain"),
        P("domain", None, None),
        P("domain", None),
        P("domain"),
    )
    out_specs = P("domain", "band")
    return jax.shard_map(local, mesh=mesh, in_specs=in_specs, out_specs=out_specs, check_vma=False)
```

```python
import functools

import jax
import jax.numpy as jnp
from jax import lax
from jax.experimental import pallas as pl
from jax.experimental.pallas import tpu as pltpu
from jax.sharding import PartitionSpec as P

CORE, NEAR, FAR = 1, 2, 4
VMEM = pl.BlockSpec(memory_space=pltpu.VMEM)
ANY = pl.BlockSpec(memory_space=pl.ANY)
F32, BF16 = jnp.float32, jnp.bfloat16


def dot(left, right):
    precision = lax.Precision.HIGHEST if left.dtype == F32 else None
    return jnp.dot(left, right, precision=precision, preferred_element_type=F32)


def split(value):
    high = value.astype(BF16)
    return high, (value - high.astype(F32)).astype(BF16)


def shifted(value, axis, steps):
    count = lax.axis_size(axis)
    leading, last = (max(0, -steps), min(count, count - steps))
    return lax.ppermute(value, axis, [(source, source + steps) for source in range(leading, last)])


def exchanged(value, axis, mask, core=None):
    sources = range(lax.axis_size(axis))
    return lax.ppermute(value, axis, [(source, source ^ mask) for source in sources if core in (None, source & CORE)])


def paired(value, mask, one):
    count, bands = lax.axis_size("domain"), lax.axis_size("band")
    pairs = []
    for place in range(count):
        for band in range(bands):
            partner = (place ^ mask, band) if place & CORE == one else (place, band ^ 1)
            pairs.append((place * bands + band, partner[0] * bands + partner[1]))
    return lax.ppermute(value, ("domain", "band"), pairs)


def call(kernel, outs, operands, after=(), spaces=None, scratch=()):
    after = tuple(after)
    count = len(operands)

    def body(*refs):
        kernel(*refs[:count], *refs[count + len(after) :])

    return pl.pallas_call(
        body,
        out_shape=outs,
        in_specs=[pl.BlockSpec(memory_space=space) for space in spaces or [pltpu.VMEM] * count] + [ANY] * len(after),
        out_specs=[VMEM] * len(outs),
        scratch_shapes=list(scratch),
        cost_estimate=pl.CostEstimate(flops=0, bytes_accessed=1024, transcendentals=0),
        compiler_params=pltpu.CompilerParams(vmem_limit_bytes=24 * 2**20),
    )(*operands, *after)


def shape(*dims, dtype=F32):
    return jax.ShapeDtypeStruct(dims, dtype)


def core():
    return lax.rem(lax.axis_index("domain"), 2)


def block_of_band():
    return lax.bitwise_xor(lax.div(lax.axis_index("domain"), 2), lax.axis_index("band"))


def pieces_kernel(one, far, near, top, bottom, done):
    cut, rest = top.shape[0], bottom.shape[0]

    @pl.when(core() == one)
    def _():
        copies = [
            pltpu.make_async_copy(far.at[pl.ds(0, cut)], top, done.at[0]),
            pltpu.make_async_copy(near.at[pl.ds(cut, rest)], bottom, done.at[1]),
        ]
        for copy in copies:
            copy.start()
        for copy in copies:
            copy.wait()


def own_kernel(mine, theirs, own, block):
    rows = mine.shape[0]
    for side, states in enumerate((mine, theirs)):
        block[side * rows : (side + 1) * rows] = jnp.dot(states[...], own[...], preferred_element_type=F32)


def early_kernel(mine, theirs, near_even, far_even, near_odd, far_odd, near_block, far_block):
    rows, width = mine.shape[0], near_even.shape[1]
    first = core() == 0
    near, far = jnp.where(first, near_even[...], near_odd[...]), jnp.where(first, far_even[...], far_odd[...])
    wide = jnp.concatenate([near, far], 1)
    for side, states in enumerate((mine, theirs)):
        result = jnp.dot(states[...], wide, preferred_element_type=F32)
        near_block[side * rows : (side + 1) * rows] = result[:, :width]
        far_block[side * rows : (side + 1) * rows] = result[:, width:]


def upper_kernel(mine, theirs, top_even, top_odd, block):
    rows = mine.shape[0]

    def multiply(top):
        for side, states in enumerate((mine, theirs)):
            result = jnp.dot(states[:, : top.shape[0]], top[...], preferred_element_type=F32)
            block[side * rows : (side + 1) * rows] = result

    pl.when(core() == 0)(lambda: multiply(top_even))
    pl.when(core() != 0)(lambda: multiply(top_odd))


def late_kernel(mine, theirs, bottom_even, bottom_odd, upper, own, near, far, kept, *refs):
    sent, last = refs[:-1], refs[-1]
    rows = mine.shape[0]

    def multiply(bottom):
        start = mine.shape[1] - bottom.shape[0]
        for side, states in enumerate((mine, theirs)):
            span = slice(side * rows, (side + 1) * rows)
            last[span] = upper[span] + jnp.dot(states[:, start:], bottom[...], preferred_element_type=F32)

    pl.when(core() == 0)(lambda: multiply(bottom_even))
    pl.when(core() != 0)(lambda: multiply(bottom_odd))
    where = block_of_band()

    def store(out, slot, block):
        @pl.when(slot == lax.bitwise_xor(where, mask))
        def _():
            out[...] = block[...].astype(out.dtype)

    for mask, out in enumerate((kept, *sent)):
        for slot, block in enumerate((own, near, far, last)):
            store(out, slot, block)


def sum_kernel(kept, *refs):
    parts, (mine, theirs) = refs[:-2], refs[-2:]
    value = kept[...]
    for part in parts:
        value = value + part[...].astype(F32)
    rows = mine.shape[0]
    mine[...] = value[:rows]
    theirs[...] = value[rows:]


def rotate_square(wavefunctions, rotation, operator):
    bands, chips = lax.axis_size("band"), lax.axis_size("domain") // 2
    rows, states = wavefunctions.shape
    width = rotation.shape[1]
    received = [paired(rotation, NEAR, 0), paired(rotation, FAR, 0)]
    theirs = exchanged(wavefunctions, "domain", CORE)
    block = [shape(2 * rows, width)]
    operator = operator(theirs)
    later, _ = lax.optimization_barrier((rotation, operator[0]))
    own = call(own_kernel, block, (wavefunctions, theirs, rotation), after=(later,))[0]
    received += [exchanged(later, "domain", NEAR, CORE), exchanged(later, "domain", FAR, CORE)]
    passed, previous = [], [own]
    for one, share in ((0, 21), (CORE, 18)):
        cut = states * share // 32
        outs = [shape(count, width, dtype=BF16) for count in (cut, states - cut)]
        pair = received[2 * one : 2 * one + 2][::-1]
        kernel = functools.partial(pieces_kernel, one)
        top, bottom = call(kernel, outs, pair, after=previous, scratch=[pltpu.SemaphoreType.DMA((2,))])
        previous = [bottom]
        if one:
            passed += [paired(top, NEAR, one), paired(bottom, FAR, one)]
        else:
            passed += [exchanged(top, "domain", NEAR, one), exchanged(bottom, "domain", FAR, one)]
    early = call(early_kernel, block * 2, (wavefunctions, theirs, *received))
    outs = block + [shape(2 * rows, width, dtype=BF16)] * (bands - 1)
    scratch = [pltpu.VMEM((2 * rows, width), F32)]
    upper = call(upper_kernel, block, (wavefunctions, theirs, *passed[::2]), after=early[:1])[0]
    operands = (wavefunctions, theirs, *passed[1::2], upper, own, *early)
    kept, *sent = call(late_kernel, outs, operands, scratch=scratch)
    parts = [exchanged(sent[mask - 1], "band", mask) for mask in reversed(range(1, bands))]
    mine, others = call(sum_kernel, [shape(rows, width)] * 2, (kept, *parts))
    return mine, exchanged(others, "domain", CORE), operator


def rotate_any(wavefunctions, rotation):
    columns = lax.all_gather(rotation, "domain", axis=1, tiled=True)
    return lax.psum_scatter(dot(wavefunctions, columns), "band", scatter_dimension=1, tiled=True)


def faces_kernel(mine, other, assembled, pick, total, faces, onward):
    own, width = mine.shape
    columns = 2 * width
    first = core() == 0
    for side, half in enumerate((jnp.where(first, mine[...], other[...]), jnp.where(first, other[...], mine[...]))):
        total[:, side * width : (side + 1) * width] = half
    high, low = split(total[...])
    faces[...] = dot(pick[...], high).astype(BF16)
    onward[:, :columns] = (dot(assembled[own:, :own], high) + dot(assembled[own:, :own], low)).astype(BF16)
    onward[:, columns:] = assembled[own:, own:]


def inner_kernel(total, assembled, pick, out, faces):
    own, columns = total.shape
    high, low = split(total[...])
    inner = assembled[:own, :own]
    out[...] = dot(inner, high) + dot(inner, low)
    faces[:, :columns] = dot(pick[...], high).astype(BF16)
    faces[:, columns:] = dot(pick[...], low).astype(BF16)


def final_kernel(inner, faces, assembled, spread, incoming, back, out):
    own, columns = inner.shape
    domain, count = lax.axis_index("domain"), lax.axis_size("domain")
    incoming = jnp.where(domain == count - 1, jnp.zeros(incoming.shape, BF16), incoming[...])
    back = jnp.where(domain == 0, jnp.zeros(back.shape, BF16), back[...])
    extra = dot(back[:, columns:], faces[...])
    high, low = split(back[:, :columns].astype(F32) + extra[:, :columns] + extra[:, columns:])
    matrix = jnp.concatenate([assembled[:own, own:], spread[...], spread[...]], 1)
    out[...] = inner[...] + dot(matrix, jnp.concatenate([incoming, high, low], 0))


def rotated(value, axis, steps):
    count = lax.axis_size(axis)
    return lax.ppermute(value, axis, [(source, (source + steps) % count) for source in range(count)])


def finish_square(mine, other, operator):
    assembled, pick, spread = operator
    rows, width = mine.shape
    shared, columns = pick.shape[0], 2 * width
    outs = [shape(rows, columns), shape(shared, columns, dtype=BF16), shape(shared, columns + shared, dtype=BF16)]
    total, faces, onward = call(faces_kernel, outs, (mine, other, assembled, pick))
    back, incoming = rotated(onward, "domain", 1), rotated(faces, "domain", -1)
    outs = [shape(rows, columns), shape(shared, 2 * columns, dtype=BF16)]
    inner, faces = call(inner_kernel, outs, (total, assembled, pick))
    return call(final_kernel, outs[:1], (inner, faces, assembled, spread, incoming, back))[0]


def finish_any(rotated, cell_matrices, cell_nodes, face_map):
    own = rotated.shape[0]
    assembled, pick, returned = assemble_any(cell_matrices, cell_nodes, face_map, own)
    rotated = rotated.astype(BF16).astype(assembled.dtype)
    incoming = shifted(dot(pick, rotated).astype(BF16), "domain", -1).astype(assembled.dtype)
    back = shifted(dot(assembled[own:, :own], rotated), "domain", 1)
    inner = dot(assembled[:own, :own], rotated) + dot(returned, rotated) + dot(assembled[:own, own:], incoming)
    return inner + dot(pick.T.astype(F32), back)


def assemble_any(cell_matrices, cell_nodes, face_map, own):
    cells = cell_nodes.shape[0]
    extent = own + face_map.shape[0]
    held = BF16 if cells == 1 else F32
    places = jax.nn.one_hot(cell_nodes, extent, dtype=held)
    assembled = jnp.zeros((extent, extent), F32)
    for cell in range(cells):
        rows = dot(places[cell].T, cell_matrices[cell].astype(held)).astype(held)
        assembled = assembled + dot(rows, places[cell])
    assembled = assembled.astype(held)
    pick = jax.nn.one_hot(face_map, own, dtype=held)
    corner = shifted(assembled[own:, own:], "domain", 1)
    returned = dot(dot(pick.T, corner).astype(held), pick).astype(held)
    return assembled, pick, returned


def assemble_kernel(matrix, nodes, faces, assembled, pick, spread):
    extent = assembled.shape[0]
    places = jnp.where(lax.broadcasted_iota(jnp.int32, (extent, extent), 0) == nodes[...], 1.0, 0.0).astype(BF16)
    rows = dot(places, matrix[0]).astype(BF16)
    whole = lax.dot_general(rows, places, (((1,), (1,)), ((), ())), preferred_element_type=F32)
    assembled[...] = whole.astype(BF16)
    chosen = jnp.where(lax.broadcasted_iota(jnp.int32, spread.shape, 0) == faces[...], 1.0, 0.0)
    spread[...] = chosen.astype(BF16)
    pick[...] = chosen.T.astype(BF16)


def assemble(cell_matrices, cell_nodes, face_map, own, after):
    shared = face_map.shape[0]
    outs = [(own + shared, own + shared), (shared, own), (own, shared)]
    operands = (cell_matrices, cell_nodes, face_map.reshape(1, shared))
    return call(assemble_kernel, [shape(*dims, dtype=BF16) for dims in outs], operands, after=(after,))


def local(wavefunctions, rotation, cell_matrices, cell_nodes, face_map):
    chips = lax.axis_size("domain") // 2
    if chips == FAR and chips == lax.axis_size("band") and cell_nodes.shape[0] == 1:
        operator = functools.partial(assemble, cell_matrices, cell_nodes, face_map, wavefunctions.shape[0])
        return finish_square(*rotate_square(wavefunctions, rotation, operator))
    return finish_any(rotate_any(wavefunctions, rotation), cell_matrices, cell_nodes, face_map)


def solution(mesh):
    in_specs = (
        P("domain", "band"),
        P("band", "domain"),
        P("domain", None, None),
        P("domain", None),
        P("domain"),
    )
    out_specs = P("domain", "band")
    return jax.shard_map(local, mesh=mesh, in_specs=in_specs, out_specs=out_specs, check_vma=False)
```

```python
import functools

import jax
import jax.numpy as jnp
from jax import lax
from jax.experimental import pallas as pl
from jax.experimental.pallas import tpu as pltpu
from jax.sharding import PartitionSpec as P

CORE, NEAR, FAR = 1, 2, 4
VMEM = pl.BlockSpec(memory_space=pltpu.VMEM)
ANY = pl.BlockSpec(memory_space=pl.ANY)
F32, BF16 = jnp.float32, jnp.bfloat16


def dot(left, right):
    precision = lax.Precision.HIGHEST if left.dtype == F32 else None
    return jnp.dot(left, right, precision=precision, preferred_element_type=F32)


def split(value):
    high = value.astype(BF16)
    return high, (value - high.astype(F32)).astype(BF16)


def shifted(value, axis, steps):
    count = lax.axis_size(axis)
    leading, last = (max(0, -steps), min(count, count - steps))
    return lax.ppermute(value, axis, [(source, source + steps) for source in range(leading, last)])


def exchanged(value, axis, mask, core=None):
    sources = range(lax.axis_size(axis))
    return lax.ppermute(value, axis, [(source, source ^ mask) for source in sources if core in (None, source & CORE)])


def paired(value, mask, one):
    count, bands = lax.axis_size("domain"), lax.axis_size("band")
    pairs = []
    for place in range(count):
        for band in range(bands):
            partner = (place ^ mask, band) if place & CORE == one else (place, band ^ 1)
            pairs.append((place * bands + band, partner[0] * bands + partner[1]))
    return lax.ppermute(value, ("domain", "band"), pairs)


def call(kernel, outs, operands, after=(), spaces=None, scratch=()):
    after = tuple(after)
    count = len(operands)

    def body(*refs):
        kernel(*refs[:count], *refs[count + len(after) :])

    return pl.pallas_call(
        body,
        out_shape=outs,
        in_specs=[pl.BlockSpec(memory_space=space) for space in spaces or [pltpu.VMEM] * count] + [ANY] * len(after),
        out_specs=[VMEM] * len(outs),
        scratch_shapes=list(scratch),
        cost_estimate=pl.CostEstimate(flops=0, bytes_accessed=1024, transcendentals=0),
        compiler_params=pltpu.CompilerParams(vmem_limit_bytes=24 * 2**20),
    )(*operands, *after)


def shape(*dims, dtype=F32):
    return jax.ShapeDtypeStruct(dims, dtype)


def core():
    return lax.rem(lax.axis_index("domain"), 2)


def block_of_band():
    return lax.bitwise_xor(lax.div(lax.axis_index("domain"), 2), lax.axis_index("band"))


def pieces_kernel(one, far, near, top, bottom, done):
    cut, rest = top.shape[0], bottom.shape[0]

    @pl.when(core() == one)
    def _():
        copies = [
            pltpu.make_async_copy(far.at[pl.ds(0, cut)], top, done.at[0]),
            pltpu.make_async_copy(near.at[pl.ds(cut, rest)], bottom, done.at[1]),
        ]
        for copy in copies:
            copy.start()
        for copy in copies:
            copy.wait()


def own_kernel(mine, theirs, own, block):
    rows = mine.shape[0]
    for side, states in enumerate((mine, theirs)):
        block[side * rows : (side + 1) * rows] = jnp.dot(states[...], own[...], preferred_element_type=F32)


def early_kernel(mine, theirs, near_even, far_even, near_odd, far_odd, near_block, far_block):
    rows, width = mine.shape[0], near_even.shape[1]
    first = core() == 0
    near, far = jnp.where(first, near_even[...], near_odd[...]), jnp.where(first, far_even[...], far_odd[...])
    wide = jnp.concatenate([near, far], 1)
    for side, states in enumerate((mine, theirs)):
        result = jnp.dot(states[...], wide, preferred_element_type=F32)
        near_block[side * rows : (side + 1) * rows] = result[:, :width]
        far_block[side * rows : (side + 1) * rows] = result[:, width:]


def upper_kernel(mine, theirs, top_even, top_odd, block):
    rows = mine.shape[0]

    def multiply(top):
        for side, states in enumerate((mine, theirs)):
            result = jnp.dot(states[:, : top.shape[0]], top[...], preferred_element_type=F32)
            block[side * rows : (side + 1) * rows] = result

    pl.when(core() == 0)(lambda: multiply(top_even))
    pl.when(core() != 0)(lambda: multiply(top_odd))


def late_kernel(mine, theirs, bottom_even, bottom_odd, upper, own, near, far, kept, *refs):
    sent, last = refs[:-1], refs[-1]
    rows = mine.shape[0]

    def multiply(bottom):
        start = mine.shape[1] - bottom.shape[0]
        for side, states in enumerate((mine, theirs)):
            span = slice(side * rows, (side + 1) * rows)
            last[span] = upper[span] + jnp.dot(states[:, start:], bottom[...], preferred_element_type=F32)

    pl.when(core() == 0)(lambda: multiply(bottom_even))
    pl.when(core() != 0)(lambda: multiply(bottom_odd))
    where = block_of_band()

    def store(out, slot, block):
        @pl.when(slot == lax.bitwise_xor(where, mask))
        def _():
            out[...] = block[...].astype(out.dtype)

    for mask, out in enumerate((kept, *sent)):
        for slot, block in enumerate((own, near, far, last)):
            store(out, slot, block)


def sum_kernel(kept, *refs):
    parts, (mine, theirs) = refs[:-2], refs[-2:]
    value = kept[...]
    for part in parts:
        value = value + part[...].astype(F32)
    rows = mine.shape[0]
    mine[...] = value[:rows]
    theirs[...] = value[rows:]


def rotate_square(wavefunctions, rotation, operator):
    bands, chips = lax.axis_size("band"), lax.axis_size("domain") // 2
    rows, states = wavefunctions.shape
    width = rotation.shape[1]
    received = [paired(rotation, NEAR, 0), paired(rotation, FAR, 0)]
    theirs = exchanged(wavefunctions, "domain", CORE)
    block = [shape(2 * rows, width)]
    operator = operator(theirs)
    later, _ = lax.optimization_barrier((rotation, operator[0]))
    own = call(own_kernel, block, (wavefunctions, theirs, rotation), after=(later,))[0]
    received += [exchanged(later, "domain", NEAR, CORE), exchanged(later, "domain", FAR, CORE)]
    passed, previous = [], [own]
    for one, share in ((0, 21), (CORE, 18)):
        cut = states * share // 32
        outs = [shape(count, width, dtype=BF16) for count in (cut, states - cut)]
        pair = received[2 * one : 2 * one + 2][::-1]
        kernel = functools.partial(pieces_kernel, one)
        top, bottom = call(kernel, outs, pair, after=previous, scratch=[pltpu.SemaphoreType.DMA((2,))])
        previous = [bottom]
        passed.append(exchanged(top, "domain", NEAR, one))
        passed.append(paired(bottom, FAR, one) if one else exchanged(bottom, "domain", FAR, one))
    early = call(early_kernel, block * 2, (wavefunctions, theirs, *received))
    outs = block + [shape(2 * rows, width, dtype=BF16)] * (bands - 1)
    scratch = [pltpu.VMEM((2 * rows, width), F32)]
    upper = call(upper_kernel, block, (wavefunctions, theirs, *passed[::2]), after=early[:1])[0]
    operands = (wavefunctions, theirs, *passed[1::2], upper, own, *early)
    kept, *sent = call(late_kernel, outs, operands, scratch=scratch)
    parts = [exchanged(sent[mask - 1], "band", mask) for mask in reversed(range(1, bands))]
    mine, others = call(sum_kernel, [shape(rows, width)] * 2, (kept, *parts))
    return mine, exchanged(others, "domain", CORE), operator


def rotate_any(wavefunctions, rotation):
    columns = lax.all_gather(rotation, "domain", axis=1, tiled=True)
    return lax.psum_scatter(dot(wavefunctions, columns), "band", scatter_dimension=1, tiled=True)


def faces_kernel(mine, other, assembled, pick, total, faces, onward):
    own, width = mine.shape
    columns = 2 * width
    first = core() == 0
    for side, half in enumerate((jnp.where(first, mine[...], other[...]), jnp.where(first, other[...], mine[...]))):
        total[:, side * width : (side + 1) * width] = half
    high, low = split(total[...])
    faces[...] = dot(pick[...], high).astype(BF16)
    onward[:, :columns] = (dot(assembled[own:, :own], high) + dot(assembled[own:, :own], low)).astype(BF16)
    onward[:, columns:] = assembled[own:, own:]


def inner_kernel(total, assembled, pick, out, faces):
    own, columns = total.shape
    high, low = split(total[...])
    inner = assembled[:own, :own]
    out[...] = dot(inner, high) + dot(inner, low)
    faces[:, :columns] = dot(pick[...], high).astype(BF16)
    faces[:, columns:] = dot(pick[...], low).astype(BF16)


def final_kernel(inner, faces, assembled, spread, incoming, back, out):
    own, columns = inner.shape
    domain, count = lax.axis_index("domain"), lax.axis_size("domain")
    incoming = jnp.where(domain == count - 1, jnp.zeros(incoming.shape, BF16), incoming[...])
    back = jnp.where(domain == 0, jnp.zeros(back.shape, BF16), back[...])
    extra = dot(back[:, columns:], faces[...])
    high, low = split(back[:, :columns].astype(F32) + extra[:, :columns] + extra[:, columns:])
    matrix = jnp.concatenate([assembled[:own, own:], spread[...], spread[...]], 1)
    out[...] = inner[...] + dot(matrix, jnp.concatenate([incoming, high, low], 0))


def rotated(value, axis, steps):
    count = lax.axis_size(axis)
    return lax.ppermute(value, axis, [(source, (source + steps) % count) for source in range(count)])


def finish_square(mine, other, operator):
    assembled, pick, spread = operator
    rows, width = mine.shape
    shared, columns = pick.shape[0], 2 * width
    outs = [shape(rows, columns), shape(shared, columns, dtype=BF16), shape(shared, columns + shared, dtype=BF16)]
    total, faces, onward = call(faces_kernel, outs, (mine, other, assembled, pick))
    back, incoming = rotated(onward, "domain", 1), rotated(faces, "domain", -1)
    outs = [shape(rows, columns), shape(shared, 2 * columns, dtype=BF16)]
    inner, faces = call(inner_kernel, outs, (total, assembled, pick))
    return call(final_kernel, outs[:1], (inner, faces, assembled, spread, incoming, back))[0]


def finish_any(rotated, cell_matrices, cell_nodes, face_map):
    own = rotated.shape[0]
    assembled, pick, returned = assemble_any(cell_matrices, cell_nodes, face_map, own)
    rotated = rotated.astype(BF16).astype(assembled.dtype)
    incoming = shifted(dot(pick, rotated).astype(BF16), "domain", -1).astype(assembled.dtype)
    back = shifted(dot(assembled[own:, :own], rotated), "domain", 1)
    inner = dot(assembled[:own, :own], rotated) + dot(returned, rotated) + dot(assembled[:own, own:], incoming)
    return inner + dot(pick.T.astype(F32), back)


def assemble_any(cell_matrices, cell_nodes, face_map, own):
    cells = cell_nodes.shape[0]
    extent = own + face_map.shape[0]
    held = BF16 if cells == 1 else F32
    places = jax.nn.one_hot(cell_nodes, extent, dtype=held)
    assembled = jnp.zeros((extent, extent), F32)
    for cell in range(cells):
        rows = dot(places[cell].T, cell_matrices[cell].astype(held)).astype(held)
        assembled = assembled + dot(rows, places[cell])
    assembled = assembled.astype(held)
    pick = jax.nn.one_hot(face_map, own, dtype=held)
    corner = shifted(assembled[own:, own:], "domain", 1)
    returned = dot(dot(pick.T, corner).astype(held), pick).astype(held)
    return assembled, pick, returned


def assemble_kernel(matrix, nodes, faces, assembled, pick, spread):
    extent = assembled.shape[0]
    places = jnp.where(lax.broadcasted_iota(jnp.int32, (extent, extent), 0) == nodes[...], 1.0, 0.0).astype(BF16)
    rows = dot(places, matrix[0]).astype(BF16)
    whole = lax.dot_general(rows, places, (((1,), (1,)), ((), ())), preferred_element_type=F32)
    assembled[...] = whole.astype(BF16)
    chosen = jnp.where(lax.broadcasted_iota(jnp.int32, spread.shape, 0) == faces[...], 1.0, 0.0)
    spread[...] = chosen.astype(BF16)
    pick[...] = chosen.T.astype(BF16)


def assemble(cell_matrices, cell_nodes, face_map, own, after):
    shared = face_map.shape[0]
    outs = [(own + shared, own + shared), (shared, own), (own, shared)]
    operands = (cell_matrices, cell_nodes, face_map.reshape(1, shared))
    return call(assemble_kernel, [shape(*dims, dtype=BF16) for dims in outs], operands, after=(after,))


def local(wavefunctions, rotation, cell_matrices, cell_nodes, face_map):
    chips = lax.axis_size("domain") // 2
    if chips == FAR and chips == lax.axis_size("band") and cell_nodes.shape[0] == 1:
        operator = functools.partial(assemble, cell_matrices, cell_nodes, face_map, wavefunctions.shape[0])
        return finish_square(*rotate_square(wavefunctions, rotation, operator))
    return finish_any(rotate_any(wavefunctions, rotation), cell_matrices, cell_nodes, face_map)


def solution(mesh):
    in_specs = (
        P("domain", "band"),
        P("band", "domain"),
        P("domain", None, None),
        P("domain", None),
        P("domain"),
    )
    out_specs = P("domain", "band")
    return jax.shard_map(local, mesh=mesh, in_specs=in_specs, out_specs=out_specs, check_vma=False)
```

```python
import functools

import jax
import jax.numpy as jnp
from jax import lax
from jax.experimental import pallas as pl
from jax.experimental.pallas import tpu as pltpu
from jax.sharding import PartitionSpec as P

CORE, NEAR, FAR = 1, 2, 4
VMEM = pl.BlockSpec(memory_space=pltpu.VMEM)
ANY = pl.BlockSpec(memory_space=pl.ANY)
F32, BF16 = jnp.float32, jnp.bfloat16


def dot(left, right):
    precision = lax.Precision.HIGHEST if left.dtype == F32 else None
    return jnp.dot(left, right, precision=precision, preferred_element_type=F32)


def split(value):
    high = value.astype(BF16)
    return high, (value - high.astype(F32)).astype(BF16)


def shifted(value, axis, steps):
    count = lax.axis_size(axis)
    leading, last = (max(0, -steps), min(count, count - steps))
    return lax.ppermute(value, axis, [(source, source + steps) for source in range(leading, last)])


def exchanged(value, axis, mask, core=None):
    sources = range(lax.axis_size(axis))
    return lax.ppermute(value, axis, [(source, source ^ mask) for source in sources if core in (None, source & CORE)])


def paired(value, mask, one):
    count, bands = lax.axis_size("domain"), lax.axis_size("band")
    pairs = []
    for place in range(count):
        for band in range(bands):
            partner = (place ^ mask, band) if place & CORE == one else (place, band ^ 1)
            pairs.append((place * bands + band, partner[0] * bands + partner[1]))
    return lax.ppermute(value, ("domain", "band"), pairs)


def call(kernel, outs, operands, after=(), spaces=None, scratch=()):
    after = tuple(after)
    count = len(operands)

    def body(*refs):
        kernel(*refs[:count], *refs[count + len(after) :])

    return pl.pallas_call(
        body,
        out_shape=outs,
        in_specs=[pl.BlockSpec(memory_space=space) for space in spaces or [pltpu.VMEM] * count] + [ANY] * len(after),
        out_specs=[VMEM] * len(outs),
        scratch_shapes=list(scratch),
        cost_estimate=pl.CostEstimate(flops=0, bytes_accessed=1024, transcendentals=0),
        compiler_params=pltpu.CompilerParams(vmem_limit_bytes=24 * 2**20),
    )(*operands, *after)


def shape(*dims, dtype=F32):
    return jax.ShapeDtypeStruct(dims, dtype)


def core():
    return lax.rem(lax.axis_index("domain"), 2)


def block_of_band():
    return lax.bitwise_xor(lax.div(lax.axis_index("domain"), 2), lax.axis_index("band"))


def pieces_kernel(one, far, near, top, bottom, done):
    cut, rest = top.shape[0], bottom.shape[0]

    @pl.when(core() == one)
    def _():
        copies = [
            pltpu.make_async_copy(far.at[pl.ds(0, cut)], top, done.at[0]),
            pltpu.make_async_copy(near.at[pl.ds(cut, rest)], bottom, done.at[1]),
        ]
        for copy in copies:
            copy.start()
        for copy in copies:
            copy.wait()


def own_kernel(mine, theirs, own, block):
    rows = mine.shape[0]
    for side, states in enumerate((mine, theirs)):
        block[side * rows : (side + 1) * rows] = jnp.dot(states[...], own[...], preferred_element_type=F32)


def early_kernel(mine, theirs, near_even, far_even, near_odd, far_odd, near_block, far_block):
    rows, width = mine.shape[0], near_even.shape[1]
    first = core() == 0
    near, far = jnp.where(first, near_even[...], near_odd[...]), jnp.where(first, far_even[...], far_odd[...])
    wide = jnp.concatenate([near, far], 1)
    for side, states in enumerate((mine, theirs)):
        result = jnp.dot(states[...], wide, preferred_element_type=F32)
        near_block[side * rows : (side + 1) * rows] = result[:, :width]
        far_block[side * rows : (side + 1) * rows] = result[:, width:]


def upper_kernel(mine, theirs, top_even, top_odd, block):
    rows = mine.shape[0]

    def multiply(top):
        for side, states in enumerate((mine, theirs)):
            result = jnp.dot(states[:, : top.shape[0]], top[...], preferred_element_type=F32)
            block[side * rows : (side + 1) * rows] = result

    pl.when(core() == 0)(lambda: multiply(top_even))
    pl.when(core() != 0)(lambda: multiply(top_odd))


def late_kernel(mine, theirs, bottom_even, bottom_odd, upper, own, near, far, kept, *refs):
    sent, last = refs[:-1], refs[-1]
    rows = mine.shape[0]

    def multiply(bottom):
        start = mine.shape[1] - bottom.shape[0]
        for side, states in enumerate((mine, theirs)):
            span = slice(side * rows, (side + 1) * rows)
            last[span] = upper[span] + jnp.dot(states[:, start:], bottom[...], preferred_element_type=F32)

    pl.when(core() == 0)(lambda: multiply(bottom_even))
    pl.when(core() != 0)(lambda: multiply(bottom_odd))
    where = block_of_band()

    def store(out, slot, block):
        @pl.when(slot == lax.bitwise_xor(where, mask))
        def _():
            out[...] = block[...].astype(out.dtype)

    for mask, out in enumerate((kept, *sent)):
        for slot, block in enumerate((own, near, far, last)):
            store(out, slot, block)


def sum_kernel(kept, *refs):
    parts, (mine, theirs) = refs[:-2], refs[-2:]
    value = kept[...]
    for part in parts:
        value = value + part[...].astype(F32)
    rows = mine.shape[0]
    mine[...] = value[:rows]
    theirs[...] = value[rows:]


def rotate_square(wavefunctions, rotation, operator):
    bands, chips = lax.axis_size("band"), lax.axis_size("domain") // 2
    rows, states = wavefunctions.shape
    width = rotation.shape[1]
    received = [paired(rotation, NEAR, 0), paired(rotation, FAR, 0)]
    theirs = exchanged(wavefunctions, "domain", CORE)
    block = [shape(2 * rows, width)]
    operator = operator(theirs)
    later, _ = lax.optimization_barrier((rotation, operator[0]))
    own = call(own_kernel, block, (wavefunctions, theirs, rotation), after=(later,))[0]
    received += [exchanged(later, "domain", NEAR, CORE), exchanged(later, "domain", FAR, CORE)]
    passed, previous = [], [own]
    for one, share in ((0, 21), (CORE, 18)):
        cut = states * share // 32
        outs = [shape(count, width, dtype=BF16) for count in (cut, states - cut)]
        pair = received[2 * one : 2 * one + 2][::-1]
        kernel = functools.partial(pieces_kernel, one)
        top, bottom = call(kernel, outs, pair, after=previous, scratch=[pltpu.SemaphoreType.DMA((2,))])
        previous = [bottom]
        passed.append(exchanged(top, "domain", NEAR, one) if one else paired(top, NEAR, one))
        passed.append(paired(bottom, FAR, one) if one else exchanged(bottom, "domain", FAR, one))
    early = call(early_kernel, block * 2, (wavefunctions, theirs, *received))
    outs = block + [shape(2 * rows, width, dtype=BF16)] * (bands - 1)
    scratch = [pltpu.VMEM((2 * rows, width), F32)]
    upper = call(upper_kernel, block, (wavefunctions, theirs, *passed[::2]), after=early[:1])[0]
    operands = (wavefunctions, theirs, *passed[1::2], upper, own, *early)
    kept, *sent = call(late_kernel, outs, operands, scratch=scratch)
    parts = [exchanged(sent[mask - 1], "band", mask) for mask in reversed(range(1, bands))]
    mine, others = call(sum_kernel, [shape(rows, width)] * 2, (kept, *parts))
    return mine, exchanged(others, "domain", CORE), operator


def rotate_any(wavefunctions, rotation):
    columns = lax.all_gather(rotation, "domain", axis=1, tiled=True)
    return lax.psum_scatter(dot(wavefunctions, columns), "band", scatter_dimension=1, tiled=True)


def faces_kernel(mine, other, assembled, pick, total, faces, onward):
    own, width = mine.shape
    columns = 2 * width
    first = core() == 0
    for side, half in enumerate((jnp.where(first, mine[...], other[...]), jnp.where(first, other[...], mine[...]))):
        total[:, side * width : (side + 1) * width] = half
    high, low = split(total[...])
    faces[...] = dot(pick[...], high).astype(BF16)
    onward[:, :columns] = (dot(assembled[own:, :own], high) + dot(assembled[own:, :own], low)).astype(BF16)
    onward[:, columns:] = assembled[own:, own:]


def inner_kernel(total, assembled, pick, out, faces):
    own, columns = total.shape
    high, low = split(total[...])
    inner = assembled[:own, :own]
    out[...] = dot(inner, high) + dot(inner, low)
    faces[:, :columns] = dot(pick[...], high).astype(BF16)
    faces[:, columns:] = dot(pick[...], low).astype(BF16)


def final_kernel(inner, faces, assembled, spread, incoming, back, out):
    own, columns = inner.shape
    domain, count = lax.axis_index("domain"), lax.axis_size("domain")
    incoming = jnp.where(domain == count - 1, jnp.zeros(incoming.shape, BF16), incoming[...])
    back = jnp.where(domain == 0, jnp.zeros(back.shape, BF16), back[...])
    extra = dot(back[:, columns:], faces[...])
    high, low = split(back[:, :columns].astype(F32) + extra[:, :columns] + extra[:, columns:])
    matrix = jnp.concatenate([assembled[:own, own:], spread[...], spread[...]], 1)
    out[...] = inner[...] + dot(matrix, jnp.concatenate([incoming, high, low], 0))


def rotated(value, axis, steps):
    count = lax.axis_size(axis)
    return lax.ppermute(value, axis, [(source, (source + steps) % count) for source in range(count)])


def finish_square(mine, other, operator):
    assembled, pick, spread = operator
    rows, width = mine.shape
    shared, columns = pick.shape[0], 2 * width
    outs = [shape(rows, columns), shape(shared, columns, dtype=BF16), shape(shared, columns + shared, dtype=BF16)]
    total, faces, onward = call(faces_kernel, outs, (mine, other, assembled, pick))
    back, incoming = rotated(onward, "domain", 1), rotated(faces, "domain", -1)
    outs = [shape(rows, columns), shape(shared, 2 * columns, dtype=BF16)]
    inner, faces = call(inner_kernel, outs, (total, assembled, pick))
    return call(final_kernel, outs[:1], (inner, faces, assembled, spread, incoming, back))[0]


def finish_any(rotated, cell_matrices, cell_nodes, face_map):
    own = rotated.shape[0]
    assembled, pick, returned = assemble_any(cell_matrices, cell_nodes, face_map, own)
    rotated = rotated.astype(BF16).astype(assembled.dtype)
    incoming = shifted(dot(pick, rotated).astype(BF16), "domain", -1).astype(assembled.dtype)
    back = shifted(dot(assembled[own:, :own], rotated), "domain", 1)
    inner = dot(assembled[:own, :own], rotated) + dot(returned, rotated) + dot(assembled[:own, own:], incoming)
    return inner + dot(pick.T.astype(F32), back)


def assemble_any(cell_matrices, cell_nodes, face_map, own):
    cells = cell_nodes.shape[0]
    extent = own + face_map.shape[0]
    held = BF16 if cells == 1 else F32
    places = jax.nn.one_hot(cell_nodes, extent, dtype=held)
    assembled = jnp.zeros((extent, extent), F32)
    for cell in range(cells):
        rows = dot(places[cell].T, cell_matrices[cell].astype(held)).astype(held)
        assembled = assembled + dot(rows, places[cell])
    assembled = assembled.astype(held)
    pick = jax.nn.one_hot(face_map, own, dtype=held)
    corner = shifted(assembled[own:, own:], "domain", 1)
    returned = dot(dot(pick.T, corner).astype(held), pick).astype(held)
    return assembled, pick, returned


def assemble_kernel(matrix, nodes, faces, assembled, pick, spread):
    extent = assembled.shape[0]
    places = jnp.where(lax.broadcasted_iota(jnp.int32, (extent, extent), 0) == nodes[...], 1.0, 0.0).astype(BF16)
    rows = dot(places, matrix[0]).astype(BF16)
    whole = lax.dot_general(rows, places, (((1,), (1,)), ((), ())), preferred_element_type=F32)
    assembled[...] = whole.astype(BF16)
    chosen = jnp.where(lax.broadcasted_iota(jnp.int32, spread.shape, 0) == faces[...], 1.0, 0.0)
    spread[...] = chosen.astype(BF16)
    pick[...] = chosen.T.astype(BF16)


def assemble(cell_matrices, cell_nodes, face_map, own, after):
    shared = face_map.shape[0]
    outs = [(own + shared, own + shared), (shared, own), (own, shared)]
    operands = (cell_matrices, cell_nodes, face_map.reshape(1, shared))
    return call(assemble_kernel, [shape(*dims, dtype=BF16) for dims in outs], operands, after=(after,))


def local(wavefunctions, rotation, cell_matrices, cell_nodes, face_map):
    chips = lax.axis_size("domain") // 2
    if chips == FAR and chips == lax.axis_size("band") and cell_nodes.shape[0] == 1:
        operator = functools.partial(assemble, cell_matrices, cell_nodes, face_map, wavefunctions.shape[0])
        return finish_square(*rotate_square(wavefunctions, rotation, operator))
    return finish_any(rotate_any(wavefunctions, rotation), cell_matrices, cell_nodes, face_map)


def solution(mesh):
    in_specs = (
        P("domain", "band"),
        P("band", "domain"),
        P("domain", None, None),
        P("domain", None),
        P("domain"),
    )
    out_specs = P("domain", "band")
    return jax.shard_map(local, mesh=mesh, in_specs=in_specs, out_specs=out_specs, check_vma=False)
```

```python
import functools

import jax
import jax.numpy as jnp
from jax import lax
from jax.experimental import pallas as pl
from jax.experimental.pallas import tpu as pltpu
from jax.sharding import PartitionSpec as P

CORE, NEAR, FAR = 1, 2, 4
VMEM = pl.BlockSpec(memory_space=pltpu.VMEM)
ANY = pl.BlockSpec(memory_space=pl.ANY)
F32, BF16 = jnp.float32, jnp.bfloat16


def dot(left, right):
    precision = lax.Precision.HIGHEST if left.dtype == F32 else None
    return jnp.dot(left, right, precision=precision, preferred_element_type=F32)


def split(value):
    high = value.astype(BF16)
    return high, (value - high.astype(F32)).astype(BF16)


def shifted(value, axis, steps):
    count = lax.axis_size(axis)
    leading, last = (max(0, -steps), min(count, count - steps))
    return lax.ppermute(value, axis, [(source, source + steps) for source in range(leading, last)])


def exchanged(value, axis, mask, core=None):
    sources = range(lax.axis_size(axis))
    return lax.ppermute(value, axis, [(source, source ^ mask) for source in sources if core in (None, source & CORE)])


def paired(value, mask, one):
    count, bands = lax.axis_size("domain"), lax.axis_size("band")
    pairs = []
    for place in range(count):
        for band in range(bands):
            partner = (place ^ mask, band) if place & CORE == one else (place, band ^ 1)
            pairs.append((place * bands + band, partner[0] * bands + partner[1]))
    return lax.ppermute(value, ("domain", "band"), pairs)


def call(kernel, outs, operands, after=(), spaces=None, scratch=()):
    after = tuple(after)
    count = len(operands)

    def body(*refs):
        kernel(*refs[:count], *refs[count + len(after) :])

    return pl.pallas_call(
        body,
        out_shape=outs,
        in_specs=[pl.BlockSpec(memory_space=space) for space in spaces or [pltpu.VMEM] * count] + [ANY] * len(after),
        out_specs=[VMEM] * len(outs),
        scratch_shapes=list(scratch),
        cost_estimate=pl.CostEstimate(flops=0, bytes_accessed=1024, transcendentals=0),
        compiler_params=pltpu.CompilerParams(vmem_limit_bytes=24 * 2**20),
    )(*operands, *after)


def shape(*dims, dtype=F32):
    return jax.ShapeDtypeStruct(dims, dtype)


def core():
    return lax.rem(lax.axis_index("domain"), 2)


def block_of_band():
    return lax.bitwise_xor(lax.div(lax.axis_index("domain"), 2), lax.axis_index("band"))


def pieces_kernel(one, far, near, top, bottom, done):
    cut, rest = top.shape[0], bottom.shape[0]

    @pl.when(core() == one)
    def _():
        copies = [
            pltpu.make_async_copy(far.at[pl.ds(0, cut)], top, done.at[0]),
            pltpu.make_async_copy(near.at[pl.ds(cut, rest)], bottom, done.at[1]),
        ]
        for copy in copies:
            copy.start()
        for copy in copies:
            copy.wait()


def own_kernel(mine, theirs, own, block):
    rows = mine.shape[0]
    for side, states in enumerate((mine, theirs)):
        block[side * rows : (side + 1) * rows] = jnp.dot(states[...], own[...], preferred_element_type=F32)


def early_kernel(mine, theirs, near_even, far_even, near_odd, far_odd, near_block, far_block):
    rows, width = mine.shape[0], near_even.shape[1]
    first = core() == 0
    near, far = jnp.where(first, near_even[...], near_odd[...]), jnp.where(first, far_even[...], far_odd[...])
    wide = jnp.concatenate([near, far], 1)
    for side, states in enumerate((mine, theirs)):
        result = jnp.dot(states[...], wide, preferred_element_type=F32)
        near_block[side * rows : (side + 1) * rows] = result[:, :width]
        far_block[side * rows : (side + 1) * rows] = result[:, width:]


def upper_kernel(mine, theirs, top_even, top_odd, block):
    rows = mine.shape[0]

    def multiply(top):
        for side, states in enumerate((mine, theirs)):
            result = jnp.dot(states[:, : top.shape[0]], top[...], preferred_element_type=F32)
            block[side * rows : (side + 1) * rows] = result

    pl.when(core() == 0)(lambda: multiply(top_even))
    pl.when(core() != 0)(lambda: multiply(top_odd))


def late_kernel(mine, theirs, bottom_even, bottom_odd, upper, own, near, far, kept, *refs):
    sent, last = refs[:-1], refs[-1]
    rows = mine.shape[0]

    def multiply(bottom):
        start = mine.shape[1] - bottom.shape[0]
        for side, states in enumerate((mine, theirs)):
            span = slice(side * rows, (side + 1) * rows)
            last[span] = upper[span] + jnp.dot(states[:, start:], bottom[...], preferred_element_type=F32)

    pl.when(core() == 0)(lambda: multiply(bottom_even))
    pl.when(core() != 0)(lambda: multiply(bottom_odd))
    where = block_of_band()

    def store(out, slot, block):
        @pl.when(slot == lax.bitwise_xor(where, mask))
        def _():
            out[...] = block[...].astype(out.dtype)

    for mask, out in enumerate((kept, *sent)):
        for slot, block in enumerate((own, near, far, last)):
            store(out, slot, block)


def sum_kernel(kept, *refs):
    parts, (mine, theirs) = refs[:-2], refs[-2:]
    value = kept[...]
    for part in parts:
        value = value + part[...].astype(F32)
    rows = mine.shape[0]
    mine[...] = value[:rows]
    theirs[...] = value[rows:]


def rotate_square(wavefunctions, rotation, operator):
    bands, chips = lax.axis_size("band"), lax.axis_size("domain") // 2
    rows, states = wavefunctions.shape
    width = rotation.shape[1]
    received = [paired(rotation, NEAR, 0), paired(rotation, FAR, 0)]
    theirs = exchanged(wavefunctions, "domain", CORE)
    block = [shape(2 * rows, width)]
    operator = operator(theirs)
    later, _ = lax.optimization_barrier((rotation, operator[0]))
    own = call(own_kernel, block, (wavefunctions, theirs, rotation), after=(later,))[0]
    received += [exchanged(later, "domain", NEAR, CORE), exchanged(later, "domain", FAR, CORE)]
    passed, previous = [], [own]
    for one, share in ((0, 19), (CORE, 17)):
        cut = states * share // 32
        outs = [shape(count, width, dtype=BF16) for count in (cut, states - cut)]
        pair = received[2 * one : 2 * one + 2][::-1]
        kernel = functools.partial(pieces_kernel, one)
        top, bottom = call(kernel, outs, pair, after=previous, scratch=[pltpu.SemaphoreType.DMA((2,))])
        previous = [bottom]
        passed.append(exchanged(top, "domain", NEAR, one))
        passed.append(paired(bottom, FAR, one) if one else exchanged(bottom, "domain", FAR, one))
    early = call(early_kernel, block * 2, (wavefunctions, theirs, *received))
    outs = block + [shape(2 * rows, width, dtype=BF16)] * (bands - 1)
    scratch = [pltpu.VMEM((2 * rows, width), F32)]
    upper = call(upper_kernel, block, (wavefunctions, theirs, *passed[::2]), after=early[:1])[0]
    operands = (wavefunctions, theirs, *passed[1::2], upper, own, *early)
    kept, *sent = call(late_kernel, outs, operands, scratch=scratch)
    parts = [exchanged(sent[mask - 1], "band", mask) for mask in reversed(range(1, bands))]
    mine, others = call(sum_kernel, [shape(rows, width)] * 2, (kept, *parts))
    return mine, exchanged(others, "domain", CORE), operator


def rotate_any(wavefunctions, rotation):
    columns = lax.all_gather(rotation, "domain", axis=1, tiled=True)
    return lax.psum_scatter(dot(wavefunctions, columns), "band", scatter_dimension=1, tiled=True)


def faces_kernel(mine, other, assembled, pick, total, faces, onward):
    own, width = mine.shape
    columns = 2 * width
    first = core() == 0
    for side, half in enumerate((jnp.where(first, mine[...], other[...]), jnp.where(first, other[...], mine[...]))):
        total[:, side * width : (side + 1) * width] = half
    high, low = split(total[...])
    faces[...] = dot(pick[...], high).astype(BF16)
    onward[:, :columns] = (dot(assembled[own:, :own], high) + dot(assembled[own:, :own], low)).astype(BF16)
    onward[:, columns:] = assembled[own:, own:]


def inner_kernel(total, assembled, pick, out, faces):
    own, columns = total.shape
    high, low = split(total[...])
    inner = assembled[:own, :own]
    out[...] = dot(inner, high) + dot(inner, low)
    faces[:, :columns] = dot(pick[...], high).astype(BF16)
    faces[:, columns:] = dot(pick[...], low).astype(BF16)


def final_kernel(inner, faces, assembled, spread, incoming, back, out):
    own, columns = inner.shape
    domain, count = lax.axis_index("domain"), lax.axis_size("domain")
    incoming = jnp.where(domain == count - 1, jnp.zeros(incoming.shape, BF16), incoming[...])
    back = jnp.where(domain == 0, jnp.zeros(back.shape, BF16), back[...])
    extra = dot(back[:, columns:], faces[...])
    high, low = split(back[:, :columns].astype(F32) + extra[:, :columns] + extra[:, columns:])
    matrix = jnp.concatenate([assembled[:own, own:], spread[...], spread[...]], 1)
    out[...] = inner[...] + dot(matrix, jnp.concatenate([incoming, high, low], 0))


def rotated(value, axis, steps):
    count = lax.axis_size(axis)
    return lax.ppermute(value, axis, [(source, (source + steps) % count) for source in range(count)])


def finish_square(mine, other, operator):
    assembled, pick, spread = operator
    rows, width = mine.shape
    shared, columns = pick.shape[0], 2 * width
    outs = [shape(rows, columns), shape(shared, columns, dtype=BF16), shape(shared, columns + shared, dtype=BF16)]
    total, faces, onward = call(faces_kernel, outs, (mine, other, assembled, pick))
    back, incoming = rotated(onward, "domain", 1), rotated(faces, "domain", -1)
    outs = [shape(rows, columns), shape(shared, 2 * columns, dtype=BF16)]
    inner, faces = call(inner_kernel, outs, (total, assembled, pick))
    return call(final_kernel, outs[:1], (inner, faces, assembled, spread, incoming, back))[0]


def finish_any(rotated, cell_matrices, cell_nodes, face_map):
    own = rotated.shape[0]
    assembled, pick, returned = assemble_any(cell_matrices, cell_nodes, face_map, own)
    rotated = rotated.astype(BF16).astype(assembled.dtype)
    incoming = shifted(dot(pick, rotated).astype(BF16), "domain", -1).astype(assembled.dtype)
    back = shifted(dot(assembled[own:, :own], rotated), "domain", 1)
    inner = dot(assembled[:own, :own], rotated) + dot(returned, rotated) + dot(assembled[:own, own:], incoming)
    return inner + dot(pick.T.astype(F32), back)


def assemble_any(cell_matrices, cell_nodes, face_map, own):
    cells = cell_nodes.shape[0]
    extent = own + face_map.shape[0]
    held = BF16 if cells == 1 else F32
    places = jax.nn.one_hot(cell_nodes, extent, dtype=held)
    assembled = jnp.zeros((extent, extent), F32)
    for cell in range(cells):
        rows = dot(places[cell].T, cell_matrices[cell].astype(held)).astype(held)
        assembled = assembled + dot(rows, places[cell])
    assembled = assembled.astype(held)
    pick = jax.nn.one_hot(face_map, own, dtype=held)
    corner = shifted(assembled[own:, own:], "domain", 1)
    returned = dot(dot(pick.T, corner).astype(held), pick).astype(held)
    return assembled, pick, returned


def assemble_kernel(matrix, nodes, faces, assembled, pick, spread):
    extent = assembled.shape[0]
    places = jnp.where(lax.broadcasted_iota(jnp.int32, (extent, extent), 0) == nodes[...], 1.0, 0.0).astype(BF16)
    rows = dot(places, matrix[0]).astype(BF16)
    whole = lax.dot_general(rows, places, (((1,), (1,)), ((), ())), preferred_element_type=F32)
    assembled[...] = whole.astype(BF16)
    chosen = jnp.where(lax.broadcasted_iota(jnp.int32, spread.shape, 0) == faces[...], 1.0, 0.0)
    spread[...] = chosen.astype(BF16)
    pick[...] = chosen.T.astype(BF16)


def assemble(cell_matrices, cell_nodes, face_map, own, after):
    shared = face_map.shape[0]
    outs = [(own + shared, own + shared), (shared, own), (own, shared)]
    operands = (cell_matrices, cell_nodes, face_map.reshape(1, shared))
    return call(assemble_kernel, [shape(*dims, dtype=BF16) for dims in outs], operands, after=(after,))


def local(wavefunctions, rotation, cell_matrices, cell_nodes, face_map):
    chips = lax.axis_size("domain") // 2
    if chips == FAR and chips == lax.axis_size("band") and cell_nodes.shape[0] == 1:
        operator = functools.partial(assemble, cell_matrices, cell_nodes, face_map, wavefunctions.shape[0])
        return finish_square(*rotate_square(wavefunctions, rotation, operator))
    return finish_any(rotate_any(wavefunctions, rotation), cell_matrices, cell_nodes, face_map)


def solution(mesh):
    in_specs = (
        P("domain", "band"),
        P("band", "domain"),
        P("domain", None, None),
        P("domain", None),
        P("domain"),
    )
    out_specs = P("domain", "band")
    return jax.shard_map(local, mesh=mesh, in_specs=in_specs, out_specs=out_specs, check_vma=False)
```

```python
import functools

import jax
import jax.numpy as jnp
from jax import lax
from jax.experimental import pallas as pl
from jax.experimental.pallas import tpu as pltpu
from jax.sharding import PartitionSpec as P

CORE, NEAR, FAR = 1, 2, 4
VMEM = pl.BlockSpec(memory_space=pltpu.VMEM)
ANY = pl.BlockSpec(memory_space=pl.ANY)
F32, BF16 = jnp.float32, jnp.bfloat16


def dot(left, right):
    precision = lax.Precision.HIGHEST if left.dtype == F32 else None
    return jnp.dot(left, right, precision=precision, preferred_element_type=F32)


def split(value):
    high = value.astype(BF16)
    return high, (value - high.astype(F32)).astype(BF16)


def shifted(value, axis, steps):
    count = lax.axis_size(axis)
    leading, last = (max(0, -steps), min(count, count - steps))
    return lax.ppermute(value, axis, [(source, source + steps) for source in range(leading, last)])


def exchanged(value, axis, mask, core=None):
    sources = range(lax.axis_size(axis))
    return lax.ppermute(value, axis, [(source, source ^ mask) for source in sources if core in (None, source & CORE)])


def paired(value, mask, one):
    count, bands = lax.axis_size("domain"), lax.axis_size("band")
    pairs = []
    for place in range(count):
        for band in range(bands):
            partner = (place ^ mask, band) if place & CORE == one else (place, band ^ 1)
            pairs.append((place * bands + band, partner[0] * bands + partner[1]))
    return lax.ppermute(value, ("domain", "band"), pairs)


def call(kernel, outs, operands, after=(), spaces=None, scratch=()):
    after = tuple(after)
    count = len(operands)

    def body(*refs):
        kernel(*refs[:count], *refs[count + len(after) :])

    return pl.pallas_call(
        body,
        out_shape=outs,
        in_specs=[pl.BlockSpec(memory_space=space) for space in spaces or [pltpu.VMEM] * count] + [ANY] * len(after),
        out_specs=[VMEM] * len(outs),
        scratch_shapes=list(scratch),
        cost_estimate=pl.CostEstimate(flops=0, bytes_accessed=1024, transcendentals=0),
        compiler_params=pltpu.CompilerParams(vmem_limit_bytes=24 * 2**20),
    )(*operands, *after)


def shape(*dims, dtype=F32):
    return jax.ShapeDtypeStruct(dims, dtype)


def core():
    return lax.rem(lax.axis_index("domain"), 2)


def block_of_band():
    return lax.bitwise_xor(lax.div(lax.axis_index("domain"), 2), lax.axis_index("band"))


def pieces_kernel(one, far, near, top, bottom, done):
    cut, rest = top.shape[0], bottom.shape[0]

    @pl.when(core() == one)
    def _():
        copies = [
            pltpu.make_async_copy(far.at[pl.ds(0, cut)], top, done.at[0]),
            pltpu.make_async_copy(near.at[pl.ds(cut, rest)], bottom, done.at[1]),
        ]
        for copy in copies:
            copy.start()
        for copy in copies:
            copy.wait()


def own_kernel(mine, theirs, own, block):
    rows = mine.shape[0]
    for side, states in enumerate((mine, theirs)):
        block[side * rows : (side + 1) * rows] = jnp.dot(states[...], own[...], preferred_element_type=F32)


def early_kernel(mine, theirs, near_even, far_even, near_odd, far_odd, near_block, far_block):
    rows, width = mine.shape[0], near_even.shape[1]
    first = core() == 0
    near, far = jnp.where(first, near_even[...], near_odd[...]), jnp.where(first, far_even[...], far_odd[...])
    wide = jnp.concatenate([near, far], 1)
    for side, states in enumerate((mine, theirs)):
        result = jnp.dot(states[...], wide, preferred_element_type=F32)
        near_block[side * rows : (side + 1) * rows] = result[:, :width]
        far_block[side * rows : (side + 1) * rows] = result[:, width:]


def upper_kernel(mine, theirs, top_even, top_odd, block):
    rows = mine.shape[0]

    def multiply(top):
        for side, states in enumerate((mine, theirs)):
            result = jnp.dot(states[:, : top.shape[0]], top[...], preferred_element_type=F32)
            block[side * rows : (side + 1) * rows] = result

    pl.when(core() == 0)(lambda: multiply(top_even))
    pl.when(core() != 0)(lambda: multiply(top_odd))


def late_kernel(mine, theirs, bottom_even, bottom_odd, upper, own, near, far, kept, *refs):
    sent, last = refs[:-1], refs[-1]
    rows = mine.shape[0]

    def multiply(bottom):
        start = mine.shape[1] - bottom.shape[0]
        for side, states in enumerate((mine, theirs)):
            span = slice(side * rows, (side + 1) * rows)
            last[span] = upper[span] + jnp.dot(states[:, start:], bottom[...], preferred_element_type=F32)

    pl.when(core() == 0)(lambda: multiply(bottom_even))
    pl.when(core() != 0)(lambda: multiply(bottom_odd))
    where = block_of_band()

    def store(out, slot, block):
        @pl.when(slot == lax.bitwise_xor(where, mask))
        def _():
            out[...] = block[...].astype(out.dtype)

    for mask, out in enumerate((kept, *sent)):
        for slot, block in enumerate((own, near, far, last)):
            store(out, slot, block)


def sum_kernel(kept, *refs):
    parts, (mine, theirs) = refs[:-2], refs[-2:]
    value = kept[...]
    for part in parts:
        value = value + part[...].astype(F32)
    rows = mine.shape[0]
    mine[...] = value[:rows]
    theirs[...] = value[rows:]


def rotate_square(wavefunctions, rotation, operator):
    bands, chips = lax.axis_size("band"), lax.axis_size("domain") // 2
    rows, states = wavefunctions.shape
    width = rotation.shape[1]
    received = [paired(rotation, NEAR, 0), paired(rotation, FAR, 0)]
    theirs = exchanged(wavefunctions, "domain", CORE)
    block = [shape(2 * rows, width)]
    operator = operator(theirs)
    later, _ = lax.optimization_barrier((rotation, operator[0]))
    own = call(own_kernel, block, (wavefunctions, theirs, rotation), after=(later,))[0]
    received += [exchanged(later, "domain", NEAR, CORE), exchanged(later, "domain", FAR, CORE)]
    passed, previous = [], [own]
    for one, share in ((0, 18), (CORE, 17)):
        cut = states * share // 32
        outs = [shape(count, width, dtype=BF16) for count in (cut, states - cut)]
        pair = received[2 * one : 2 * one + 2][::-1]
        kernel = functools.partial(pieces_kernel, one)
        top, bottom = call(kernel, outs, pair, after=previous, scratch=[pltpu.SemaphoreType.DMA((2,))])
        previous = [bottom]
        passed.append(exchanged(top, "domain", NEAR, one))
        passed.append(paired(bottom, FAR, one) if one else exchanged(bottom, "domain", FAR, one))
    early = call(early_kernel, block * 2, (wavefunctions, theirs, *received))
    outs = block + [shape(2 * rows, width, dtype=BF16)] * (bands - 1)
    scratch = [pltpu.VMEM((2 * rows, width), F32)]
    upper = call(upper_kernel, block, (wavefunctions, theirs, *passed[::2]), after=early[:1])[0]
    operands = (wavefunctions, theirs, *passed[1::2], upper, own, *early)
    kept, *sent = call(late_kernel, outs, operands, scratch=scratch)
    parts = [exchanged(sent[mask - 1], "band", mask) for mask in reversed(range(1, bands))]
    mine, others = call(sum_kernel, [shape(rows, width)] * 2, (kept, *parts))
    return mine, exchanged(others, "domain", CORE), operator


def rotate_any(wavefunctions, rotation):
    columns = lax.all_gather(rotation, "domain", axis=1, tiled=True)
    return lax.psum_scatter(dot(wavefunctions, columns), "band", scatter_dimension=1, tiled=True)


def faces_kernel(mine, other, assembled, pick, total, faces, onward):
    own, width = mine.shape
    columns = 2 * width
    first = core() == 0
    for side, half in enumerate((jnp.where(first, mine[...], other[...]), jnp.where(first, other[...], mine[...]))):
        total[:, side * width : (side + 1) * width] = half
    high, low = split(total[...])
    faces[...] = dot(pick[...], high).astype(BF16)
    onward[:, :columns] = (dot(assembled[own:, :own], high) + dot(assembled[own:, :own], low)).astype(BF16)
    onward[:, columns:] = assembled[own:, own:]


def inner_kernel(total, assembled, pick, out, faces):
    own, columns = total.shape
    high, low = split(total[...])
    inner = assembled[:own, :own]
    out[...] = dot(inner, high) + dot(inner, low)
    faces[:, :columns] = dot(pick[...], high).astype(BF16)
    faces[:, columns:] = dot(pick[...], low).astype(BF16)


def final_kernel(inner, faces, assembled, spread, incoming, back, out):
    own, columns = inner.shape
    domain, count = lax.axis_index("domain"), lax.axis_size("domain")
    incoming = jnp.where(domain == count - 1, jnp.zeros(incoming.shape, BF16), incoming[...])
    back = jnp.where(domain == 0, jnp.zeros(back.shape, BF16), back[...])
    extra = dot(back[:, columns:], faces[...])
    high, low = split(back[:, :columns].astype(F32) + extra[:, :columns] + extra[:, columns:])
    matrix = jnp.concatenate([assembled[:own, own:], spread[...], spread[...]], 1)
    out[...] = inner[...] + dot(matrix, jnp.concatenate([incoming, high, low], 0))


def rotated(value, axis, steps):
    count = lax.axis_size(axis)
    return lax.ppermute(value, axis, [(source, (source + steps) % count) for source in range(count)])


def finish_square(mine, other, operator):
    assembled, pick, spread = operator
    rows, width = mine.shape
    shared, columns = pick.shape[0], 2 * width
    outs = [shape(rows, columns), shape(shared, columns, dtype=BF16), shape(shared, columns + shared, dtype=BF16)]
    total, faces, onward = call(faces_kernel, outs, (mine, other, assembled, pick))
    back, incoming = rotated(onward, "domain", 1), rotated(faces, "domain", -1)
    outs = [shape(rows, columns), shape(shared, 2 * columns, dtype=BF16)]
    inner, faces = call(inner_kernel, outs, (total, assembled, pick))
    return call(final_kernel, outs[:1], (inner, faces, assembled, spread, incoming, back))[0]


def finish_any(rotated, cell_matrices, cell_nodes, face_map):
    own = rotated.shape[0]
    assembled, pick, returned = assemble_any(cell_matrices, cell_nodes, face_map, own)
    rotated = rotated.astype(BF16).astype(assembled.dtype)
    incoming = shifted(dot(pick, rotated).astype(BF16), "domain", -1).astype(assembled.dtype)
    back = shifted(dot(assembled[own:, :own], rotated), "domain", 1)
    inner = dot(assembled[:own, :own], rotated) + dot(returned, rotated) + dot(assembled[:own, own:], incoming)
    return inner + dot(pick.T.astype(F32), back)


def assemble_any(cell_matrices, cell_nodes, face_map, own):
    cells = cell_nodes.shape[0]
    extent = own + face_map.shape[0]
    held = BF16 if cells == 1 else F32
    places = jax.nn.one_hot(cell_nodes, extent, dtype=held)
    assembled = jnp.zeros((extent, extent), F32)
    for cell in range(cells):
        rows = dot(places[cell].T, cell_matrices[cell].astype(held)).astype(held)
        assembled = assembled + dot(rows, places[cell])
    assembled = assembled.astype(held)
    pick = jax.nn.one_hot(face_map, own, dtype=held)
    corner = shifted(assembled[own:, own:], "domain", 1)
    returned = dot(dot(pick.T, corner).astype(held), pick).astype(held)
    return assembled, pick, returned


def assemble_kernel(matrix, nodes, faces, assembled, pick, spread):
    extent = assembled.shape[0]
    places = jnp.where(lax.broadcasted_iota(jnp.int32, (extent, extent), 0) == nodes[...], 1.0, 0.0).astype(BF16)
    rows = dot(places, matrix[0]).astype(BF16)
    whole = lax.dot_general(rows, places, (((1,), (1,)), ((), ())), preferred_element_type=F32)
    assembled[...] = whole.astype(BF16)
    chosen = jnp.where(lax.broadcasted_iota(jnp.int32, spread.shape, 0) == faces[...], 1.0, 0.0)
    spread[...] = chosen.astype(BF16)
    pick[...] = chosen.T.astype(BF16)


def assemble(cell_matrices, cell_nodes, face_map, own, after):
    shared = face_map.shape[0]
    outs = [(own + shared, own + shared), (shared, own), (own, shared)]
    operands = (cell_matrices, cell_nodes, face_map.reshape(1, shared))
    return call(assemble_kernel, [shape(*dims, dtype=BF16) for dims in outs], operands, after=(after,))


def local(wavefunctions, rotation, cell_matrices, cell_nodes, face_map):
    chips = lax.axis_size("domain") // 2
    if chips == FAR and chips == lax.axis_size("band") and cell_nodes.shape[0] == 1:
        operator = functools.partial(assemble, cell_matrices, cell_nodes, face_map, wavefunctions.shape[0])
        return finish_square(*rotate_square(wavefunctions, rotation, operator))
    return finish_any(rotate_any(wavefunctions, rotation), cell_matrices, cell_nodes, face_map)


def solution(mesh):
    in_specs = (
        P("domain", "band"),
        P("band", "domain"),
        P("domain", None, None),
        P("domain", None),
        P("domain"),
    )
    out_specs = P("domain", "band")
    return jax.shard_map(local, mesh=mesh, in_specs=in_specs, out_specs=out_specs, check_vma=False)
```

```python
import functools

import jax
import jax.numpy as jnp
from jax import lax
from jax.experimental import pallas as pl
from jax.experimental.pallas import tpu as pltpu
from jax.sharding import PartitionSpec as P

CORE, NEAR, FAR = 1, 2, 4
VMEM = pl.BlockSpec(memory_space=pltpu.VMEM)
ANY = pl.BlockSpec(memory_space=pl.ANY)
F32, BF16 = jnp.float32, jnp.bfloat16


def dot(left, right):
    precision = lax.Precision.HIGHEST if left.dtype == F32 else None
    return jnp.dot(left, right, precision=precision, preferred_element_type=F32)


def split(value):
    high = value.astype(BF16)
    return high, (value - high.astype(F32)).astype(BF16)


def shifted(value, axis, steps):
    count = lax.axis_size(axis)
    leading, last = (max(0, -steps), min(count, count - steps))
    return lax.ppermute(value, axis, [(source, source + steps) for source in range(leading, last)])


def exchanged(value, axis, mask, core=None):
    sources = range(lax.axis_size(axis))
    return lax.ppermute(value, axis, [(source, source ^ mask) for source in sources if core in (None, source & CORE)])


def paired(value, mask, one):
    count, bands = lax.axis_size("domain"), lax.axis_size("band")
    pairs = []
    for place in range(count):
        for band in range(bands):
            partner = (place ^ mask, band) if place & CORE == one else (place, band ^ 1)
            pairs.append((place * bands + band, partner[0] * bands + partner[1]))
    return lax.ppermute(value, ("domain", "band"), pairs)


def call(kernel, outs, operands, after=(), spaces=None, scratch=()):
    after = tuple(after)
    count = len(operands)

    def body(*refs):
        kernel(*refs[:count], *refs[count + len(after) :])

    return pl.pallas_call(
        body,
        out_shape=outs,
        in_specs=[pl.BlockSpec(memory_space=space) for space in spaces or [pltpu.VMEM] * count] + [ANY] * len(after),
        out_specs=[VMEM] * len(outs),
        scratch_shapes=list(scratch),
        cost_estimate=pl.CostEstimate(flops=0, bytes_accessed=1024, transcendentals=0),
        compiler_params=pltpu.CompilerParams(vmem_limit_bytes=24 * 2**20),
    )(*operands, *after)


def shape(*dims, dtype=F32):
    return jax.ShapeDtypeStruct(dims, dtype)


def core():
    return lax.rem(lax.axis_index("domain"), 2)


def block_of_band():
    return lax.bitwise_xor(lax.div(lax.axis_index("domain"), 2), lax.axis_index("band"))


def pieces_kernel(one, far, near, top, bottom, done):
    cut, rest = top.shape[0], bottom.shape[0]

    @pl.when(core() == one)
    def _():
        copies = [
            pltpu.make_async_copy(far.at[pl.ds(0, cut)], top, done.at[0]),
            pltpu.make_async_copy(near.at[pl.ds(cut, rest)], bottom, done.at[1]),
        ]
        for copy in copies:
            copy.start()
        for copy in copies:
            copy.wait()


def own_kernel(mine, theirs, own, block):
    rows = mine.shape[0]
    for side, states in enumerate((mine, theirs)):
        block[side * rows : (side + 1) * rows] = jnp.dot(states[...], own[...], preferred_element_type=F32)


def early_kernel(mine, theirs, near_even, far_even, near_odd, far_odd, near_block, far_block):
    rows, width = mine.shape[0], near_even.shape[1]
    first = core() == 0
    near, far = jnp.where(first, near_even[...], near_odd[...]), jnp.where(first, far_even[...], far_odd[...])
    wide = jnp.concatenate([near, far], 1)
    for side, states in enumerate((mine, theirs)):
        result = jnp.dot(states[...], wide, preferred_element_type=F32)
        near_block[side * rows : (side + 1) * rows] = result[:, :width]
        far_block[side * rows : (side + 1) * rows] = result[:, width:]


def upper_kernel(mine, theirs, top_even, top_odd, block):
    rows = mine.shape[0]

    def multiply(top):
        for side, states in enumerate((mine, theirs)):
            result = jnp.dot(states[:, : top.shape[0]], top[...], preferred_element_type=F32)
            block[side * rows : (side + 1) * rows] = result

    pl.when(core() == 0)(lambda: multiply(top_even))
    pl.when(core() != 0)(lambda: multiply(top_odd))


def late_kernel(mine, theirs, bottom_even, bottom_odd, upper, own, near, far, kept, *refs):
    sent, last = refs[:-1], refs[-1]
    rows = mine.shape[0]

    def multiply(bottom):
        start = mine.shape[1] - bottom.shape[0]
        for side, states in enumerate((mine, theirs)):
            span = slice(side * rows, (side + 1) * rows)
            last[span] = upper[span] + jnp.dot(states[:, start:], bottom[...], preferred_element_type=F32)

    pl.when(core() == 0)(lambda: multiply(bottom_even))
    pl.when(core() != 0)(lambda: multiply(bottom_odd))
    where = block_of_band()

    def store(out, slot, block):
        @pl.when(slot == lax.bitwise_xor(where, mask))
        def _():
            out[...] = block[...].astype(out.dtype)

    for mask, out in enumerate((kept, *sent)):
        for slot, block in enumerate((own, near, far, last)):
            store(out, slot, block)


def sum_kernel(kept, *refs):
    parts, (mine, theirs) = refs[:-2], refs[-2:]
    value = kept[...]
    for part in parts:
        value = value + part[...].astype(F32)
    rows = mine.shape[0]
    mine[...] = value[:rows]
    theirs[...] = value[rows:]


def rotate_square(wavefunctions, rotation, operator):
    bands, chips = lax.axis_size("band"), lax.axis_size("domain") // 2
    rows, states = wavefunctions.shape
    width = rotation.shape[1]
    received = [paired(rotation, NEAR, 0), paired(rotation, FAR, 0)]
    theirs = exchanged(wavefunctions, "domain", CORE)
    block = [shape(2 * rows, width)]
    operator = operator(theirs)
    later, _ = lax.optimization_barrier((rotation, operator[0]))
    own = call(own_kernel, block, (wavefunctions, theirs, rotation), after=(later,))[0]
    received += [exchanged(later, "domain", NEAR, CORE), exchanged(later, "domain", FAR, CORE)]
    passed, previous = [], [own]
    for one, share in ((0, 17), (CORE, 17)):
        cut = states * share // 32
        outs = [shape(count, width, dtype=BF16) for count in (cut, states - cut)]
        pair = received[2 * one : 2 * one + 2][::-1]
        kernel = functools.partial(pieces_kernel, one)
        top, bottom = call(kernel, outs, pair, after=previous, scratch=[pltpu.SemaphoreType.DMA((2,))])
        previous = [bottom]
        passed.append(exchanged(top, "domain", NEAR, one))
        passed.append(paired(bottom, FAR, one) if one else exchanged(bottom, "domain", FAR, one))
    early = call(early_kernel, block * 2, (wavefunctions, theirs, *received))
    outs = block + [shape(2 * rows, width, dtype=BF16)] * (bands - 1)
    scratch = [pltpu.VMEM((2 * rows, width), F32)]
    upper = call(upper_kernel, block, (wavefunctions, theirs, *passed[::2]), after=early[:1])[0]
    operands = (wavefunctions, theirs, *passed[1::2], upper, own, *early)
    kept, *sent = call(late_kernel, outs, operands, scratch=scratch)
    parts = [exchanged(sent[mask - 1], "band", mask) for mask in reversed(range(1, bands))]
    mine, others = call(sum_kernel, [shape(rows, width)] * 2, (kept, *parts))
    return mine, exchanged(others, "domain", CORE), operator


def rotate_any(wavefunctions, rotation):
    columns = lax.all_gather(rotation, "domain", axis=1, tiled=True)
    return lax.psum_scatter(dot(wavefunctions, columns), "band", scatter_dimension=1, tiled=True)


def faces_kernel(mine, other, assembled, pick, total, faces, onward):
    own, width = mine.shape
    columns = 2 * width
    first = core() == 0
    for side, half in enumerate((jnp.where(first, mine[...], other[...]), jnp.where(first, other[...], mine[...]))):
        total[:, side * width : (side + 1) * width] = half
    high, low = split(total[...])
    faces[...] = dot(pick[...], high).astype(BF16)
    onward[:, :columns] = (dot(assembled[own:, :own], high) + dot(assembled[own:, :own], low)).astype(BF16)
    onward[:, columns:] = assembled[own:, own:]


def inner_kernel(total, assembled, pick, out, faces):
    own, columns = total.shape
    high, low = split(total[...])
    inner = assembled[:own, :own]
    out[...] = dot(inner, high) + dot(inner, low)
    faces[:, :columns] = dot(pick[...], high).astype(BF16)
    faces[:, columns:] = dot(pick[...], low).astype(BF16)


def final_kernel(inner, faces, assembled, spread, incoming, back, out):
    own, columns = inner.shape
    domain, count = lax.axis_index("domain"), lax.axis_size("domain")
    incoming = jnp.where(domain == count - 1, jnp.zeros(incoming.shape, BF16), incoming[...])
    back = jnp.where(domain == 0, jnp.zeros(back.shape, BF16), back[...])
    extra = dot(back[:, columns:], faces[...])
    high, low = split(back[:, :columns].astype(F32) + extra[:, :columns] + extra[:, columns:])
    matrix = jnp.concatenate([assembled[:own, own:], spread[...], spread[...]], 1)
    out[...] = inner[...] + dot(matrix, jnp.concatenate([incoming, high, low], 0))


def rotated(value, axis, steps):
    count = lax.axis_size(axis)
    return lax.ppermute(value, axis, [(source, (source + steps) % count) for source in range(count)])


def finish_square(mine, other, operator):
    assembled, pick, spread = operator
    rows, width = mine.shape
    shared, columns = pick.shape[0], 2 * width
    outs = [shape(rows, columns), shape(shared, columns, dtype=BF16), shape(shared, columns + shared, dtype=BF16)]
    total, faces, onward = call(faces_kernel, outs, (mine, other, assembled, pick))
    back, incoming = rotated(onward, "domain", 1), rotated(faces, "domain", -1)
    outs = [shape(rows, columns), shape(shared, 2 * columns, dtype=BF16)]
    inner, faces = call(inner_kernel, outs, (total, assembled, pick))
    return call(final_kernel, outs[:1], (inner, faces, assembled, spread, incoming, back))[0]


def finish_any(rotated, cell_matrices, cell_nodes, face_map):
    own = rotated.shape[0]
    assembled, pick, returned = assemble_any(cell_matrices, cell_nodes, face_map, own)
    rotated = rotated.astype(BF16).astype(assembled.dtype)
    incoming = shifted(dot(pick, rotated).astype(BF16), "domain", -1).astype(assembled.dtype)
    back = shifted(dot(assembled[own:, :own], rotated), "domain", 1)
    inner = dot(assembled[:own, :own], rotated) + dot(returned, rotated) + dot(assembled[:own, own:], incoming)
    return inner + dot(pick.T.astype(F32), back)


def assemble_any(cell_matrices, cell_nodes, face_map, own):
    cells = cell_nodes.shape[0]
    extent = own + face_map.shape[0]
    held = BF16 if cells == 1 else F32
    places = jax.nn.one_hot(cell_nodes, extent, dtype=held)
    assembled = jnp.zeros((extent, extent), F32)
    for cell in range(cells):
        rows = dot(places[cell].T, cell_matrices[cell].astype(held)).astype(held)
        assembled = assembled + dot(rows, places[cell])
    assembled = assembled.astype(held)
    pick = jax.nn.one_hot(face_map, own, dtype=held)
    corner = shifted(assembled[own:, own:], "domain", 1)
    returned = dot(dot(pick.T, corner).astype(held), pick).astype(held)
    return assembled, pick, returned


def assemble_kernel(matrix, nodes, faces, assembled, pick, spread):
    extent = assembled.shape[0]
    places = jnp.where(lax.broadcasted_iota(jnp.int32, (extent, extent), 0) == nodes[...], 1.0, 0.0).astype(BF16)
    rows = dot(places, matrix[0]).astype(BF16)
    whole = lax.dot_general(rows, places, (((1,), (1,)), ((), ())), preferred_element_type=F32)
    assembled[...] = whole.astype(BF16)
    chosen = jnp.where(lax.broadcasted_iota(jnp.int32, spread.shape, 0) == faces[...], 1.0, 0.0)
    spread[...] = chosen.astype(BF16)
    pick[...] = chosen.T.astype(BF16)


def assemble(cell_matrices, cell_nodes, face_map, own, after):
    shared = face_map.shape[0]
    outs = [(own + shared, own + shared), (shared, own), (own, shared)]
    operands = (cell_matrices, cell_nodes, face_map.reshape(1, shared))
    return call(assemble_kernel, [shape(*dims, dtype=BF16) for dims in outs], operands, after=(after,))


def local(wavefunctions, rotation, cell_matrices, cell_nodes, face_map):
    chips = lax.axis_size("domain") // 2
    if chips == FAR and chips == lax.axis_size("band") and cell_nodes.shape[0] == 1:
        operator = functools.partial(assemble, cell_matrices, cell_nodes, face_map, wavefunctions.shape[0])
        return finish_square(*rotate_square(wavefunctions, rotation, operator))
    return finish_any(rotate_any(wavefunctions, rotation), cell_matrices, cell_nodes, face_map)


def solution(mesh):
    in_specs = (
        P("domain", "band"),
        P("band", "domain"),
        P("domain", None, None),
        P("domain", None),
        P("domain"),
    )
    out_specs = P("domain", "band")
    return jax.shard_map(local, mesh=mesh, in_specs=in_specs, out_specs=out_specs, check_vma=False)
```
